512 devices in a mesh: depth: 8 (over y), lat: 16 (over z_lo, x, core), tx: 4 (over z_hi).
Axes of the slice: x: 4, y: 8, z: 8 (z_hi: 4, z_lo: 2; z = z_hi * 2 + z_lo), core: 2. Of those that a mesh axis runs over, the one named last changes fastest.
Arguments:
- conductivity: float32 [16, 128, 512], P('depth', 'lat'), may hold values from 0.1 to 10
- field_guess: float32 [4, 2, 2, 3, 16, 128, 512], P('tx', None, None, None, 'depth', 'lat'), may hold values from -56 to 56, as said below
- tx_cell: int32 [4], P('tx'), may hold values from 0 to 1048575
- rx_cell: int32 [4, 64], P('tx'), may hold values from 0 to 1048575
- rx_weight: float32 [4, 64, 2], P('tx'), may hold values from -16 to 16
Outputs:
- fields: float32 [4, 2, 2, 3, 16, 128, 512], P('tx', None, None, None, 'depth', 'lat')
- gradient: float32 [16, 128, 512], P('depth', 'lat', 'tx')
The draws below stay inside these ranges and needn't reach their ends.
Inputs may be any that keep to these rules, and one draw needn't show every extreme that they name: `tx_cell`: a cell number (z * 128 + x) * 512 + y. `rx_cell`: cell numbers (z * 128 + x) * 512 + y; two receivers may share a cell. `field_guess`: a starting field.
All inputs are finite; a program needn't handle non-finite values.
Results may differ from the reference program's by a relative error of at most 0.0001.
Values sent between devices are 32-bit elements; how exact they have to be, the bound alone decides.
No kernel may reach another device: no remote copies, remote signals or barrier semaphores. Data moves between devices by JAX's collectives and lax.ppermute only.
A program may use at most 64 MiB of HBM per device.

```python
import math
import jax
import jax.numpy as jnp
from jax import lax

NY = 512
NRX = 64
ITERS = 2
NZ = 16
NX = 128
NTX = 4


def draw_field_guess(key, part):
    full_shape = (NTX, 2, 2, 3, NZ, NX, NY)
    key_noise = jax.random.fold_in(key, 0)
    depth_ramp = 1.0 + 2.0 * jnp.arange(NZ, dtype=jnp.float32) / max(NZ - 1, 1)
    lat_ramp = 1.0 + 2.0 * jnp.arange(NX, dtype=jnp.float32) / max(NX - 1, 1)
    profile = depth_ramp[:, None, None] * lat_ramp[None, :, None]
    noise_field = jnp.clip(jax.random.normal(key_noise, full_shape, jnp.float32), -6.0, 6.0)
    return (0.4 * noise_field * profile).astype(jnp.float32)


def with_ends(entries, stream_key, low, largest):
    longest = entries.shape.index(max(entries.shape))
    spots = []
    for shift in (0, 1):
        where = [jax.random.randint(jax.random.fold_in(stream_key, axis), (), 0, length) for axis, length in enumerate(entries.shape)]
        where[longest] = (where[longest] + shift) % entries.shape[longest]
        spots.append(tuple(where))
    return entries.at[spots[0]].set(low).at[spots[1]].set(largest)


def shard_levels(own_key, dims, cuts, low, top_value):
    def one(position, parts):
        heights = jax.random.uniform(jax.random.fold_in(jax.random.fold_in(own_key, 6), position), (parts,), jnp.float32, low / len(cuts), top_value / len(cuts))
        return jnp.repeat(jnp.exp(heights), dims[position] // parts).reshape((-1,) + (1,) * (len(dims) - position - 1))

    loudness = one(*cuts[0])
    for cut in cuts[1:]:
        loudness = loudness * one(*cut)
    return loudness


def noise(own_key, dims, scale, bound, cuts=(), kind=jnp.bfloat16):
    values = scale * jax.random.normal(own_key, dims, jnp.float32)
    if cuts:
        values = values * shard_levels(own_key, dims, cuts, -0.22, 0.18)
    return jnp.clip(values, -bound, bound).astype(kind)


def setup_inputs(seed: int = 0) -> dict:
    key_list = jax.random.split(jax.random.key(seed), 6)
    conductivity = jnp.clip(jnp.exp(math.log(10.0) - 4.6051702 * jax.random.uniform(key_list[0], (NZ, NX, NY), jnp.float32) ** shard_levels(key_list[0], (NZ, NX, NY), ((0, 8), (1, 16)), -0.2, 0.2)), 0.1, 10.0)
    field_guess = draw_field_guess(jax.random.fold_in(key_list[5], 71), 0)
    tx_cell = with_ends(jax.random.randint(key_list[2], (NTX,), 0, NZ * NX * NY), jax.random.fold_in(key_list[2], 1), 0, (NZ * NX * NY) - 1).astype(jnp.int32)
    rx_cell = with_ends(jax.random.randint(key_list[3], (NTX, NRX), 0, NZ * NX * NY), jax.random.fold_in(key_list[3], 1), 0, (NZ * NX * NY) - 1).astype(jnp.int32)
    rx_weight = noise(key_list[4], (NTX, NRX, 2), 4.0, 16.0, ((0, 4),), jnp.float32)
    return dict(conductivity=conductivity, field_guess=field_guess, tx_cell=tx_cell, rx_cell=rx_cell, rx_weight=rx_weight)


source_amplitude = 20.0


def step_ahead(values, plane, along_axis):
    length = values.shape[along_axis]
    return jnp.concatenate([lax.slice_in_dim(values, 1, length, axis=along_axis), plane], axis=along_axis) - values


def step_behind(values, plane, along_axis):
    length = values.shape[along_axis]
    return values - jnp.concatenate([plane, lax.slice_in_dim(values, 0, length - 1, axis=along_axis)], axis=along_axis)


def curl_pair(electric, depth_plane, lat_plane, difference):
    def along(component, direction_axis):
        values = electric[:, :, component]
        if direction_axis == 2:
            plane = depth_plane[:, :, component]
        elif direction_axis == 3:
            plane = lat_plane[:, :, component]
        else:
            plane = jnp.zeros_like(values[..., :1])
        return difference(values, plane, direction_axis)
    out_depth = along(2, 3) - along(1, 4)
    out_lat = along(0, 4) - along(2, 2)
    out_span = along(1, 2) - along(0, 3)
    return jnp.stack([out_depth, out_lat, out_span], axis=2)


def apply_operator(electric, conductivity):
    depth_zero = jnp.zeros_like(electric[:, :, :, :1])
    lat_zero = jnp.zeros_like(electric[:, :, :, :, :1])
    magnetic = curl_pair(electric, depth_zero, lat_zero, step_ahead)
    curled = curl_pair(magnetic, depth_zero, lat_zero, step_behind)
    real_part = curled[:, 0] - conductivity * electric[:, 1]
    imag_part = curled[:, 1] + conductivity * electric[:, 0]
    return jnp.stack([real_part, imag_part], axis=1)


def inner_local(left_side, right_side):
    real_part = jnp.sum(left_side[:, 0] * right_side[:, 0] + left_side[:, 1] * right_side[:, 1], axis=(1, 2, 3, 4))
    imag_part = jnp.sum(left_side[:, 0] * right_side[:, 1] - left_side[:, 1] * right_side[:, 0], axis=(1, 2, 3, 4))
    return (real_part, imag_part)


def complex_product(first_pair, second_pair):
    return (first_pair[0] * second_pair[0] - first_pair[1] * second_pair[1], first_pair[0] * second_pair[1] + first_pair[1] * second_pair[0])


def complex_quotient(first_pair, second_pair):
    denominator = second_pair[0] * second_pair[0] + second_pair[1] * second_pair[1]
    return ((first_pair[0] * second_pair[0] + first_pair[1] * second_pair[1]) / denominator, (first_pair[1] * second_pair[0] - first_pair[0] * second_pair[1]) / denominator)


def scale_field(factor, electric):
    real_factor = factor[0].reshape(-1, 1, 1, 1, 1)
    imag_factor = factor[1].reshape(-1, 1, 1, 1, 1)
    real_part = real_factor * electric[:, 0] - imag_factor * electric[:, 1]
    imag_part = real_factor * electric[:, 1] + imag_factor * electric[:, 0]
    return jnp.stack([real_part, imag_part], axis=1)


def solve(start_field, right_hand, conductivity):
    solution = start_field
    residual = right_hand - apply_operator(start_field, conductivity)
    shadow = residual
    direction = residual
    shadow_dot = inner_local(shadow, residual)
    for iteration in range(ITERS):
        applied = apply_operator(direction, conductivity)
        step_length = complex_quotient(shadow_dot, inner_local(shadow, applied))
        halfway = residual - scale_field(step_length, applied)
        second = apply_operator(halfway, conductivity)
        cross_sum = inner_local(second, halfway)
        energy = jnp.sum(second * second, axis=(1, 2, 3, 4, 5))
        relax_weight = (cross_sum[0] / energy, cross_sum[1] / energy)
        solution = solution + scale_field(step_length, direction) + scale_field(relax_weight, halfway)
        residual = halfway - scale_field(relax_weight, second)
        if iteration + 1 < ITERS:
            new_dot = inner_local(shadow, residual)
            mixing = complex_product(complex_quotient(new_dot, shadow_dot), complex_quotient(step_length, relax_weight))
            direction = residual + scale_field(mixing, direction - scale_field(relax_weight, applied))
            shadow_dot = new_dot
    return solution


def reference(conductivity, field_guess, tx_cell, rx_cell, rx_weight):
    cell_total = NZ * NX * NY

    def one_transmitter(pieces):
        start_field, source_cell, receiver_cells, receiver_weights = pieces
        tx_plane = jnp.zeros((cell_total,), jnp.float32).at[source_cell].add(-source_amplitude).reshape(NZ, NX, NY)
        rx_real = jnp.zeros((cell_total,), jnp.float32).at[receiver_cells].add(receiver_weights[:, 0]).reshape(NZ, NX, NY)
        rx_imag = jnp.zeros((cell_total,), jnp.float32).at[receiver_cells].add(receiver_weights[:, 1]).reshape(NZ, NX, NY)
        blank_plane = jnp.zeros((NZ, NX, NY), jnp.float32)
        tx_side = jnp.stack([jnp.stack([blank_plane, blank_plane, blank_plane]), jnp.stack([tx_plane, blank_plane, blank_plane])])
        rx_side = jnp.stack([jnp.stack([rx_real, blank_plane, blank_plane]), jnp.stack([rx_imag, blank_plane, blank_plane])])
        right_hand = jnp.stack([tx_side, rx_side])
        return solve(start_field, right_hand, conductivity)

    fields = lax.map(one_transmitter, (field_guess, tx_cell, rx_cell, rx_weight))
    gradient = jnp.sum(fields[:, 0, 0] * fields[:, 1, 0] - fields[:, 0, 1] * fields[:, 1, 1], axis=(0, 1))
    return (fields, gradient)
```

```python
import jax
import jax.numpy as jnp
from jax import lax
from jax.sharding import PartitionSpec as P

ITERS = 2


source_amplitude = 20.0


def with_halo(cells, sides, width):
    for axis, dim in sides:
        count = lax.axis_size(axis)
        ends = count - 1
        head = lax.slice_in_dim(cells, 0, width, axis=dim)
        tail = lax.slice_in_dim(cells, cells.shape[dim] - width, cells.shape[dim], axis=dim)
        cells = jnp.concatenate(
            [
                lax.ppermute(tail, axis, [(i, (i + 1) % count) for i in range(ends)]),
                cells,
                lax.ppermute(head, axis, [((i + 1) % count, i) for i in range(ends)]),
            ],
            axis=dim,
        )
    return cells


def step_ahead(values, plane, along_axis):
    length = values.shape[along_axis]
    return (
        jnp.concatenate(
            [lax.slice_in_dim(values, 1, length, axis=along_axis), plane], axis=along_axis
        )
        - values
    )


def step_behind(values, plane, along_axis):
    length = values.shape[along_axis]
    return values - jnp.concatenate(
        [plane, lax.slice_in_dim(values, 0, length - 1, axis=along_axis)], axis=along_axis
    )


def curl_pair(electric, depth_plane, lat_plane, difference):

    def along(component, direction_axis):
        values = electric[:, :, component]
        if direction_axis == 2:
            plane = depth_plane[:, :, component]
        elif direction_axis == 3:
            plane = lat_plane[:, :, component]
        else:
            plane = jnp.zeros_like(values[..., :1])
        return difference(values, plane, direction_axis)

    out_depth = along(2, 3) - along(1, 4)
    out_lat = along(0, 4) - along(2, 2)
    out_span = along(1, 2) - along(0, 3)
    return jnp.stack([out_depth, out_lat, out_span], axis=2)


def inner_local(left_side, right_side):
    real_part = jnp.sum(
        left_side[:, 0] * right_side[:, 0] + left_side[:, 1] * right_side[:, 1], axis=(1, 2, 3, 4)
    )
    imag_part = jnp.sum(
        left_side[:, 0] * right_side[:, 1] - left_side[:, 1] * right_side[:, 0], axis=(1, 2, 3, 4)
    )
    return (real_part, imag_part)


def sum_over_grid(values):
    parts = lax.axis_size("depth") * lax.axis_size("lat")
    row = jnp.concatenate([v.reshape(-1) for v in values])
    rows = jnp.broadcast_to(jnp.pad(row, (0, 128 - row.size))[None], (parts, 128))
    totals = jnp.sum(lax.all_to_all(rows, ("depth", "lat"), 0, 0), axis=0)
    return tuple(totals[2 * k : 2 * k + 2] for k in range(len(values)))


def complex_product(first_pair, second_pair):
    return (
        first_pair[0] * second_pair[0] - first_pair[1] * second_pair[1],
        first_pair[0] * second_pair[1] + first_pair[1] * second_pair[0],
    )


def complex_quotient(first_pair, second_pair):
    denominator = second_pair[0] * second_pair[0] + second_pair[1] * second_pair[1]
    return (
        (first_pair[0] * second_pair[0] + first_pair[1] * second_pair[1]) / denominator,
        (first_pair[1] * second_pair[0] - first_pair[0] * second_pair[1]) / denominator,
    )


def scale_field(factor, electric):
    real_factor = factor[0].reshape(-1, 1, 1, 1, 1)
    imag_factor = factor[1].reshape(-1, 1, 1, 1, 1)
    real_part = real_factor * electric[:, 0] - imag_factor * electric[:, 1]
    imag_part = real_factor * electric[:, 1] + imag_factor * electric[:, 0]
    return jnp.stack([real_part, imag_part], axis=1)


def local(conductivity, field_guess, tx_cell, rx_cell, rx_weight):
    depth_cells, lat_cells, width = conductivity.shape
    depth_index = lax.axis_index("depth")
    lat_index = lax.axis_index("lat")
    total_lat = lat_cells * lax.axis_size("lat")
    depth_keep = (depth_index > 0).astype(jnp.float32)
    lat_keep = (lat_index > 0).astype(jnp.float32)
    local_total = depth_cells * lat_cells * width

    def apply_operator(electric):
        padded = with_halo(electric, (("depth", 3), ("lat", 4)), 1)
        inner_block = padded[:, :, :, : depth_cells + 1, : lat_cells + 1]
        depth_ahead = padded[:, :, :, depth_cells + 1 :, : lat_cells + 1]
        lat_ahead = padded[:, :, :, : depth_cells + 1, lat_cells + 1 :]
        magnetic = curl_pair(inner_block, depth_ahead, lat_ahead, step_ahead)
        depth_behind = magnetic[:, :, :, :1, 1:] * depth_keep
        lat_behind = magnetic[:, :, :, 1:, :1] * lat_keep
        curled = curl_pair(magnetic[:, :, :, 1:, 1:], depth_behind, lat_behind, step_behind)
        real_part = curled[:, 0] - conductivity * electric[:, 1]
        imag_part = curled[:, 1] + conductivity * electric[:, 0]
        return jnp.stack([real_part, imag_part], axis=1)

    def place(cell_ids, amounts):
        depth_pos = cell_ids // (total_lat * width)
        lat_pos = cell_ids // width % total_lat
        span_pos = cell_ids % width
        local_depth = depth_pos - depth_index * depth_cells
        local_lat = lat_pos - lat_index * lat_cells
        inside = (
            (local_depth >= 0)
            & (local_depth < depth_cells)
            & (local_lat >= 0)
            & (local_lat < lat_cells)
        )
        local_flat = jnp.where(
            inside, (local_depth * lat_cells + local_lat) * width + span_pos, local_total
        )
        plane = jnp.zeros((local_total,), jnp.float32).at[local_flat].add(amounts, mode="drop")
        return plane.reshape(depth_cells, lat_cells, width)

    blank_plane = jnp.zeros((depth_cells, lat_cells, width), jnp.float32)
    tx_plane = place(tx_cell, jnp.full((1,), -source_amplitude, jnp.float32))
    rx_real = place(rx_cell[0], rx_weight[0, :, 0])
    rx_imag = place(rx_cell[0], rx_weight[0, :, 1])
    tx_side = jnp.stack(
        [
            jnp.stack([blank_plane, blank_plane, blank_plane]),
            jnp.stack([tx_plane, blank_plane, blank_plane]),
        ]
    )
    rx_side = jnp.stack(
        [
            jnp.stack([rx_real, blank_plane, blank_plane]),
            jnp.stack([rx_imag, blank_plane, blank_plane]),
        ]
    )
    start_field = field_guess[0]
    solution = start_field
    residual = jnp.stack([tx_side, rx_side]) - apply_operator(start_field)
    shadow = residual
    direction = residual
    start_pair = inner_local(shadow, residual)
    shadow_dot = sum_over_grid((start_pair[0], start_pair[1]))
    for iteration in range(ITERS):
        applied = apply_operator(direction)
        curve_pair = inner_local(shadow, applied)
        curve_sum = sum_over_grid((curve_pair[0], curve_pair[1]))
        step_length = complex_quotient(shadow_dot, curve_sum)
        halfway = residual - scale_field(step_length, applied)
        second = apply_operator(halfway)
        cross_pair = inner_local(second, halfway)
        energy = jnp.sum(second * second, axis=(1, 2, 3, 4, 5))
        cross_real, cross_imag, energy_sum = sum_over_grid((cross_pair[0], cross_pair[1], energy))
        relax_weight = (cross_real / energy_sum, cross_imag / energy_sum)
        solution = (
            solution + scale_field(step_length, direction) + scale_field(relax_weight, halfway)
        )
        residual = halfway - scale_field(relax_weight, second)
        if iteration + 1 < ITERS:
            next_pair = inner_local(shadow, residual)
            new_dot = sum_over_grid((next_pair[0], next_pair[1]))
            mixing = complex_product(
                complex_quotient(new_dot, shadow_dot), complex_quotient(step_length, relax_weight)
            )
            direction = residual + scale_field(
                mixing, direction - scale_field(relax_weight, applied)
            )
            shadow_dot = new_dot
    solutions = [solution]
    fields = jnp.stack(solutions)
    term = jnp.sum(
        fields[:, 0, 0] * fields[:, 1, 0] - fields[:, 0, 1] * fields[:, 1, 1], axis=(0, 1)
    )
    pieces = term.reshape(depth_cells, lat_cells, lax.axis_size("tx"), -1).transpose(2, 0, 1, 3)
    gradient = jnp.sum(lax.all_to_all(pieces, "tx", 0, 0), axis=0)
    return (fields, gradient)


def solution(mesh):
    return jax.shard_map(
        local,
        mesh=mesh,
        in_specs=(
            P("depth", "lat", None),
            P("tx", None, None, None, "depth", "lat", None),
            P("tx"),
            P("tx", None),
            P("tx", None, None),
        ),
        out_specs=(P("tx", None, None, None, "depth", "lat", None), P("depth", "lat", "tx")),
        check_vma=False,
    )
```

```python
import functools

import jax
import jax.numpy as jnp
from jax import lax
from jax.experimental import pallas as pl
from jax.experimental.pallas import tpu as pltpu
from jax.sharding import PartitionSpec as P

SOURCE = 20.0
KINDS = 2
BASIS = 5
ROWS = 8
LANES = 128
GRID_AXES = ("depth", "lat")
PAIRS = [(i, j) for i in range(BASIS) for j in range(i, BASIS)]
ENTRIES = [(i, j, part) for i, j in PAIRS for part in range(1 if i == j else 2)]
MIB = 1 << 20


def in_vmem():
    return pl.BlockSpec(memory_space=pltpu.VMEM)


def in_smem():
    return pl.BlockSpec(memory_space=pltpu.SMEM)


def slot(part, component, layer):
    return (part * 3 + component) * 2 + layer


def pack_kernel(pieces, guess_ref, cond_ref, out_ref):
    lane = lax.broadcasted_iota(jnp.int32, (ROWS, LANES), 1)
    blank = jnp.zeros((ROWS, LANES), jnp.float32)
    for kind in range(KINDS):
        for piece in range(pieces):
            to = kind * pieces + piece
            edges = [blank, blank]
            for item in range(14):

                def tile(number):
                    if number < 0 or number >= pieces:
                        return blank
                    cols = slice(number * LANES, (number + 1) * LANES)
                    if item < 12:
                        return guess_ref[kind * 12 + item, :, cols]
                    return cond_ref[item - 12, :, cols]

                out_ref[to, item] = tile(piece)
                ends = jnp.where(lane >= LANES // 2, tile(piece - 1), tile(piece + 1))
                place = item % 8
                moved = pltpu.roll(ends, (16 * place + 8) % LANES, 1)
                edges[item // 8] = jnp.where(lane // 16 == place, moved, edges[item // 8])
            out_ref[to, 14] = edges[0]
            out_ref[to, 15] = edges[1]


def two_sum(a, b):
    total = a + b
    other = total - a
    return total, (a - (total - other)) + (b - other)


def basis_kernel(
    sizes, tx_ref, rx_ref, weight_ref, left_ref, mid_ref, right_ref, basis_ref, gram_ref,
    field, curl, cond, inside, acc,
):
    depths, lats, pieces = sizes
    layers = 2 * depths
    wide = 3 * ROWS
    span = 2 * LANES
    depth_index = lax.axis_index("depth")
    lat_index = lax.axis_index("lat")
    kind = depth_index // pieces
    piece = depth_index % pieces
    lane = lax.broadcasted_iota(jnp.int32, (ROWS, LANES), 1)
    blank = jnp.zeros((ROWS, LANES), jnp.float32)

    row_w = lax.broadcasted_iota(jnp.int32, (wide, span), 0)
    lane_w = lax.broadcasted_iota(jnp.int32, (wide, span), 1)
    x_at = lat_index * ROWS - ROWS + row_w
    y_at = piece * LANES + jnp.where(lane_w >= LANES + 64, lane_w - span, lane_w)
    good = (x_at >= 0) & (x_at < lats * ROWS) & (y_at >= 0) & (y_at < pieces * LANES)
    inside[...] = jnp.where(good, 1.0, 0.0)

    for number, ref in enumerate((left_ref, mid_ref, right_ref)):
        rows = slice(number * ROWS, (number + 1) * ROWS)

        def spread(source, carry, ref=ref, rows=rows):
            for item in range(14):
                place = item % 8
                edge = pltpu.roll(ref[source, 14 + item // 8], LANES - (16 * place + 8), 1)
                edge = jnp.where((lane < 8) | (lane >= LANES - 8), edge, blank)
                body = ref[source, item]
                z = 2 * source + item % 2
                if item < 12:
                    field[0, item // 2, z, rows, 0:LANES] = body
                    field[0, item // 2, z, rows, LANES:span] = edge
                else:
                    cond[z, rows, 0:LANES] = body
                    cond[z, rows, LANES:span] = edge
            return carry

        lax.fori_loop(0, depths, spread, 0)

    empty = jnp.zeros((wide, span), jnp.float32)
    for number in range(BASIS):
        for component in range(6):
            field[number, component, layers] = empty

    def ahead(values, axis):
        return pltpu.roll(values, values.shape[axis] - 1, axis) - values

    def behind(values, axis):
        return values - pltpu.roll(values, 1, axis)

    for step in range(BASIS):
        for component in range(4):
            curl[component] = empty

        def apply_layer(z, carry, step=step):
            keep = inside[...]
            sigma = cond[z]
            for part in range(2):
                uz = field[step, part * 3, z]
                ux = field[step, part * 3 + 1, z]
                uy = field[step, part * 3 + 2, z]
                dz_ux = field[step, part * 3 + 1, z + 1] - ux
                dz_uy = field[step, part * 3 + 2, z + 1] - uy
                hz = (ahead(uy, 0) - ahead(ux, 1)) * keep
                hx = (ahead(uz, 1) - dz_uy) * keep
                hy = (dz_ux - ahead(uz, 0)) * keep
                dz_hx = hx - curl[part * 2]
                dz_hy = hy - curl[part * 2 + 1]
                curl[part * 2] = hx
                curl[part * 2 + 1] = hy
                outs = (
                    behind(hy, 0) - behind(hx, 1),
                    behind(hz, 1) - dz_hy,
                    dz_hx - behind(hz, 0),
                )
                for component, value in enumerate(outs):
                    other = sigma * field[step, (1 - part) * 3 + component, z]
                    value = value - other if part == 0 else value + other
                    if step == 0:
                        value = -value
                    field[step + 1, part * 3 + component, z] = value * keep
            return carry

        lax.fori_loop(0, layers, apply_layer, 0)

        if step == 0:
            line = lax.broadcasted_iota(jnp.int32, (1, span), 1)

            def add_source(cell, real, imag):
                y = cell % (pieces * LANES)
                x = cell // (pieces * LANES) % (lats * ROWS)
                z = cell // (pieces * LANES * lats * ROWS)
                row = x - lat_index * ROWS + ROWS
                col = y - piece * LANES

                @pl.when((row >= 0) & (row < wide) & (col >= -8) & (col < LANES + 8))
                def _():
                    hit = line == jnp.where(col < 0, col + span, col)
                    at = pl.ds(row, 1)
                    field[1, 0, z, at] = field[1, 0, z, at] + jnp.where(hit, real, 0.0)
                    field[1, 3, z, at] = field[1, 3, z, at] + jnp.where(hit, imag, 0.0)

            @pl.when(kind == 0)
            def _():
                add_source(tx_ref[0], jnp.float32(0.0), jnp.float32(-SOURCE))

            @pl.when(kind == 1)
            def _():
                def each(r, carry):
                    add_source(rx_ref[0, r], weight_ref[0, 2 * r], weight_ref[0, 2 * r + 1])
                    return carry

                lax.fori_loop(0, rx_ref.shape[1], each, 0)

    for entry in range(2 * len(ENTRIES)):
        acc[entry] = blank
    own = slice(ROWS, 2 * ROWS)

    def gram_layer(source, carry):
        for layer in range(2):
            z = 2 * source + layer
            tiles = [[field[b + 1, c, z, own, 0:LANES] for c in range(6)] for b in range(BASIS)]
            for b in range(BASIS - 1):
                for c in range(6):
                    basis_ref[b, source, 2 * c + layer] = tiles[b][c]
            for entry, (i, j, part) in enumerate(ENTRIES):
                first, second = tiles[i], tiles[j]
                if part == 0:
                    terms = [first[c] * second[c] for c in range(6)]
                    value = (terms[0] + terms[3]) + (terms[1] + terms[4]) + (terms[2] + terms[5])
                else:
                    terms = [first[c] * second[c + 3] - first[c + 3] * second[c] for c in range(3)]
                    value = terms[0] + terms[1] + terms[2]
                total, error = two_sum(acc[2 * entry], value)
                acc[2 * entry] = total
                acc[2 * entry + 1] = acc[2 * entry + 1] + error
        return carry

    lax.fori_loop(0, depths, gram_layer, 0)

    def fold(high, low, shift, axis):
        total, error = two_sum(high, pltpu.roll(high, shift, axis))
        return total, low + pltpu.roll(low, shift, axis) + error

    sub = lax.broadcasted_iota(jnp.int32, (ROWS, LANES), 0)
    row = blank
    for start in range(0, len(ENTRIES), 8):
        highs, lows = blank, blank
        for entry in range(start, min(start + 8, len(ENTRIES))):
            high, low = acc[2 * entry], acc[2 * entry + 1]
            for shift in (4, 2, 1):
                high, low = fold(high, low, shift, 0)
            highs = jnp.where(sub == entry - start, high, highs)
            lows = jnp.where(sub == entry - start, low, lows)
        for shift in (64, 32, 16, 8, 4, 2, 1):
            highs, lows = fold(highs, lows, shift, 1)
        row = jnp.where(lane == sub + start, highs, row)
        row = jnp.where(lane == sub + start + 64, lows, row)
    for shift in (4, 2, 1):
        row = row + pltpu.roll(row, shift, 0)
    for number in range(depths * lats // ROWS):
        gram_ref[number * ROWS : (number + 1) * ROWS] = row


def quick(a, b):
    total = a + b
    return total, b - (total - a)


def split(a):
    big = a * 4097.0
    high = big - (big - a)
    return high, a - high


def two_product(a, b):
    value = a * b
    ah, al = split(a)
    bh, bl = split(b)
    return value, ((ah * bh - value) + ah * bl + al * bh) + al * bl


def add(a, b):
    total, error = two_sum(a[0], b[0])
    return quick(total, error + (a[1] + b[1]))


def neg(a):
    return (-a[0], -a[1])


def mul(a, b):
    value, error = two_product(a[0], b[0])
    return quick(value, error + (a[0] * b[1] + a[1] * b[0]))


def div(a, b):
    first = a[0] / b[0]
    zero = jnp.zeros_like(first)
    rest = add(a, neg(mul(b, (first, zero))))
    second = rest[0] / b[0]
    rest = add(rest, neg(mul(b, (second, zero))))
    third = rest[0] / b[0]
    return add(quick(first, second), (third, zero))


def c_add(a, b):
    return (add(a[0], b[0]), add(a[1], b[1]))


def c_neg(a):
    return (neg(a[0]), neg(a[1]))


def c_conj(a):
    return (a[0], neg(a[1]))


def c_mul(a, b):
    return (
        add(mul(a[0], b[0]), neg(mul(a[1], b[1]))),
        add(mul(a[0], b[1]), mul(a[1], b[0])),
    )


def c_div(a, b):
    top = c_mul(a, c_conj(b))
    bottom = add(mul(b[0], b[0]), mul(b[1], b[1]))
    return (div(top[0], bottom), div(top[1], bottom))


def c_over(a, real):
    return (div(a[0], real), div(a[1], real))


def total_of(values):
    result = values[0]
    for value in values[1:]:
        result = c_add(result, value)
    return result


def coefficients(gram):
    rho = gram[0, 0]
    alpha = c_div(rho, gram[0, 1])
    one_half = c_neg(alpha)

    def form(coeffs, left, right):
        rows = []
        for i, factor in enumerate(coeffs):
            inner = total_of(
                [
                    gram[i + left, j + right]
                    if other is None
                    else c_mul(gram[i + left, j + right], other)
                    for j, other in enumerate(coeffs)
                ]
            )
            rows.append(inner if factor is None else c_mul(c_conj(factor), inner))
        return total_of(rows)

    omega = c_over(form([None, one_half], 1, 0), form([None, one_half], 1, 1)[0])
    res1 = c_neg(c_add(alpha, omega))
    res2 = c_mul(alpha, omega)
    new_rho = total_of([gram[0, 0], c_mul(gram[0, 1], res1), c_mul(gram[0, 2], res2)])
    mix = c_mul(c_div(new_rho, rho), c_div(alpha, omega))
    dir0 = (add((jnp.ones_like(mix[0][0]), jnp.zeros_like(mix[0][0])), mix[0]), mix[1])
    dir1 = c_add(res1, c_neg(c_mul(mix, omega)))
    dir2 = res2
    along = total_of(
        [c_mul(gram[0, 1], dir0), c_mul(gram[0, 2], dir1), c_mul(gram[0, 3], dir2)]
    )
    alpha2 = c_div(new_rho, along)
    half1 = c_add(res1, c_neg(c_mul(alpha2, dir0)))
    half2 = c_add(res2, c_neg(c_mul(alpha2, dir1)))
    half3 = c_neg(c_mul(alpha2, dir2))
    half = [None, half1, half2, half3]
    omega2 = c_over(form(half, 1, 0), form(half, 1, 1)[0])
    out0 = total_of([alpha, omega, c_mul(alpha2, dir0), omega2])
    out1 = total_of([c_mul(omega, one_half), c_mul(alpha2, dir1), c_mul(omega2, half1)])
    out2 = c_add(c_mul(alpha2, dir2), c_mul(omega2, half2))
    out3 = c_mul(omega2, half3)
    return [(c[0][0], c[1][0]) for c in (out0, out1, out2, out3)]


def update_kernel(sizes, rows_ref, start_ref, basis_ref, out_ref):
    depths, lats, pieces = sizes
    kind = lax.axis_index("depth") // pieces
    count = pieces * lats
    sub = lax.broadcasted_iota(jnp.int32, (ROWS, LANES), 0)
    high = jnp.zeros((ROWS, LANES), jnp.float32)
    low = high
    for number in range(KINDS * count // ROWS):
        mine = (sub >= kind * count - number * ROWS) & (sub < (kind + 1) * count - number * ROWS)
        rows = jnp.where(mine, rows_ref[number * ROWS : (number + 1) * ROWS], 0.0)
        high, error = two_sum(high, rows)
        low = low + error
    for shift in (4, 2, 1):
        high, error = two_sum(high, pltpu.roll(high, shift, 0))
        low = low + pltpu.roll(low, shift, 0) + error
    high, low = quick(high, low + pltpu.roll(high, 64, 1))

    def entry(number):
        return (
            jnp.broadcast_to(high[:, number : number + 1], (ROWS, LANES)),
            jnp.broadcast_to(low[:, number : number + 1], (ROWS, LANES)),
        )

    zero = jnp.zeros((ROWS, LANES), jnp.float32)
    gram = {}
    at = 0
    for i, j in PAIRS:
        real = entry(at)
        at += 1
        if i == j:
            gram[i, i] = (real, (zero, zero))
        else:
            gram[i, j] = (real, entry(at))
            gram[j, i] = c_conj(gram[i, j])
            at += 1
    factors = coefficients(gram)

    def layer(source, carry):
        for component in range(3):
            for z in range(2):
                real = start_ref[source, slot(0, component, z)]
                imag = start_ref[source, slot(1, component, z)]
                for b, (fr, fi) in enumerate(factors):
                    br = basis_ref[b, source, slot(0, component, z)]
                    bi = basis_ref[b, source, slot(1, component, z)]
                    real = real + (fr * br - fi * bi)
                    imag = imag + (fr * bi + fi * br)
                out_ref[source, slot(0, component, z)] = real
                out_ref[source, slot(1, component, z)] = imag
        return carry

    lax.fori_loop(0, depths, layer, 0)


def output_kernel(pieces, in_ref, field_ref, term_ref):
    for piece in range(pieces):
        cols = slice(piece * LANES, (piece + 1) * LANES)
        for z in range(2):
            term = None
            for component in range(3):
                values = []
                for kind in range(KINDS):
                    for part in range(2):
                        value = in_ref[kind * pieces + piece, slot(part, component, z)]
                        field_ref[kind * 12 + slot(part, component, z), :, cols] = value
                        values.append(value)
                product = values[0] * values[2] - values[1] * values[3]
                term = product if term is None else term + product
            term_ref[piece, z] = term


def local(conductivity, field_guess, tx_cell, rx_cell, rx_weight):
    depths, lats = lax.axis_size("depth"), lax.axis_size("lat")
    pieces = depths // KINDS
    sizes = (depths, lats, pieces)
    width = conductivity.shape[2]
    layers = 2 * depths
    f32 = jnp.float32
    params = pltpu.CompilerParams

    packed = pl.pallas_call(
        functools.partial(pack_kernel, pieces),
        out_shape=jax.ShapeDtypeStruct((depths, 16, ROWS, LANES), f32),
        in_specs=[in_vmem()] * 2,
        out_specs=in_vmem(),
        compiler_params=params(vmem_limit_bytes=4 * MIB),
    )(field_guess.reshape(24, ROWS, width), conductivity)
    mid = lax.all_to_all(packed, "depth", 0, 0)
    left = lax.ppermute(mid, "lat", [(i, i + 1) for i in range(lats - 1)])
    right = lax.ppermute(mid, "lat", [(i + 1, i) for i in range(lats - 1)])

    basis, rows = pl.pallas_call(
        functools.partial(basis_kernel, sizes),
        out_shape=(
            jax.ShapeDtypeStruct((BASIS - 1, depths, 12, ROWS, LANES), f32),
            jax.ShapeDtypeStruct((depths * lats, LANES), f32),
        ),
        in_specs=[in_smem()] * 3 + [in_vmem()] * 3,
        out_specs=(in_vmem(), in_vmem()),
        scratch_shapes=[
            pltpu.VMEM((BASIS + 1, 6, layers + 1, 3 * ROWS, 2 * LANES), f32),
            pltpu.VMEM((4, 3 * ROWS, 2 * LANES), f32),
            pltpu.VMEM((layers, 3 * ROWS, 2 * LANES), f32),
            pltpu.VMEM((3 * ROWS, 2 * LANES), f32),
            pltpu.VMEM((2 * len(ENTRIES), ROWS, LANES), f32),
        ],
        compiler_params=params(vmem_limit_bytes=28 * MIB),
    )(tx_cell, rx_cell, rx_weight.reshape(1, -1), left, mid, right)

    rows = lax.all_to_all(rows, GRID_AXES, 0, 0)
    moved = pl.pallas_call(
        functools.partial(update_kernel, sizes),
        out_shape=jax.ShapeDtypeStruct((depths, 12, ROWS, LANES), f32),
        in_specs=[in_vmem()] * 3,
        out_specs=in_vmem(),
        compiler_params=params(vmem_limit_bytes=8 * MIB),
    )(rows, mid, basis)
    moved = lax.all_to_all(moved, "depth", 0, 0)
    fields, terms = pl.pallas_call(
        functools.partial(output_kernel, pieces),
        out_shape=(
            jax.ShapeDtypeStruct((24, ROWS, width), f32),
            jax.ShapeDtypeStruct((pieces, 2, ROWS, LANES), f32),
        ),
        in_specs=[in_vmem()],
        out_specs=(in_vmem(), in_vmem()),
        compiler_params=params(vmem_limit_bytes=4 * MIB),
    )(moved)
    gradient = jnp.sum(lax.all_to_all(terms, "tx", 0, 0), axis=0)
    return (fields.reshape(field_guess.shape), gradient)


def solution(mesh):
    return jax.shard_map(
        local,
        mesh=mesh,
        in_specs=(
            P("depth", "lat", None),
            P("tx", None, None, None, "depth", "lat", None),
            P("tx"),
            P("tx", None),
            P("tx", None, None),
        ),
        out_specs=(P("tx", None, None, None, "depth", "lat", None), P("depth", "lat", "tx")),
        check_vma=False,
    )
```

```python
import functools

import jax
import jax.numpy as jnp
from jax import lax
from jax.experimental import pallas as pl
from jax.experimental.pallas import tpu as pltpu
from jax.sharding import Mesh
from jax.sharding import PartitionSpec as P

SOURCE = 20.0
KINDS = 2
BASIS = 5
ROWS = 8
LANES = 128
DEPTH = ("kind", "piece")
PAIRS = [(i, j) for i in range(BASIS) for j in range(i, BASIS)]
ENTRIES = [(i, j, part) for i, j in PAIRS for part in range(1 if i == j else 2)]
MIB = 1 << 20


def in_vmem():
    return pl.BlockSpec(memory_space=pltpu.VMEM)


def in_smem():
    return pl.BlockSpec(memory_space=pltpu.SMEM)


def slot(part, component, layer):
    return (part * 3 + component) * 2 + layer


def pack_kernel(pieces, guess_ref, cond_ref, out_ref):
    lane = lax.broadcasted_iota(jnp.int32, (ROWS, LANES), 1)
    blank = jnp.zeros((ROWS, LANES), jnp.float32)
    for kind in range(KINDS):
        for piece in range(pieces):
            to = kind * pieces + piece
            edges = [blank, blank]
            for item in range(14):

                def tile(number):
                    if number < 0 or number >= pieces:
                        return blank
                    cols = slice(number * LANES, (number + 1) * LANES)
                    if item < 12:
                        return guess_ref[kind * 12 + item, :, cols]
                    return cond_ref[item - 12, :, cols]

                out_ref[to, item] = tile(piece)
                ends = jnp.where(lane >= LANES // 2, tile(piece - 1), tile(piece + 1))
                place = item % 8
                moved = pltpu.roll(ends, (16 * place + 8) % LANES, 1)
                edges[item // 8] = jnp.where(lane // 16 == place, moved, edges[item // 8])
            out_ref[to, 14] = edges[0]
            out_ref[to, 15] = edges[1]


def two_sum(a, b):
    total = a + b
    other = total - a
    return total, (a - (total - other)) + (b - other)


def basis_scratch(depths):
    layers = 2 * depths
    f32 = jnp.float32
    return [
        pltpu.VMEM((BASIS, 6, layers + 1, 2 * ROWS, 2 * LANES), f32),
        pltpu.VMEM((7, layers, 3 * ROWS, LANES), f32),
        pltpu.VMEM((4, 3 * ROWS, 2 * LANES), f32),
        pltpu.VMEM((4, 2 * ROWS, 2 * LANES), f32),
        pltpu.VMEM((layers, 2 * ROWS, 2 * LANES), f32),
        pltpu.VMEM((3 * ROWS, 2 * LANES), f32),
        pltpu.VMEM((2 * ROWS, 2 * LANES), f32),
        pltpu.VMEM((2 * len(ENTRIES), ROWS, LANES), f32),
    ]


def basis_kernel(
    sizes, tx_ref, rx_ref, weight_ref, left_ref, mid_ref, right_ref, basis_ref, gram_ref,
    field, edges, curl_start, curl, cond, inside_start, inside, acc,
):
    depths, lats, pieces = sizes
    layers = 2 * depths
    span = 2 * LANES
    width = pieces * LANES
    lat_index = lax.axis_index("lat")
    kind = lax.axis_index("kind")
    piece = lax.axis_index("piece")
    lane = lax.broadcasted_iota(jnp.int32, (ROWS, LANES), 1)
    blank = jnp.zeros((ROWS, LANES), jnp.float32)

    def within(rows, row):
        lane_w = lax.broadcasted_iota(jnp.int32, (rows, span), 1)
        x_at = lat_index * ROWS + row
        y_at = piece * LANES + jnp.where(lane_w >= LANES + 64, lane_w - span, lane_w)
        good = (x_at >= 0) & (x_at < lats * ROWS) & (y_at >= 0) & (y_at < width)
        return jnp.where(good, 1.0, 0.0)

    row_s = lax.broadcasted_iota(jnp.int32, (3 * ROWS, span), 0)
    inside_start[...] = within(3 * ROWS, row_s - ROWS)
    row_b = lax.broadcasted_iota(jnp.int32, (2 * ROWS, span), 0)
    inside[...] = within(2 * ROWS, jnp.where(row_b >= 12, row_b - 16, row_b))

    received = (left_ref, mid_ref, right_ref)

    def spread(source, carry):
        for number, ref in enumerate(received):
            packs = [ref[source, 14], ref[source, 15]]
            for item in range(14):
                edge = pltpu.roll(packs[item // 8], LANES - (16 * (item % 8) + 8), 1)
                edge = jnp.where((lane < 8) | (lane >= LANES - 8), edge, blank)
                at = slice(number * ROWS, (number + 1) * ROWS)
                edges[item // 2, 2 * source + item % 2, at] = edge
        return carry

    lax.fori_loop(0, depths, spread, 0, unroll=2)

    empty = jnp.zeros((2 * ROWS, span), jnp.float32)
    for number in range(BASIS - 1):
        for component in range(6):
            field[number, component, layers] = empty

    def ahead(values, axis):
        return pltpu.roll(values, values.shape[axis] - 1, axis) - values

    def behind(values, axis):
        return values - pltpu.roll(values, 1, axis)

    def curl_ahead(here, above, keep):
        uz, ux, uy = here
        hz = (ahead(uy, 0) - ahead(ux, 1)) * keep
        hx = (ahead(uz, 1) - (above[1] - uy)) * keep
        hy = ((above[0] - ux) - ahead(uz, 0)) * keep
        return hz, hx, hy

    def curl_behind(h, below):
        hz, hx, hy = h
        return (
            behind(hy, 0) - behind(hx, 1),
            behind(hz, 1) - (hy - below[1]),
            (hx - below[0]) - behind(hz, 0),
        )

    def start_tile(number, z, source, layer):
        body = jnp.concatenate([ref[source, 2 * number + layer] for ref in received], axis=0)
        return jnp.concatenate([body, edges[number, z]], axis=1)

    def merge(values):
        sub = lax.broadcasted_iota(jnp.int32, (ROWS, span), 0)
        sides = jnp.where(sub < 4, values[2 * ROWS :], values[:ROWS])
        return jnp.concatenate([values[ROWS : 2 * ROWS], sides], axis=0)

    for number in range(4):
        curl_start[number] = jnp.zeros((3 * ROWS, span), jnp.float32)

    def start_layers(source, carry):
        keep = inside_start[...]
        below = [[curl_start[0], curl_start[1]], [curl_start[2], curl_start[3]]]
        for layer in range(2):
            z = 2 * source + layer
            tiles = [start_tile(c, z, source, layer) for c in range(6)]
            sigma = start_tile(6, z, source, layer)
            cond[z] = merge(sigma)
            for part in range(2):
                here = tiles[3 * part : 3 * part + 3]
                if layer == 0:
                    above = [start_tile(3 * part + c, z + 1, source, 1) for c in (1, 2)]
                else:
                    last = source == depths - 1
                    after = jnp.minimum(source + 1, depths - 1)
                    above = [
                        jnp.where(last, 0.0, start_tile(3 * part + c, 2 * after, after, 0))
                        for c in (1, 2)
                    ]
                h = curl_ahead(here, above, keep)
                outs = curl_behind(h, below[part])
                below[part] = [h[1], h[2]]
                for component, value in enumerate(outs):
                    other = sigma * tiles[3 * (1 - part) + component]
                    value = other - value if part == 0 else -value - other
                    field[0, 3 * part + component, z] = merge(value) * inside[...]
        for number in range(4):
            curl_start[number] = below[number // 2][number % 2]
        return carry

    lax.fori_loop(0, depths, start_layers, 0)

    line = lax.broadcasted_iota(jnp.int32, (1, span), 1)

    def add_source(cell, real, imag):
        col = (cell & (width - 1)) - piece * LANES
        rest = lax.shift_right_logical(cell, width.bit_length() - 1)
        row = (rest & (lats * ROWS - 1)) - lat_index * ROWS
        z = lax.shift_right_logical(rest, (lats * ROWS).bit_length() - 1)

        @pl.when((row >= -4) & (row < 12) & (col >= -8) & (col < LANES + 8))
        def _():
            hit = line == (col & (span - 1))
            at = pl.ds(row & (2 * ROWS - 1), 1)
            field[0, 0, z, at] = field[0, 0, z, at] + jnp.where(hit, real, 0.0)
            field[0, 3, z, at] = field[0, 3, z, at] + jnp.where(hit, imag, 0.0)

    @pl.when(kind == 0)
    def _():
        add_source(tx_ref[0], jnp.float32(0.0), jnp.float32(-SOURCE))

    @pl.when(kind == 1)
    def _():
        def each(r, carry):
            add_source(rx_ref[0, r], weight_ref[0, 2 * r], weight_ref[0, 2 * r + 1])
            return carry

        lax.fori_loop(0, rx_ref.shape[1], each, 0)

    for step in range(BASIS - 1):
        for number in range(4):
            curl[number] = empty

        def apply_layers(source, carry, step=step):
            keep = inside[...]
            below = [[curl[0], curl[1]], [curl[2], curl[3]]]
            for layer in range(2):
                z = 2 * source + layer
                sigma = cond[z]
                for part in range(2):
                    here = [field[step, 3 * part + c, z] for c in range(3)]
                    above = [field[step, 3 * part + c, z + 1] for c in (1, 2)]
                    h = curl_ahead(here, above, keep)
                    outs = curl_behind(h, below[part])
                    below[part] = [h[1], h[2]]
                    for component, value in enumerate(outs):
                        if step == BASIS - 2:
                            mine = (slice(0, ROWS), slice(0, LANES))
                        else:
                            mine = (slice(None), slice(None))
                        near = field[(step, 3 * (1 - part) + component, z) + mine]
                        other = sigma[mine] * near
                        value = value[mine]
                        value = value - other if part == 0 else value + other
                        if step < BASIS - 2:
                            value = value * keep
                        field[(step + 1, 3 * part + component, z) + mine] = value
            for number in range(4):
                curl[number] = below[number // 2][number % 2]
            return carry

        lax.fori_loop(0, depths, apply_layers, 0, unroll=2)

    for entry in range(2 * len(ENTRIES)):
        acc[entry] = blank

    def gram_layer(source, carry):
        for layer in range(2):
            z = 2 * source + layer
            tiles = [[field[b, c, z, 0:ROWS, 0:LANES] for c in range(6)] for b in range(BASIS)]
            for b in range(BASIS - 1):
                for c in range(6):
                    basis_ref[b, source, 2 * c + layer] = tiles[b][c]
            for entry, (i, j, part) in enumerate(ENTRIES):
                first, second = tiles[i], tiles[j]
                if part == 0:
                    terms = [first[c] * second[c] for c in range(6)]
                    value = (terms[0] + terms[3]) + (terms[1] + terms[4]) + (terms[2] + terms[5])
                else:
                    terms = [first[c] * second[c + 3] - first[c + 3] * second[c] for c in range(3)]
                    value = terms[0] + terms[1] + terms[2]
                total, error = two_sum(acc[2 * entry], value)
                acc[2 * entry] = total
                acc[2 * entry + 1] = acc[2 * entry + 1] + error
        return carry

    lax.fori_loop(0, depths, gram_layer, 0, unroll=2)

    def fold(high, low, shift, axis):
        total, error = two_sum(high, pltpu.roll(high, shift, axis))
        return total, low + pltpu.roll(low, shift, axis) + error

    sub = lax.broadcasted_iota(jnp.int32, (ROWS, LANES), 0)
    row = blank
    for start in range(0, len(ENTRIES), 8):
        highs, lows = blank, blank
        for entry in range(start, min(start + 8, len(ENTRIES))):
            high, low = acc[2 * entry], acc[2 * entry + 1]
            for shift in (4, 2, 1):
                high, low = fold(high, low, shift, 0)
            highs = jnp.where(sub == entry - start, high, highs)
            lows = jnp.where(sub == entry - start, low, lows)
        for shift in (64, 32, 16, 8, 4, 2, 1):
            highs, lows = fold(highs, lows, shift, 1)
        row = jnp.where(lane == sub + start, highs, row)
        row = jnp.where(lane == sub + start + 64, lows, row)
    for shift in (4, 2, 1):
        row = row + pltpu.roll(row, shift, 0)
    for number in range(pieces * lats // ROWS):
        gram_ref[number * ROWS : (number + 1) * ROWS] = row


def quick(a, b):
    total = a + b
    return total, b - (total - a)


def split(a):
    big = a * 4097.0
    high = big - (big - a)
    return high, a - high


def two_product(a, b):
    value = a * b
    ah, al = split(a)
    bh, bl = split(b)
    return value, ((ah * bh - value) + ah * bl + al * bh) + al * bl


def add(a, b):
    total, error = two_sum(a[0], b[0])
    return quick(total, error + (a[1] + b[1]))


def neg(a):
    return (-a[0], -a[1])


def mul(a, b):
    value, error = two_product(a[0], b[0])
    return quick(value, error + (a[0] * b[1] + a[1] * b[0]))


def div(a, b):
    first = a[0] / b[0]
    zero = jnp.zeros_like(first)
    rest = add(a, neg(mul(b, (first, zero))))
    second = rest[0] / b[0]
    rest = add(rest, neg(mul(b, (second, zero))))
    third = rest[0] / b[0]
    return add(quick(first, second), (third, zero))


def c_add(a, b):
    return (add(a[0], b[0]), add(a[1], b[1]))


def c_neg(a):
    return (neg(a[0]), neg(a[1]))


def c_conj(a):
    return (a[0], neg(a[1]))


def c_mul(a, b):
    return (
        add(mul(a[0], b[0]), neg(mul(a[1], b[1]))),
        add(mul(a[0], b[1]), mul(a[1], b[0])),
    )


def c_div(a, b):
    top = c_mul(a, c_conj(b))
    bottom = add(mul(b[0], b[0]), mul(b[1], b[1]))
    return (div(top[0], bottom), div(top[1], bottom))


def c_over(a, real):
    return (div(a[0], real), div(a[1], real))


def total_of(values):
    result = values[0]
    for value in values[1:]:
        result = c_add(result, value)
    return result


def coefficients(gram):
    rho = gram[0, 0]
    alpha = c_div(rho, gram[0, 1])
    one_half = c_neg(alpha)

    def form(coeffs, left, right):
        rows = []
        for i, factor in enumerate(coeffs):
            inner = total_of(
                [
                    gram[i + left, j + right]
                    if other is None
                    else c_mul(gram[i + left, j + right], other)
                    for j, other in enumerate(coeffs)
                ]
            )
            rows.append(inner if factor is None else c_mul(c_conj(factor), inner))
        return total_of(rows)

    omega = c_over(form([None, one_half], 1, 0), form([None, one_half], 1, 1)[0])
    res1 = c_neg(c_add(alpha, omega))
    res2 = c_mul(alpha, omega)
    new_rho = total_of([gram[0, 0], c_mul(gram[0, 1], res1), c_mul(gram[0, 2], res2)])
    mix = c_mul(c_div(new_rho, rho), c_div(alpha, omega))
    dir0 = (add((jnp.ones_like(mix[0][0]), jnp.zeros_like(mix[0][0])), mix[0]), mix[1])
    dir1 = c_add(res1, c_neg(c_mul(mix, omega)))
    dir2 = res2
    along = total_of(
        [c_mul(gram[0, 1], dir0), c_mul(gram[0, 2], dir1), c_mul(gram[0, 3], dir2)]
    )
    alpha2 = c_div(new_rho, along)
    half1 = c_add(res1, c_neg(c_mul(alpha2, dir0)))
    half2 = c_add(res2, c_neg(c_mul(alpha2, dir1)))
    half3 = c_neg(c_mul(alpha2, dir2))
    half = [None, half1, half2, half3]
    omega2 = c_over(form(half, 1, 0), form(half, 1, 1)[0])
    out0 = total_of([alpha, omega, c_mul(alpha2, dir0), omega2])
    out1 = total_of([c_mul(omega, one_half), c_mul(alpha2, dir1), c_mul(omega2, half1)])
    out2 = c_add(c_mul(alpha2, dir2), c_mul(omega2, half2))
    out3 = c_mul(omega2, half3)
    return [(c[0][0], c[1][0]) for c in (out0, out1, out2, out3)]


def update_kernel(sizes, rows_ref, start_ref, basis_ref, out_ref):
    depths, lats, pieces = sizes
    high = jnp.zeros((ROWS, LANES), jnp.float32)
    low = high
    for number in range(pieces * lats // ROWS):
        high, error = two_sum(high, rows_ref[number * ROWS : (number + 1) * ROWS])
        low = low + error
    for shift in (4, 2, 1):
        high, error = two_sum(high, pltpu.roll(high, shift, 0))
        low = low + pltpu.roll(low, shift, 0) + error
    high, low = quick(high, low + pltpu.roll(high, 64, 1))

    def entry(number):
        return (
            jnp.broadcast_to(high[:, number : number + 1], (ROWS, LANES)),
            jnp.broadcast_to(low[:, number : number + 1], (ROWS, LANES)),
        )

    zero = jnp.zeros((ROWS, LANES), jnp.float32)
    gram = {}
    at = 0
    for i, j in PAIRS:
        real = entry(at)
        at += 1
        if i == j:
            gram[i, i] = (real, (zero, zero))
        else:
            gram[i, j] = (real, entry(at))
            gram[j, i] = c_conj(gram[i, j])
            at += 1
    factors = coefficients(gram)

    def layer(source, carry):
        for component in range(3):
            for z in range(2):
                real = start_ref[source, slot(0, component, z)]
                imag = start_ref[source, slot(1, component, z)]
                for b, (fr, fi) in enumerate(factors):
                    br = basis_ref[b, source, slot(0, component, z)]
                    bi = basis_ref[b, source, slot(1, component, z)]
                    real = real + (fr * br - fi * bi)
                    imag = imag + (fr * bi + fi * br)
                out_ref[source, slot(0, component, z)] = real
                out_ref[source, slot(1, component, z)] = imag
        return carry

    lax.fori_loop(0, depths, layer, 0)


def output_kernel(pieces, in_ref, field_ref, term_ref):
    for piece in range(pieces):
        cols = slice(piece * LANES, (piece + 1) * LANES)
        for z in range(2):
            term = None
            for component in range(3):
                values = []
                for kind in range(KINDS):
                    for part in range(2):
                        value = in_ref[kind * pieces + piece, slot(part, component, z)]
                        field_ref[kind * 12 + slot(part, component, z), :, cols] = value
                        values.append(value)
                product = values[0] * values[2] - values[1] * values[3]
                term = product if term is None else term + product
            term_ref[piece, z] = term


def local(conductivity, field_guess, tx_cell, rx_cell, rx_weight):
    pieces, lats = lax.axis_size("piece"), lax.axis_size("lat")
    depths = KINDS * pieces
    sizes = (depths, lats, pieces)
    width = conductivity.shape[2]
    layers = 2 * depths
    f32 = jnp.float32
    params = pltpu.CompilerParams

    packed = pl.pallas_call(
        functools.partial(pack_kernel, pieces),
        out_shape=jax.ShapeDtypeStruct((depths, 16, ROWS, LANES), f32),
        in_specs=[in_vmem()] * 2,
        out_specs=in_vmem(),
        compiler_params=params(vmem_limit_bytes=4 * MIB),
    )(field_guess.reshape(24, ROWS, width), conductivity)
    mid = lax.all_to_all(packed, DEPTH, 0, 0)
    left = lax.ppermute(mid, "lat", [(i, i + 1) for i in range(lats - 1)])
    right = lax.ppermute(mid, "lat", [(i + 1, i) for i in range(lats - 1)])

    basis, rows = pl.pallas_call(
        functools.partial(basis_kernel, sizes),
        out_shape=(
            jax.ShapeDtypeStruct((BASIS - 1, depths, 12, ROWS, LANES), f32),
            jax.ShapeDtypeStruct((pieces * lats, LANES), f32),
        ),
        in_specs=[in_smem()] * 3 + [in_vmem()] * 3,
        out_specs=(in_vmem(), in_vmem()),
        scratch_shapes=basis_scratch(depths),
        compiler_params=params(vmem_limit_bytes=28 * MIB),
    )(tx_cell, rx_cell, rx_weight.reshape(1, -1), left, mid, right)

    rows = lax.all_to_all(rows, ("piece", "lat"), 0, 0)
    moved = pl.pallas_call(
        functools.partial(update_kernel, sizes),
        out_shape=jax.ShapeDtypeStruct((depths, 12, ROWS, LANES), f32),
        in_specs=[in_vmem()] * 3,
        out_specs=in_vmem(),
        compiler_params=params(vmem_limit_bytes=8 * MIB),
    )(rows, mid, basis)
    moved = lax.all_to_all(moved, DEPTH, 0, 0)
    fields, terms = pl.pallas_call(
        functools.partial(output_kernel, pieces),
        out_shape=(
            jax.ShapeDtypeStruct((24, ROWS, width), f32),
            jax.ShapeDtypeStruct((pieces, 2, ROWS, LANES), f32),
        ),
        in_specs=[in_vmem()],
        out_specs=(in_vmem(), in_vmem()),
        compiler_params=params(vmem_limit_bytes=4 * MIB),
    )(moved)
    gradient = jnp.sum(lax.all_to_all(terms, "tx", 0, 0), axis=0)
    return (fields.reshape(field_guess.shape), gradient)


def solution(mesh):
    grid = mesh.devices
    split = Mesh(
        grid.reshape((KINDS, grid.shape[0] // KINDS) + grid.shape[1:]),
        DEPTH + tuple(mesh.axis_names[1:]),
    )
    return jax.shard_map(
        local,
        mesh=split,
        in_specs=(
            P(DEPTH, "lat", None),
            P("tx", None, None, None, DEPTH, "lat", None),
            P("tx"),
            P("tx", None),
            P("tx", None, None),
        ),
        out_specs=(P("tx", None, None, None, DEPTH, "lat", None), P(DEPTH, "lat", "tx")),
        check_vma=False,
    )
```

```python
import functools

import jax
import jax.numpy as jnp
from jax import lax
from jax.experimental import pallas as pl
from jax.experimental.pallas import tpu as pltpu
from jax.sharding import Mesh
from jax.sharding import PartitionSpec as P

SOURCE = 20.0
KINDS = 2
BASIS = 5
ROWS = 8
LANES = 128
HALF = 64
OWN_ROWS = 2 * ROWS
BASIS_ROWS = OWN_ROWS + ROWS
START_ROWS = OWN_ROWS + 2 * ROWS
DEPTH = ("kind", "piece")
LAT = ("chip", "core")
SPREAD = ("core",) + DEPTH
PAIRS = [(i, j) for i in range(BASIS) for j in range(i, BASIS)]
ENTRIES = [(i, j, part) for i, j in PAIRS for part in range(1 if i == j else 2)]
MIB = 1 << 20


def in_vmem():
    return pl.BlockSpec(memory_space=pltpu.VMEM)


def in_smem():
    return pl.BlockSpec(memory_space=pltpu.SMEM)


def pack_kernel(pieces, guess_ref, cond_ref, out_ref):
    lane = lax.broadcasted_iota(jnp.int32, (ROWS, LANES), 1)
    low = lane < HALF
    blank = jnp.zeros((ROWS, LANES), jnp.float32)
    for kind in range(KINDS):
        planes = []
        for layer in range(2):
            group = []
            for ref, row in [(guess_ref, kind * 12 + n * 2 + layer) for n in range(6)] + [
                (cond_ref, layer)
            ]:
                straight = [ref[row, :, n * LANES : (n + 1) * LANES] for n in range(pieces)]
                group.append((straight, [pltpu.roll(v, HALF, 1) for v in straight]))
            planes.append(group)
        for piece in range(pieces):
            for core in range(2):
                to = (core * KINDS + kind) * pieces + piece
                for number in range(7):
                    first = planes[0][number][core]
                    second = planes[1][number][1 - core]
                    out_ref[to, number] = jnp.where(low, first[piece], second[piece])
                for layer in range(2):
                    edge = blank
                    for number in range(7):
                        straight, turned = planes[layer][number]
                        if core:
                            right = straight[piece + 1] if piece + 1 < pieces else blank
                            left = straight[piece]
                        else:
                            right = turned[piece]
                            left = turned[piece - 1] if piece > 0 else blank
                        ends = jnp.where(lane < 32, right, left)
                        at = 8 * number
                        ends = pltpu.roll(ends, at, 1) if at else ends
                        here = (lane // 8 == number) | (lane // 8 == number + 7)
                        edge = jnp.where(here, ends, edge)
                    out_ref[to, 7 + layer] = edge


def two_sum(a, b):
    total = a + b
    other = total - a
    return total, (a - (total - other)) + (b - other)


def basis_scratch(depths):
    layers = 2 * depths
    f32 = jnp.float32
    return [
        pltpu.VMEM((BASIS, 6, layers + 1, BASIS_ROWS, LANES), f32),
        pltpu.VMEM((7, layers + 1, START_ROWS, LANES), f32),
        pltpu.VMEM((4, START_ROWS, LANES), f32),
        pltpu.VMEM((4, BASIS_ROWS, LANES), f32),
        pltpu.VMEM((layers, BASIS_ROWS, LANES), f32),
        pltpu.VMEM((START_ROWS, LANES), f32),
        pltpu.VMEM((BASIS_ROWS, LANES), f32),
        pltpu.VMEM((2 * len(ENTRIES), ROWS, LANES), f32),
    ]


def basis_kernel(
    sizes, tx_ref, rx_ref, weight_ref, left_ref, mid_ref, right_ref, basis_ref, gram_ref,
    field, start, curl_start, curl, cond, inside_start, inside, acc,
):
    depths, chips, pieces = sizes
    layers = 2 * depths
    width = pieces * LANES
    x_size = chips * OWN_ROWS
    chip = lax.axis_index("chip")
    kind = lax.axis_index("kind")
    x_first = chip * OWN_ROWS
    y_first = (lax.axis_index("piece") * 2 + lax.axis_index("core")) * HALF
    lane = lax.broadcasted_iota(jnp.int32, (ROWS, LANES), 1)
    low = lane < HALF
    blank = jnp.zeros((ROWS, LANES), jnp.float32)

    def within(rows, row):
        lane_w = lax.broadcasted_iota(jnp.int32, (rows, LANES), 1)
        x_at = x_first + row
        y_at = y_first + jnp.where(lane_w >= 96, lane_w - LANES, lane_w)
        good = (x_at >= 0) & (x_at < x_size) & (y_at >= 0) & (y_at < width)
        return jnp.where(good, 1.0, 0.0)

    row_s = lax.broadcasted_iota(jnp.int32, (START_ROWS, LANES), 0)
    inside_start[...] = within(START_ROWS, row_s - ROWS)
    row_b = lax.broadcasted_iota(jnp.int32, (BASIS_ROWS, LANES), 0)
    inside[...] = within(BASIS_ROWS, jnp.where(row_b >= 20, row_b - BASIS_ROWS, row_b))

    received = ((left_ref, 0), (mid_ref, 0), (mid_ref, depths), (right_ref, 0))
    rim = (lane < HALF + 8) | (lane >= LANES - 8)

    def spread(source, carry):
        for number, (ref, first) in enumerate(received):
            at = slice(number * ROWS, (number + 1) * ROWS)
            packs = [ref[first + source, 7], ref[first + source, 8]]
            for item in range(7):
                both = ref[first + source, item]
                for layer in range(2):
                    edge = pltpu.roll(packs[layer], HALF - 8 * item, 1)
                    body = pltpu.roll(both, HALF, 1) if layer else both
                    tile = jnp.where(low, body, jnp.where(rim, edge, 0.0))
                    start[item, 2 * source + layer, at] = tile
        return carry

    lax.fori_loop(0, depths, spread, 0, unroll=2)

    empty_start = jnp.zeros((START_ROWS, LANES), jnp.float32)
    empty = jnp.zeros((BASIS_ROWS, LANES), jnp.float32)
    for component in range(6):
        start[component, layers] = empty_start
        for number in range(BASIS - 1):
            field[number, component, layers] = empty

    def ahead(values, axis):
        return pltpu.roll(values, values.shape[axis] - 1, axis) - values

    def behind(values, axis):
        return values - pltpu.roll(values, 1, axis)

    def curl_ahead(here, above, keep):
        uz, ux, uy = here
        hz = (ahead(uy, 0) - ahead(ux, 1)) * keep
        hx = (ahead(uz, 1) - (above[1] - uy)) * keep
        hy = ((above[0] - ux) - ahead(uz, 0)) * keep
        return hz, hx, hy

    def curl_behind(h, below):
        hz, hx, hy = h
        return (
            behind(hy, 0) - behind(hx, 1),
            behind(hz, 1) - (hy - below[1]),
            (hx - below[0]) - behind(hz, 0),
        )

    def merge(values):
        sides = jnp.where(
            lax.broadcasted_iota(jnp.int32, (ROWS, LANES), 0) < 4,
            values[START_ROWS - ROWS :],
            values[:ROWS],
        )
        return jnp.concatenate([values[ROWS : ROWS + OWN_ROWS], sides], axis=0)

    for number in range(4):
        curl_start[number] = empty_start

    def start_layers(source, carry):
        keep = inside_start[...]
        below = [[curl_start[0], curl_start[1]], [curl_start[2], curl_start[3]]]
        for layer in range(2):
            z = 2 * source + layer
            sigma = start[6, z]
            cond[z] = merge(sigma)
            for part in range(2):
                here = [start[3 * part + c, z] for c in range(3)]
                above = [start[3 * part + c, z + 1] for c in (1, 2)]
                h = curl_ahead(here, above, keep)
                outs = curl_behind(h, below[part])
                below[part] = [h[1], h[2]]
                for component, value in enumerate(outs):
                    other = sigma * start[3 * (1 - part) + component, z]
                    value = other - value if part == 0 else -value - other
                    field[0, 3 * part + component, z] = merge(value) * inside[...]
        for number in range(4):
            curl_start[number] = below[number // 2][number % 2]
        return carry

    lax.fori_loop(0, depths, start_layers, 0, unroll=2)

    line = lax.broadcasted_iota(jnp.int32, (1, LANES), 1)

    def place_of(cell):
        col = (cell & (width - 1)) - y_first
        rest = lax.shift_right_logical(cell, width.bit_length() - 1)
        row = (rest & (x_size - 1)) - x_first
        z = lax.shift_right_logical(rest, x_size.bit_length() - 1)
        return (row >= -4) & (row < OWN_ROWS + 4) & (col >= -8) & (col < HALF + 8), z, row, col

    def add_source(cell, real, imag):
        held, z, row, col = place_of(cell)

        @pl.when(held)
        def _():
            hit = line == (col & (LANES - 1))
            at = pl.ds(jnp.where(row < 0, row + BASIS_ROWS, row), 1)
            field[0, 0, z, at] = field[0, 0, z, at] + jnp.where(hit, real, 0.0)
            field[0, 3, z, at] = field[0, 3, z, at] + jnp.where(hit, imag, 0.0)

    @pl.when(kind == 0)
    def _():
        add_source(tx_ref[0], jnp.float32(0.0), jnp.float32(-SOURCE))

    @pl.when(kind == 1)
    def _():
        def each(group, carry):
            numbers = [8 * group + n for n in range(8)]
            some = place_of(rx_ref[0, numbers[0]])[0]
            for r in numbers[1:]:
                some = some | place_of(rx_ref[0, r])[0]

            @pl.when(some)
            def _():
                for r in numbers:
                    add_source(rx_ref[0, r], weight_ref[0, 2 * r], weight_ref[0, 2 * r + 1])

            return carry

        lax.fori_loop(0, rx_ref.shape[1] // 8, each, 0)

    for step in range(BASIS - 1):
        for number in range(4):
            curl[number] = empty

        def apply_layers(source, carry, step=step):
            keep = inside[...]
            below = [[curl[0], curl[1]], [curl[2], curl[3]]]
            mine = slice(0, OWN_ROWS) if step == BASIS - 2 else slice(0, BASIS_ROWS)
            for layer in range(2):
                z = 2 * source + layer
                sigma = cond[z, mine]
                for part in range(2):
                    here = [field[step, 3 * part + c, z] for c in range(3)]
                    above = [field[step, 3 * part + c, z + 1] for c in (1, 2)]
                    h = curl_ahead(here, above, keep)
                    outs = curl_behind(h, below[part])
                    below[part] = [h[1], h[2]]
                    for component, value in enumerate(outs):
                        value = value[mine]
                        other = sigma * field[step, 3 * (1 - part) + component, z, mine]
                        value = value - other if part == 0 else value + other
                        if step < BASIS - 2:
                            value = value * keep
                        field[step + 1, 3 * part + component, z, mine] = value
            for number in range(4):
                curl[number] = below[number // 2][number % 2]
            return carry

        lax.fori_loop(0, depths, apply_layers, 0, unroll=2)

    for entry in range(2 * len(ENTRIES)):
        acc[entry] = blank

    def gram_layers(source, carry):
        tiles = []
        for b in range(BASIS):
            group = []
            for component in range(6):
                for core in range(2):
                    at = slice(core * ROWS, (core + 1) * ROWS)
                    first = field[b, component, 2 * source, at]
                    second = field[b, component, 2 * source + 1, at]
                    group.append(jnp.where(low, first, pltpu.roll(second, HALF, 1)))
                    if b < BASIS - 1:
                        basis_ref[b, core * depths + source, component] = group[-1]
            tiles.append(group)
        for entry, (i, j, part) in enumerate(ENTRIES):
            first, second = tiles[i], tiles[j]
            if part:
                terms = [first[n] * second[n + 6] - first[n + 6] * second[n] for n in range(6)]
            else:
                terms = [first[n] * second[n] + first[n + 6] * second[n + 6] for n in range(6)]
            value = (terms[0] + terms[1]) + (terms[2] + terms[3]) + (terms[4] + terms[5])
            total, error = two_sum(acc[2 * entry], value)
            acc[2 * entry] = total
            acc[2 * entry + 1] = acc[2 * entry + 1] + error
        return carry

    lax.fori_loop(0, depths, gram_layers, 0)

    def fold(high, low, shift, axis):
        total, error = two_sum(high, pltpu.roll(high, shift, axis))
        return total, low + pltpu.roll(low, shift, axis) + error

    sub = lax.broadcasted_iota(jnp.int32, (ROWS, LANES), 0)
    row = blank
    for first in range(0, len(ENTRIES), 8):
        highs, lows = blank, blank
        for entry in range(first, min(first + 8, len(ENTRIES))):
            value, rest = acc[2 * entry], acc[2 * entry + 1]
            for shift in (4, 2, 1):
                value, rest = fold(value, rest, shift, 0)
            highs = jnp.where(sub == entry - first, value, highs)
            lows = jnp.where(sub == entry - first, rest, lows)
        for shift in (64, 32, 16, 8, 4, 2, 1):
            highs, lows = fold(highs, lows, shift, 1)
        row = jnp.where(lane == sub + first, highs, row)
        row = jnp.where(lane == sub + first + 64, lows, row)
    for shift in (4, 2, 1):
        row = row + pltpu.roll(row, shift, 0)
    for number in range(pieces * chips * 2 // ROWS):
        gram_ref[number * ROWS : (number + 1) * ROWS] = row


def quick(a, b):
    total = a + b
    return total, b - (total - a)


def split(a):
    big = a * 4097.0
    high = big - (big - a)
    return high, a - high


def two_product(a, b):
    value = a * b
    ah, al = split(a)
    bh, bl = split(b)
    return value, ((ah * bh - value) + ah * bl + al * bh) + al * bl


def add(a, b):
    total, error = two_sum(a[0], b[0])
    return quick(total, error + (a[1] + b[1]))


def neg(a):
    return (-a[0], -a[1])


def mul(a, b):
    value, error = two_product(a[0], b[0])
    return quick(value, error + (a[0] * b[1] + a[1] * b[0]))


def div(a, b):
    first = a[0] / b[0]
    zero = jnp.zeros_like(first)
    rest = add(a, neg(mul(b, (first, zero))))
    second = rest[0] / b[0]
    rest = add(rest, neg(mul(b, (second, zero))))
    third = rest[0] / b[0]
    return add(quick(first, second), (third, zero))


def c_add(a, b):
    return (add(a[0], b[0]), add(a[1], b[1]))


def c_neg(a):
    return (neg(a[0]), neg(a[1]))


def c_conj(a):
    return (a[0], neg(a[1]))


def c_mul(a, b):
    return (
        add(mul(a[0], b[0]), neg(mul(a[1], b[1]))),
        add(mul(a[0], b[1]), mul(a[1], b[0])),
    )


def c_div(a, b):
    top = c_mul(a, c_conj(b))
    bottom = add(mul(b[0], b[0]), mul(b[1], b[1]))
    return (div(top[0], bottom), div(top[1], bottom))


def c_over(a, real):
    return (div(a[0], real), div(a[1], real))


def total_of(values):
    result = values[0]
    for value in values[1:]:
        result = c_add(result, value)
    return result


def coefficients(gram):
    rho = gram[0, 0]
    alpha = c_div(rho, gram[0, 1])
    one_half = c_neg(alpha)

    def form(coeffs, left, right):
        rows = []
        for i, factor in enumerate(coeffs):
            inner = total_of(
                [
                    gram[i + left, j + right]
                    if other is None
                    else c_mul(gram[i + left, j + right], other)
                    for j, other in enumerate(coeffs)
                ]
            )
            rows.append(inner if factor is None else c_mul(c_conj(factor), inner))
        return total_of(rows)

    omega = c_over(form([None, one_half], 1, 0), form([None, one_half], 1, 1)[0])
    res1 = c_neg(c_add(alpha, omega))
    res2 = c_mul(alpha, omega)
    new_rho = total_of([gram[0, 0], c_mul(gram[0, 1], res1), c_mul(gram[0, 2], res2)])
    mix = c_mul(c_div(new_rho, rho), c_div(alpha, omega))
    dir0 = (add((jnp.ones_like(mix[0][0]), jnp.zeros_like(mix[0][0])), mix[0]), mix[1])
    dir1 = c_add(res1, c_neg(c_mul(mix, omega)))
    dir2 = res2
    along = total_of(
        [c_mul(gram[0, 1], dir0), c_mul(gram[0, 2], dir1), c_mul(gram[0, 3], dir2)]
    )
    alpha2 = c_div(new_rho, along)
    half1 = c_add(res1, c_neg(c_mul(alpha2, dir0)))
    half2 = c_add(res2, c_neg(c_mul(alpha2, dir1)))
    half3 = c_neg(c_mul(alpha2, dir2))
    half = [None, half1, half2, half3]
    omega2 = c_over(form(half, 1, 0), form(half, 1, 1)[0])
    out0 = total_of([alpha, omega, c_mul(alpha2, dir0), omega2])
    out1 = total_of([c_mul(omega, one_half), c_mul(alpha2, dir1), c_mul(omega2, half1)])
    out2 = c_add(c_mul(alpha2, dir2), c_mul(omega2, half2))
    out3 = c_mul(omega2, half3)
    return [(c[0][0], c[1][0]) for c in (out0, out1, out2, out3)]


def update_kernel(sizes, rows_ref, start_ref, basis_ref, out_ref):
    depths, chips, pieces = sizes
    high = jnp.zeros((ROWS, LANES), jnp.float32)
    low = high
    for number in range(pieces * chips * 2 // ROWS):
        high, error = two_sum(high, rows_ref[number * ROWS : (number + 1) * ROWS])
        low = low + error
    for shift in (4, 2, 1):
        high, error = two_sum(high, pltpu.roll(high, shift, 0))
        low = low + pltpu.roll(low, shift, 0) + error
    high, low = quick(high, low + pltpu.roll(high, 64, 1))

    def entry(number):
        return (
            jnp.broadcast_to(high[:, number : number + 1], (ROWS, LANES)),
            jnp.broadcast_to(low[:, number : number + 1], (ROWS, LANES)),
        )

    zero = jnp.zeros((ROWS, LANES), jnp.float32)
    gram = {}
    at = 0
    for i, j in PAIRS:
        real = entry(at)
        at += 1
        if i == j:
            gram[i, i] = (real, (zero, zero))
        else:
            gram[i, j] = (real, entry(at))
            gram[j, i] = c_conj(gram[i, j])
            at += 1
    factors = coefficients(gram)

    def layer(source, carry):
        for component in range(3):
            real = start_ref[source, component]
            imag = start_ref[source, component + 3]
            for b, (fr, fi) in enumerate(factors):
                br = basis_ref[b, source, component]
                bi = basis_ref[b, source, component + 3]
                real = real + (fr * br - fi * bi)
                imag = imag + (fr * bi + fi * br)
            out_ref[source, component] = real
            out_ref[source, component + 3] = imag
        return carry

    lax.fori_loop(0, 2 * depths, layer, 0, unroll=2)


def output_kernel(pieces, in_ref, field_ref, term_ref):
    low = lax.broadcasted_iota(jnp.int32, (ROWS, LANES), 1) < HALF
    for piece in range(pieces):
        cols = slice(piece * LANES, (piece + 1) * LANES)
        terms = [None, None]
        for component in range(3):
            values = [[], []]
            for kind in range(KINDS):
                for part in range(2):
                    number = 3 * part + component
                    first = in_ref[kind * pieces + piece, number]
                    second = in_ref[(KINDS + kind) * pieces + piece, number]
                    pair = (
                        jnp.where(low, first, pltpu.roll(second, HALF, 1)),
                        jnp.where(low, pltpu.roll(first, HALF, 1), second),
                    )
                    for z in range(2):
                        field_ref[kind * 12 + 2 * number + z, :, cols] = pair[z]
                        values[z].append(pair[z])
            for z in range(2):
                v = values[z]
                product = v[0] * v[2] - v[1] * v[3]
                terms[z] = product if terms[z] is None else terms[z] + product
        for z in range(2):
            term_ref[piece, z] = terms[z]


def local(conductivity, field_guess, tx_cell, rx_cell, rx_weight):
    pieces, chips = lax.axis_size("piece"), lax.axis_size("chip")
    depths = KINDS * pieces
    sizes = (depths, chips, pieces)
    width = conductivity.shape[2]
    f32 = jnp.float32
    params = pltpu.CompilerParams

    packed = pl.pallas_call(
        functools.partial(pack_kernel, pieces),
        out_shape=jax.ShapeDtypeStruct((2 * depths, 9, ROWS, LANES), f32),
        in_specs=[in_vmem()] * 2,
        out_specs=in_vmem(),
        compiler_params=params(vmem_limit_bytes=4 * MIB),
    )(field_guess.reshape(24, ROWS, width), conductivity)
    mid = lax.all_to_all(packed, SPREAD, 0, 0)
    left = lax.ppermute(mid[depths:], "chip", [(i, i + 1) for i in range(chips - 1)])
    right = lax.ppermute(mid[:depths], "chip", [(i + 1, i) for i in range(chips - 1)])

    basis, rows = pl.pallas_call(
        functools.partial(basis_kernel, sizes),
        out_shape=(
            jax.ShapeDtypeStruct((BASIS - 1, 2 * depths, 6, ROWS, LANES), f32),
            jax.ShapeDtypeStruct((pieces * chips * 2, LANES), f32),
        ),
        in_specs=[in_smem()] * 3 + [in_vmem()] * 3,
        out_specs=(in_vmem(), in_vmem()),
        scratch_shapes=basis_scratch(depths),
        compiler_params=params(vmem_limit_bytes=28 * MIB),
    )(tx_cell, rx_cell, rx_weight.reshape(1, -1), left, mid, right)

    rows = lax.all_to_all(rows, ("piece",) + LAT, 0, 0)
    moved = pl.pallas_call(
        functools.partial(update_kernel, sizes),
        out_shape=jax.ShapeDtypeStruct((2 * depths, 6, ROWS, LANES), f32),
        in_specs=[in_vmem()] * 3,
        out_specs=in_vmem(),
        compiler_params=params(vmem_limit_bytes=8 * MIB),
    )(rows, mid, basis)
    moved = lax.all_to_all(moved, SPREAD, 0, 0)
    fields, terms = pl.pallas_call(
        functools.partial(output_kernel, pieces),
        out_shape=(
            jax.ShapeDtypeStruct((24, ROWS, width), f32),
            jax.ShapeDtypeStruct((pieces, 2, ROWS, LANES), f32),
        ),
        in_specs=[in_vmem()],
        out_specs=(in_vmem(), in_vmem()),
        compiler_params=params(vmem_limit_bytes=4 * MIB),
    )(moved)
    gradient = jnp.sum(lax.all_to_all(terms, "tx", 0, 0), axis=0)
    return (fields.reshape(field_guess.shape), gradient)


def solution(mesh):
    grid = mesh.devices
    shape = (KINDS, grid.shape[0] // KINDS, grid.shape[1] // 2, 2, grid.shape[2])
    split = Mesh(grid.reshape(shape), DEPTH + LAT + ("tx",))
    return jax.shard_map(
        local,
        mesh=split,
        in_specs=(
            P(DEPTH, LAT, None),
            P("tx", None, None, None, DEPTH, LAT, None),
            P("tx"),
            P("tx", None),
            P("tx", None, None),
        ),
        out_specs=(P("tx", None, None, None, DEPTH, LAT, None), P(DEPTH, LAT, "tx")),
        check_vma=False,
    )
```

```python
import functools

import jax
import jax.numpy as jnp
from jax import lax
from jax.experimental import pallas as pl
from jax.experimental.pallas import tpu as pltpu
from jax.sharding import Mesh
from jax.sharding import PartitionSpec as P

SOURCE = 20.0
KINDS = 2
BASIS = 5
ROWS = 8
LANES = 128
DEPTH = ("kind", "piece")
PAIRS = [(i, j) for i in range(BASIS) for j in range(i, BASIS)]
ENTRIES = [(i, j, part) for i, j in PAIRS for part in range(1 if i == j else 2)]
MIB = 1 << 20


def in_vmem():
    return pl.BlockSpec(memory_space=pltpu.VMEM)


def in_smem():
    return pl.BlockSpec(memory_space=pltpu.SMEM)


def slot(part, component, layer):
    return (part * 3 + component) * 2 + layer


def pack_kernel(pieces, guess_ref, cond_ref, out_ref):
    lane = lax.broadcasted_iota(jnp.int32, (ROWS, LANES), 1)
    blank = jnp.zeros((ROWS, LANES), jnp.float32)
    for kind in range(KINDS):
        for piece in range(pieces):
            to = kind * pieces + piece
            edges = [blank, blank]
            for item in range(14):

                def tile(number):
                    if number < 0 or number >= pieces:
                        return blank
                    cols = slice(number * LANES, (number + 1) * LANES)
                    if item < 12:
                        return guess_ref[kind * 12 + item, :, cols]
                    return cond_ref[item - 12, :, cols]

                out_ref[to, item] = tile(piece)
                ends = jnp.where(lane >= LANES // 2, tile(piece - 1), tile(piece + 1))
                place = item % 8
                moved = pltpu.roll(ends, (16 * place + 8) % LANES, 1)
                edges[item // 8] = jnp.where(lane // 16 == place, moved, edges[item // 8])
            out_ref[to, 14] = edges[0]
            out_ref[to, 15] = edges[1]


def two_sum(a, b):
    total = a + b
    other = total - a
    return total, (a - (total - other)) + (b - other)


def basis_scratch(depths):
    layers = 2 * depths
    f32 = jnp.float32
    return [
        pltpu.VMEM((BASIS, 6, layers + 1, 2 * ROWS, 2 * LANES), f32),
        pltpu.VMEM((7, layers, 3 * ROWS, LANES), f32),
        pltpu.VMEM((4, 3 * ROWS, 2 * LANES), f32),
        pltpu.VMEM((4, 2 * ROWS, 2 * LANES), f32),
        pltpu.VMEM((layers, 2 * ROWS, 2 * LANES), f32),
        pltpu.VMEM((3 * ROWS, 2 * LANES), f32),
        pltpu.VMEM((2 * ROWS, 2 * LANES), f32),
        pltpu.VMEM((2 * len(ENTRIES), ROWS, LANES), f32),
    ]


def basis_kernel(
    sizes, tx_ref, rx_ref, weight_ref, outer_ref, mid_ref, inner_ref, basis_ref, gram_ref,
    field, edges, curl_start, curl, cond, inside_start, inside, acc,
):
    depths, lats, pieces = sizes
    layers = 2 * depths
    span = 2 * LANES
    width = pieces * LANES
    lat_index = lax.axis_index("lat")
    kind = lax.axis_index("kind")
    piece = lax.axis_index("piece")
    lane = lax.broadcasted_iota(jnp.int32, (ROWS, LANES), 1)
    blank = jnp.zeros((ROWS, LANES), jnp.float32)

    def within(rows, row):
        lane_w = lax.broadcasted_iota(jnp.int32, (rows, span), 1)
        x_at = lat_index * ROWS + row
        y_at = piece * LANES + jnp.where(lane_w >= LANES + 64, lane_w - span, lane_w)
        good = (x_at >= 0) & (x_at < lats * ROWS) & (y_at >= 0) & (y_at < width)
        return jnp.where(good, 1.0, 0.0)

    row_s = lax.broadcasted_iota(jnp.int32, (3 * ROWS, span), 0)
    inside_start[...] = within(3 * ROWS, row_s - ROWS)
    row_b = lax.broadcasted_iota(jnp.int32, (2 * ROWS, span), 0)
    inside[...] = within(2 * ROWS, jnp.where(row_b >= 12, row_b - 16, row_b))

    first_core = lat_index % 2 == 0

    def received(source, item):
        outer, inner = outer_ref[source, item], inner_ref[source, item]
        left = jnp.where(first_core, outer, inner)
        right = jnp.where(first_core, inner, outer)
        return left, mid_ref[source, item], right


    def spread(source, carry):
        for number, packs in enumerate(zip(received(source, 14), received(source, 15))):
            for item in range(14):
                edge = pltpu.roll(packs[item // 8], LANES - (16 * (item % 8) + 8), 1)
                edge = jnp.where((lane < 8) | (lane >= LANES - 8), edge, blank)
                at = slice(number * ROWS, (number + 1) * ROWS)
                edges[item // 2, 2 * source + item % 2, at] = edge
        return carry

    lax.fori_loop(0, depths, spread, 0, unroll=2)

    empty = jnp.zeros((2 * ROWS, span), jnp.float32)
    for number in range(BASIS - 1):
        for component in range(6):
            field[number, component, layers] = empty

    def ahead(values, axis):
        return pltpu.roll(values, values.shape[axis] - 1, axis) - values

    def behind(values, axis):
        return values - pltpu.roll(values, 1, axis)

    def curl_ahead(here, above, keep):
        uz, ux, uy = here
        hz = (ahead(uy, 0) - ahead(ux, 1)) * keep
        hx = (ahead(uz, 1) - (above[1] - uy)) * keep
        hy = ((above[0] - ux) - ahead(uz, 0)) * keep
        return hz, hx, hy

    def curl_behind(h, below):
        hz, hx, hy = h
        return (
            behind(hy, 0) - behind(hx, 1),
            behind(hz, 1) - (hy - below[1]),
            (hx - below[0]) - behind(hz, 0),
        )

    def start_tile(number, z, source, layer):
        body = jnp.concatenate(received(source, 2 * number + layer), axis=0)
        return jnp.concatenate([body, edges[number, z]], axis=1)

    def merge(values):
        sub = lax.broadcasted_iota(jnp.int32, (ROWS, span), 0)
        sides = jnp.where(sub < 4, values[2 * ROWS :], values[:ROWS])
        return jnp.concatenate([values[ROWS : 2 * ROWS], sides], axis=0)

    for number in range(4):
        curl_start[number] = jnp.zeros((3 * ROWS, span), jnp.float32)

    def start_layers(source, carry):
        keep = inside_start[...]
        below = [[curl_start[0], curl_start[1]], [curl_start[2], curl_start[3]]]
        for layer in range(2):
            z = 2 * source + layer
            tiles = [start_tile(c, z, source, layer) for c in range(6)]
            sigma = start_tile(6, z, source, layer)
            cond[z] = merge(sigma)
            for part in range(2):
                here = tiles[3 * part : 3 * part + 3]
                if layer == 0:
                    above = [start_tile(3 * part + c, z + 1, source, 1) for c in (1, 2)]
                else:
                    last = source == depths - 1
                    after = jnp.minimum(source + 1, depths - 1)
                    above = [
                        jnp.where(last, 0.0, start_tile(3 * part + c, 2 * after, after, 0))
                        for c in (1, 2)
                    ]
                h = curl_ahead(here, above, keep)
                outs = curl_behind(h, below[part])
                below[part] = [h[1], h[2]]
                for component, value in enumerate(outs):
                    other = sigma * tiles[3 * (1 - part) + component]
                    value = other - value if part == 0 else -value - other
                    field[0, 3 * part + component, z] = merge(value) * inside[...]
        for number in range(4):
            curl_start[number] = below[number // 2][number % 2]
        return carry

    lax.fori_loop(0, depths, start_layers, 0)

    line = lax.broadcasted_iota(jnp.int32, (1, span), 1)

    def place_of(cell):
        col = (cell & (width - 1)) - piece * LANES
        rest = lax.shift_right_logical(cell, width.bit_length() - 1)
        row = (rest & (lats * ROWS - 1)) - lat_index * ROWS
        z = lax.shift_right_logical(rest, (lats * ROWS).bit_length() - 1)
        return (row >= -4) & (row < 12) & (col >= -8) & (col < LANES + 8), z, row, col

    def add_source(cell, real, imag):
        held, z, row, col = place_of(cell)

        @pl.when(held)
        def _():
            hit = line == (col & (span - 1))
            at = pl.ds(row & (2 * ROWS - 1), 1)
            field[0, 0, z, at] = field[0, 0, z, at] + jnp.where(hit, real, 0.0)
            field[0, 3, z, at] = field[0, 3, z, at] + jnp.where(hit, imag, 0.0)

    @pl.when(kind == 0)
    def _():
        add_source(tx_ref[0], jnp.float32(0.0), jnp.float32(-SOURCE))

    @pl.when(kind == 1)
    def _():
        def each(group, carry):
            numbers = [8 * group + n for n in range(8)]
            some = place_of(rx_ref[0, numbers[0]])[0]
            for r in numbers[1:]:
                some = some | place_of(rx_ref[0, r])[0]

            @pl.when(some)
            def _():
                for r in numbers:
                    add_source(rx_ref[0, r], weight_ref[0, 2 * r], weight_ref[0, 2 * r + 1])

            return carry

        lax.fori_loop(0, rx_ref.shape[1] // 8, each, 0)

    for step in range(BASIS - 1):
        for number in range(4):
            curl[number] = empty

        def apply_layers(source, carry, step=step):
            keep = inside[...]
            below = [[curl[0], curl[1]], [curl[2], curl[3]]]
            for layer in range(2):
                z = 2 * source + layer
                sigma = cond[z]
                for part in range(2):
                    here = [field[step, 3 * part + c, z] for c in range(3)]
                    above = [field[step, 3 * part + c, z + 1] for c in (1, 2)]
                    h = curl_ahead(here, above, keep)
                    outs = curl_behind(h, below[part])
                    below[part] = [h[1], h[2]]
                    for component, value in enumerate(outs):
                        if step == BASIS - 2:
                            mine = (slice(0, ROWS), slice(0, LANES))
                        else:
                            mine = (slice(None), slice(None))
                        near = field[(step, 3 * (1 - part) + component, z) + mine]
                        other = sigma[mine] * near
                        value = value[mine]
                        value = value - other if part == 0 else value + other
                        if step < BASIS - 2:
                            value = value * keep
                        field[(step + 1, 3 * part + component, z) + mine] = value
            for number in range(4):
                curl[number] = below[number // 2][number % 2]
            return carry

        lax.fori_loop(0, depths, apply_layers, 0, unroll=2)

    for entry in range(2 * len(ENTRIES)):
        acc[entry] = blank

    def gram_layers(source, carry):
        tiles = []
        for b in range(BASIS):
            group = []
            for component in range(6):
                for layer in range(2):
                    tile = field[b, component, 2 * source + layer, 0:ROWS, 0:LANES]
                    group.append(tile)
                    if b < BASIS - 1:
                        basis_ref[b, source, 2 * component + layer] = tile
            tiles.append(group)
        for entry, (i, j, part) in enumerate(ENTRIES):
            first, second = tiles[i], tiles[j]
            if part:
                terms = [first[n] * second[n + 6] - first[n + 6] * second[n] for n in range(6)]
            else:
                terms = [first[n] * second[n] + first[n + 6] * second[n + 6] for n in range(6)]
            value = (terms[0] + terms[1]) + (terms[2] + terms[3]) + (terms[4] + terms[5])
            total, error = two_sum(acc[2 * entry], value)
            acc[2 * entry] = total
            acc[2 * entry + 1] = acc[2 * entry + 1] + error
        return carry

    lax.fori_loop(0, depths, gram_layers, 0)

    def fold(high, low, shift, axis):
        total, error = two_sum(high, pltpu.roll(high, shift, axis))
        return total, low + pltpu.roll(low, shift, axis) + error

    sub = lax.broadcasted_iota(jnp.int32, (ROWS, LANES), 0)
    row = blank
    for start in range(0, len(ENTRIES), 8):
        highs, lows = blank, blank
        for entry in range(start, min(start + 8, len(ENTRIES))):
            high, low = acc[2 * entry], acc[2 * entry + 1]
            for shift in (4, 2, 1):
                high, low = fold(high, low, shift, 0)
            highs = jnp.where(sub == entry - start, high, highs)
            lows = jnp.where(sub == entry - start, low, lows)
        for shift in (64, 32, 16, 8, 4, 2, 1):
            highs, lows = fold(highs, lows, shift, 1)
        row = jnp.where(lane == sub + start, highs, row)
        row = jnp.where(lane == sub + start + 64, lows, row)
    for shift in (4, 2, 1):
        row = row + pltpu.roll(row, shift, 0)
    for number in range(pieces * lats // ROWS):
        gram_ref[number * ROWS : (number + 1) * ROWS] = row


def quick(a, b):
    total = a + b
    return total, b - (total - a)


def split(a):
    big = a * 4097.0
    high = big - (big - a)
    return high, a - high


def two_product(a, b):
    value = a * b
    ah, al = split(a)
    bh, bl = split(b)
    return value, ((ah * bh - value) + ah * bl + al * bh) + al * bl


def add(a, b):
    total, error = two_sum(a[0], b[0])
    return quick(total, error + (a[1] + b[1]))


def neg(a):
    return (-a[0], -a[1])


def mul(a, b):
    value, error = two_product(a[0], b[0])
    return quick(value, error + (a[0] * b[1] + a[1] * b[0]))


def div(a, b):
    first = a[0] / b[0]
    zero = jnp.zeros_like(first)
    rest = add(a, neg(mul(b, (first, zero))))
    second = rest[0] / b[0]
    rest = add(rest, neg(mul(b, (second, zero))))
    third = rest[0] / b[0]
    return add(quick(first, second), (third, zero))


def c_add(a, b):
    return (add(a[0], b[0]), add(a[1], b[1]))


def c_neg(a):
    return (neg(a[0]), neg(a[1]))


def c_conj(a):
    return (a[0], neg(a[1]))


def c_mul(a, b):
    return (
        add(mul(a[0], b[0]), neg(mul(a[1], b[1]))),
        add(mul(a[0], b[1]), mul(a[1], b[0])),
    )


def c_div(a, b):
    top = c_mul(a, c_conj(b))
    bottom = add(mul(b[0], b[0]), mul(b[1], b[1]))
    return (div(top[0], bottom), div(top[1], bottom))


def c_over(a, real):
    return (div(a[0], real), div(a[1], real))


def total_of(values):
    result = values[0]
    for value in values[1:]:
        result = c_add(result, value)
    return result


def coefficients(gram):
    rho = gram[0, 0]
    alpha = c_div(rho, gram[0, 1])
    one_half = c_neg(alpha)

    def form(coeffs, left, right):
        rows = []
        for i, factor in enumerate(coeffs):
            inner = total_of(
                [
                    gram[i + left, j + right]
                    if other is None
                    else c_mul(gram[i + left, j + right], other)
                    for j, other in enumerate(coeffs)
                ]
            )
            rows.append(inner if factor is None else c_mul(c_conj(factor), inner))
        return total_of(rows)

    omega = c_over(form([None, one_half], 1, 0), form([None, one_half], 1, 1)[0])
    res1 = c_neg(c_add(alpha, omega))
    res2 = c_mul(alpha, omega)
    new_rho = total_of([gram[0, 0], c_mul(gram[0, 1], res1), c_mul(gram[0, 2], res2)])
    mix = c_mul(c_div(new_rho, rho), c_div(alpha, omega))
    dir0 = (add((jnp.ones_like(mix[0][0]), jnp.zeros_like(mix[0][0])), mix[0]), mix[1])
    dir1 = c_add(res1, c_neg(c_mul(mix, omega)))
    dir2 = res2
    along = total_of(
        [c_mul(gram[0, 1], dir0), c_mul(gram[0, 2], dir1), c_mul(gram[0, 3], dir2)]
    )
    alpha2 = c_div(new_rho, along)
    half1 = c_add(res1, c_neg(c_mul(alpha2, dir0)))
    half2 = c_add(res2, c_neg(c_mul(alpha2, dir1)))
    half3 = c_neg(c_mul(alpha2, dir2))
    half = [None, half1, half2, half3]
    omega2 = c_over(form(half, 1, 0), form(half, 1, 1)[0])
    out0 = total_of([alpha, omega, c_mul(alpha2, dir0), omega2])
    out1 = total_of([c_mul(omega, one_half), c_mul(alpha2, dir1), c_mul(omega2, half1)])
    out2 = c_add(c_mul(alpha2, dir2), c_mul(omega2, half2))
    out3 = c_mul(omega2, half3)
    return [(c[0][0], c[1][0]) for c in (out0, out1, out2, out3)]


def update_kernel(sizes, rows_ref, start_ref, basis_ref, out_ref):
    depths, lats, pieces = sizes
    high = jnp.zeros((ROWS, LANES), jnp.float32)
    low = high
    for number in range(pieces * lats // ROWS):
        high, error = two_sum(high, rows_ref[number * ROWS : (number + 1) * ROWS])
        low = low + error
    for shift in (4, 2, 1):
        high, error = two_sum(high, pltpu.roll(high, shift, 0))
        low = low + pltpu.roll(low, shift, 0) + error
    high, low = quick(high, low + pltpu.roll(high, 64, 1))

    def entry(number):
        return (
            jnp.broadcast_to(high[:, number : number + 1], (ROWS, LANES)),
            jnp.broadcast_to(low[:, number : number + 1], (ROWS, LANES)),
        )

    zero = jnp.zeros((ROWS, LANES), jnp.float32)
    gram = {}
    at = 0
    for i, j in PAIRS:
        real = entry(at)
        at += 1
        if i == j:
            gram[i, i] = (real, (zero, zero))
        else:
            gram[i, j] = (real, entry(at))
            gram[j, i] = c_conj(gram[i, j])
            at += 1
    factors = coefficients(gram)

    def layer(source, carry):
        for component in range(3):
            for z in range(2):
                real = start_ref[source, slot(0, component, z)]
                imag = start_ref[source, slot(1, component, z)]
                for b, (fr, fi) in enumerate(factors):
                    br = basis_ref[b, source, slot(0, component, z)]
                    bi = basis_ref[b, source, slot(1, component, z)]
                    real = real + (fr * br - fi * bi)
                    imag = imag + (fr * bi + fi * br)
                out_ref[source, slot(0, component, z)] = real
                out_ref[source, slot(1, component, z)] = imag
        return carry

    lax.fori_loop(0, depths, layer, 0)


def output_kernel(pieces, in_ref, field_ref, term_ref):
    for piece in range(pieces):
        cols = slice(piece * LANES, (piece + 1) * LANES)
        for z in range(2):
            term = None
            for component in range(3):
                values = []
                for kind in range(KINDS):
                    for part in range(2):
                        value = in_ref[kind * pieces + piece, slot(part, component, z)]
                        field_ref[kind * 12 + slot(part, component, z), :, cols] = value
                        values.append(value)
                product = values[0] * values[2] - values[1] * values[3]
                term = product if term is None else term + product
            term_ref[piece, z] = term


def local(conductivity, field_guess, tx_cell, rx_cell, rx_weight):
    pieces, lats = lax.axis_size("piece"), lax.axis_size("lat")
    depths = KINDS * pieces
    sizes = (depths, lats, pieces)
    width = conductivity.shape[2]
    layers = 2 * depths
    f32 = jnp.float32
    params = pltpu.CompilerParams

    packed = pl.pallas_call(
        functools.partial(pack_kernel, pieces),
        out_shape=jax.ShapeDtypeStruct((depths, 16, ROWS, LANES), f32),
        in_specs=[in_vmem()] * 2,
        out_specs=in_vmem(),
        compiler_params=params(vmem_limit_bytes=4 * MIB),
    )(field_guess.reshape(24, ROWS, width), conductivity)
    mid = lax.all_to_all(packed, DEPTH, 0, 0)
    border = [(i, i + 1) for i in range(1, lats - 1, 2)]
    outer = lax.ppermute(mid, "lat", border + [(b, a) for a, b in border])
    inner = lax.ppermute(mid, "lat", [(i, i ^ 1) for i in range(lats)])

    basis, rows = pl.pallas_call(
        functools.partial(basis_kernel, sizes),
        out_shape=(
            jax.ShapeDtypeStruct((BASIS - 1, depths, 12, ROWS, LANES), f32),
            jax.ShapeDtypeStruct((pieces * lats, LANES), f32),
        ),
        in_specs=[in_smem()] * 3 + [in_vmem()] * 3,
        out_specs=(in_vmem(), in_vmem()),
        scratch_shapes=basis_scratch(depths),
        compiler_params=params(vmem_limit_bytes=28 * MIB),
    )(tx_cell, rx_cell, rx_weight.reshape(1, -1), outer, mid, inner)

    rows = lax.all_to_all(rows, ("piece", "lat"), 0, 0)
    moved = pl.pallas_call(
        functools.partial(update_kernel, sizes),
        out_shape=jax.ShapeDtypeStruct((depths, 12, ROWS, LANES), f32),
        in_specs=[in_vmem()] * 3,
        out_specs=in_vmem(),
        compiler_params=params(vmem_limit_bytes=8 * MIB),
    )(rows, mid, basis)
    moved = lax.all_to_all(moved, DEPTH, 0, 0)
    fields, terms = pl.pallas_call(
        functools.partial(output_kernel, pieces),
        out_shape=(
            jax.ShapeDtypeStruct((24, ROWS, width), f32),
            jax.ShapeDtypeStruct((pieces, 2, ROWS, LANES), f32),
        ),
        in_specs=[in_vmem()],
        out_specs=(in_vmem(), in_vmem()),
        compiler_params=params(vmem_limit_bytes=4 * MIB),
    )(moved)
    gradient = jnp.sum(lax.all_to_all(terms, "tx", 0, 0), axis=0)
    return (fields.reshape(field_guess.shape), gradient)


def solution(mesh):
    grid = mesh.devices
    split = Mesh(
        grid.reshape((KINDS, grid.shape[0] // KINDS) + grid.shape[1:]),
        DEPTH + tuple(mesh.axis_names[1:]),
    )
    return jax.shard_map(
        local,
        mesh=split,
        in_specs=(
            P(DEPTH, "lat", None),
            P("tx", None, None, None, DEPTH, "lat", None),
            P("tx"),
            P("tx", None),
            P("tx", None, None),
        ),
        out_specs=(P("tx", None, None, None, DEPTH, "lat", None), P(DEPTH, "lat", "tx")),
        check_vma=False,
    )
```

```python
import functools

import jax
import jax.numpy as jnp
from jax import lax
from jax.experimental import pallas as pl
from jax.experimental.pallas import tpu as pltpu
from jax.sharding import Mesh
from jax.sharding import PartitionSpec as P

SOURCE = 20.0
KINDS = 2
BASIS = 5
ROWS = 8
LANES = 128
DEPTH = ("kind", "piece")
PAIRS = [(i, j) for i in range(BASIS) for j in range(i, BASIS)]
ENTRIES = [(i, j, part) for i, j in PAIRS for part in range(1 if i == j else 2)]
MIB = 1 << 20


def in_vmem():
    return pl.BlockSpec(memory_space=pltpu.VMEM)


def in_smem():
    return pl.BlockSpec(memory_space=pltpu.SMEM)


def slot(part, component, layer):
    return (part * 3 + component) * 2 + layer


def pack_kernel(pieces, guess_ref, cond_ref, out_ref):
    lane = lax.broadcasted_iota(jnp.int32, (ROWS, LANES), 1)
    blank = jnp.zeros((ROWS, LANES), jnp.float32)
    for kind in range(KINDS):
        for piece in range(pieces):
            to = kind * pieces + piece
            edges = [blank, blank]
            for item in range(14):

                def tile(number):
                    if number < 0 or number >= pieces:
                        return blank
                    cols = slice(number * LANES, (number + 1) * LANES)
                    if item < 12:
                        return guess_ref[kind * 12 + item, :, cols]
                    return cond_ref[item - 12, :, cols]

                out_ref[to, item] = tile(piece)
                ends = jnp.where(lane >= LANES // 2, tile(piece - 1), tile(piece + 1))
                place = item % 8
                moved = pltpu.roll(ends, (16 * place + 8) % LANES, 1)
                edges[item // 8] = jnp.where(lane // 16 == place, moved, edges[item // 8])
            out_ref[to, 14] = edges[0]
            out_ref[to, 15] = edges[1]


def two_sum(a, b):
    total = a + b
    other = total - a
    return total, (a - (total - other)) + (b - other)


def basis_scratch(depths):
    layers = 2 * depths
    f32 = jnp.float32
    return [
        pltpu.VMEM((BASIS, 6, layers + 1, 2 * ROWS, 2 * LANES), f32),
        pltpu.VMEM((7, layers, 3 * ROWS, LANES), f32),
        pltpu.VMEM((4, 3 * ROWS, 2 * LANES), f32),
        pltpu.VMEM((4, 2 * ROWS, 2 * LANES), f32),
        pltpu.VMEM((layers, 2 * ROWS, 2 * LANES), f32),
        pltpu.VMEM((3 * ROWS, 2 * LANES), f32),
        pltpu.VMEM((2 * ROWS, 2 * LANES), f32),
        pltpu.VMEM((2 * len(ENTRIES), ROWS, LANES), f32),
    ]


def basis_kernel(
    sizes, tx_ref, rx_ref, weight_ref, inner_ref, mid_ref, outer_ref, basis_ref, gram_ref,
    field, edges, curl_start, curl, cond, inside_start, inside, acc,
):
    depths, lats, pieces = sizes
    layers = 2 * depths
    span = 2 * LANES
    width = pieces * LANES
    lat_index = lax.axis_index("lat")
    kind = lax.axis_index("kind")
    piece = lax.axis_index("piece")
    lane = lax.broadcasted_iota(jnp.int32, (ROWS, LANES), 1)
    blank = jnp.zeros((ROWS, LANES), jnp.float32)

    def within(rows, row):
        lane_w = lax.broadcasted_iota(jnp.int32, (rows, span), 1)
        x_at = lat_index * ROWS + row
        y_at = piece * LANES + jnp.where(lane_w >= LANES + 64, lane_w - span, lane_w)
        good = (x_at >= 0) & (x_at < lats * ROWS) & (y_at >= 0) & (y_at < width)
        return jnp.where(good, 1.0, 0.0)

    row_s = lax.broadcasted_iota(jnp.int32, (3 * ROWS, span), 0)
    inside_start[...] = within(3 * ROWS, row_s - ROWS)
    row_b = lax.broadcasted_iota(jnp.int32, (2 * ROWS, span), 0)
    inside[...] = within(2 * ROWS, jnp.where(row_b >= 12, row_b - 16, row_b))

    first_core = lat_index % 2 == 0

    def received(source, item):
        outer, inner = outer_ref[source, item], inner_ref[source, item]
        left = jnp.where(first_core, outer, inner)
        right = jnp.where(first_core, inner, outer)
        return left, mid_ref[source, item], right


    def spread(source, carry):
        for number, packs in enumerate(zip(received(source, 14), received(source, 15))):
            for item in range(14):
                edge = pltpu.roll(packs[item // 8], LANES - (16 * (item % 8) + 8), 1)
                edge = jnp.where((lane < 8) | (lane >= LANES - 8), edge, blank)
                at = slice(number * ROWS, (number + 1) * ROWS)
                edges[item // 2, 2 * source + item % 2, at] = edge
        return carry

    lax.fori_loop(0, depths, spread, 0, unroll=2)

    empty = jnp.zeros((2 * ROWS, span), jnp.float32)
    for number in range(BASIS - 1):
        for component in range(6):
            field[number, component, layers] = empty

    def ahead(values, axis):
        return pltpu.roll(values, values.shape[axis] - 1, axis) - values

    def behind(values, axis):
        return values - pltpu.roll(values, 1, axis)

    def curl_ahead(here, above, keep):
        uz, ux, uy = here
        hz = (ahead(uy, 0) - ahead(ux, 1)) * keep
        hx = (ahead(uz, 1) - (above[1] - uy)) * keep
        hy = ((above[0] - ux) - ahead(uz, 0)) * keep
        return hz, hx, hy

    def curl_behind(h, below):
        hz, hx, hy = h
        return (
            behind(hy, 0) - behind(hx, 1),
            behind(hz, 1) - (hy - below[1]),
            (hx - below[0]) - behind(hz, 0),
        )

    def start_tile(number, z, source, layer):
        body = jnp.concatenate(received(source, 2 * number + layer), axis=0)
        return jnp.concatenate([body, edges[number, z]], axis=1)

    def merge(values):
        sub = lax.broadcasted_iota(jnp.int32, (ROWS, span), 0)
        sides = jnp.where(sub < 4, values[2 * ROWS :], values[:ROWS])
        return jnp.concatenate([values[ROWS : 2 * ROWS], sides], axis=0)

    for number in range(4):
        curl_start[number] = jnp.zeros((3 * ROWS, span), jnp.float32)

    def start_layers(source, carry):
        keep = inside_start[...]
        below = [[curl_start[0], curl_start[1]], [curl_start[2], curl_start[3]]]
        for layer in range(2):
            z = 2 * source + layer
            tiles = [start_tile(c, z, source, layer) for c in range(6)]
            sigma = start_tile(6, z, source, layer)
            cond[z] = merge(sigma)
            for part in range(2):
                here = tiles[3 * part : 3 * part + 3]
                if layer == 0:
                    above = [start_tile(3 * part + c, z + 1, source, 1) for c in (1, 2)]
                else:
                    last = source == depths - 1
                    after = jnp.minimum(source + 1, depths - 1)
                    above = [
                        jnp.where(last, 0.0, start_tile(3 * part + c, 2 * after, after, 0))
                        for c in (1, 2)
                    ]
                h = curl_ahead(here, above, keep)
                outs = curl_behind(h, below[part])
                below[part] = [h[1], h[2]]
                for component, value in enumerate(outs):
                    other = sigma * tiles[3 * (1 - part) + component]
                    value = other - value if part == 0 else -value - other
                    field[0, 3 * part + component, z] = merge(value) * inside[...]
        for number in range(4):
            curl_start[number] = below[number // 2][number % 2]
        return carry

    lax.fori_loop(0, depths, start_layers, 0)

    line = lax.broadcasted_iota(jnp.int32, (1, span), 1)

    def place_of(cell):
        col = (cell & (width - 1)) - piece * LANES
        rest = lax.shift_right_logical(cell, width.bit_length() - 1)
        row = (rest & (lats * ROWS - 1)) - lat_index * ROWS
        z = lax.shift_right_logical(rest, (lats * ROWS).bit_length() - 1)
        return (row >= -4) & (row < 12) & (col >= -8) & (col < LANES + 8), z, row, col

    def add_source(cell, real, imag):
        held, z, row, col = place_of(cell)

        @pl.when(held)
        def _():
            hit = line == (col & (span - 1))
            at = pl.ds(row & (2 * ROWS - 1), 1)
            field[0, 0, z, at] = field[0, 0, z, at] + jnp.where(hit, real, 0.0)
            field[0, 3, z, at] = field[0, 3, z, at] + jnp.where(hit, imag, 0.0)

    @pl.when(kind == 0)
    def _():
        add_source(tx_ref[0], jnp.float32(0.0), jnp.float32(-SOURCE))

    @pl.when(kind == 1)
    def _():
        def each(group, carry):
            numbers = [8 * group + n for n in range(8)]
            some = place_of(rx_ref[0, numbers[0]])[0]
            for r in numbers[1:]:
                some = some | place_of(rx_ref[0, r])[0]

            @pl.when(some)
            def _():
                for r in numbers:
                    add_source(rx_ref[0, r], weight_ref[0, 2 * r], weight_ref[0, 2 * r + 1])

            return carry

        lax.fori_loop(0, rx_ref.shape[1] // 8, each, 0)

    for step in range(BASIS - 1):
        for number in range(4):
            curl[number] = empty

        def apply_layers(source, carry, step=step):
            keep = inside[...]
            below = [[curl[0], curl[1]], [curl[2], curl[3]]]
            for layer in range(2):
                z = 2 * source + layer
                sigma = cond[z]
                for part in range(2):
                    here = [field[step, 3 * part + c, z] for c in range(3)]
                    above = [field[step, 3 * part + c, z + 1] for c in (1, 2)]
                    h = curl_ahead(here, above, keep)
                    outs = curl_behind(h, below[part])
                    below[part] = [h[1], h[2]]
                    for component, value in enumerate(outs):
                        if step == BASIS - 2:
                            mine = (slice(0, ROWS), slice(0, LANES))
                        else:
                            mine = (slice(None), slice(None))
                        near = field[(step, 3 * (1 - part) + component, z) + mine]
                        other = sigma[mine] * near
                        value = value[mine]
                        value = value - other if part == 0 else value + other
                        if step < BASIS - 2:
                            value = value * keep
                        field[(step + 1, 3 * part + component, z) + mine] = value
            for number in range(4):
                curl[number] = below[number // 2][number % 2]
            return carry

        lax.fori_loop(0, depths, apply_layers, 0, unroll=2)

    for entry in range(2 * len(ENTRIES)):
        acc[entry] = blank

    def gram_layers(source, carry):
        tiles = []
        for b in range(BASIS):
            group = []
            for component in range(6):
                for layer in range(2):
                    tile = field[b, component, 2 * source + layer, 0:ROWS, 0:LANES]
                    group.append(tile)
                    if b < BASIS - 1:
                        basis_ref[b, source, 2 * component + layer] = tile
            tiles.append(group)
        for entry, (i, j, part) in enumerate(ENTRIES):
            first, second = tiles[i], tiles[j]
            if part:
                terms = [first[n] * second[n + 6] - first[n + 6] * second[n] for n in range(6)]
            else:
                terms = [first[n] * second[n] + first[n + 6] * second[n + 6] for n in range(6)]
            value = (terms[0] + terms[1]) + (terms[2] + terms[3]) + (terms[4] + terms[5])
            total, error = two_sum(acc[2 * entry], value)
            acc[2 * entry] = total
            acc[2 * entry + 1] = acc[2 * entry + 1] + error
        return carry

    lax.fori_loop(0, depths, gram_layers, 0)

    def fold(high, low, shift, axis):
        total, error = two_sum(high, pltpu.roll(high, shift, axis))
        return total, low + pltpu.roll(low, shift, axis) + error

    sub = lax.broadcasted_iota(jnp.int32, (ROWS, LANES), 0)
    row = blank
    for start in range(0, len(ENTRIES), 8):
        highs, lows = blank, blank
        for entry in range(start, min(start + 8, len(ENTRIES))):
            high, low = acc[2 * entry], acc[2 * entry + 1]
            for shift in (4, 2, 1):
                high, low = fold(high, low, shift, 0)
            highs = jnp.where(sub == entry - start, high, highs)
            lows = jnp.where(sub == entry - start, low, lows)
        for shift in (64, 32, 16, 8, 4, 2, 1):
            highs, lows = fold(highs, lows, shift, 1)
        row = jnp.where(lane == sub + start, highs, row)
        row = jnp.where(lane == sub + start + 64, lows, row)
    for shift in (4, 2, 1):
        row = row + pltpu.roll(row, shift, 0)
    for number in range(pieces * lats // ROWS):
        gram_ref[number * ROWS : (number + 1) * ROWS] = row


def quick(a, b):
    total = a + b
    return total, b - (total - a)


def split(a):
    big = a * 4097.0
    high = big - (big - a)
    return high, a - high


def two_product(a, b):
    value = a * b
    ah, al = split(a)
    bh, bl = split(b)
    return value, ((ah * bh - value) + ah * bl + al * bh) + al * bl


def add(a, b):
    total, error = two_sum(a[0], b[0])
    return quick(total, error + (a[1] + b[1]))


def neg(a):
    return (-a[0], -a[1])


def mul(a, b):
    value, error = two_product(a[0], b[0])
    return quick(value, error + (a[0] * b[1] + a[1] * b[0]))


def div(a, b):
    first = a[0] / b[0]
    zero = jnp.zeros_like(first)
    rest = add(a, neg(mul(b, (first, zero))))
    second = rest[0] / b[0]
    rest = add(rest, neg(mul(b, (second, zero))))
    third = rest[0] / b[0]
    return add(quick(first, second), (third, zero))


def c_add(a, b):
    return (add(a[0], b[0]), add(a[1], b[1]))


def c_neg(a):
    return (neg(a[0]), neg(a[1]))


def c_conj(a):
    return (a[0], neg(a[1]))


def c_mul(a, b):
    return (
        add(mul(a[0], b[0]), neg(mul(a[1], b[1]))),
        add(mul(a[0], b[1]), mul(a[1], b[0])),
    )


def c_div(a, b):
    top = c_mul(a, c_conj(b))
    bottom = add(mul(b[0], b[0]), mul(b[1], b[1]))
    return (div(top[0], bottom), div(top[1], bottom))


def c_over(a, real):
    return (div(a[0], real), div(a[1], real))


def total_of(values):
    result = values[0]
    for value in values[1:]:
        result = c_add(result, value)
    return result


def coefficients(gram):
    rho = gram[0, 0]
    alpha = c_div(rho, gram[0, 1])
    one_half = c_neg(alpha)

    def form(coeffs, left, right):
        rows = []
        for i, factor in enumerate(coeffs):
            inner = total_of(
                [
                    gram[i + left, j + right]
                    if other is None
                    else c_mul(gram[i + left, j + right], other)
                    for j, other in enumerate(coeffs)
                ]
            )
            rows.append(inner if factor is None else c_mul(c_conj(factor), inner))
        return total_of(rows)

    omega = c_over(form([None, one_half], 1, 0), form([None, one_half], 1, 1)[0])
    res1 = c_neg(c_add(alpha, omega))
    res2 = c_mul(alpha, omega)
    new_rho = total_of([gram[0, 0], c_mul(gram[0, 1], res1), c_mul(gram[0, 2], res2)])
    mix = c_mul(c_div(new_rho, rho), c_div(alpha, omega))
    dir0 = (add((jnp.ones_like(mix[0][0]), jnp.zeros_like(mix[0][0])), mix[0]), mix[1])
    dir1 = c_add(res1, c_neg(c_mul(mix, omega)))
    dir2 = res2
    along = total_of(
        [c_mul(gram[0, 1], dir0), c_mul(gram[0, 2], dir1), c_mul(gram[0, 3], dir2)]
    )
    alpha2 = c_div(new_rho, along)
    half1 = c_add(res1, c_neg(c_mul(alpha2, dir0)))
    half2 = c_add(res2, c_neg(c_mul(alpha2, dir1)))
    half3 = c_neg(c_mul(alpha2, dir2))
    half = [None, half1, half2, half3]
    omega2 = c_over(form(half, 1, 0), form(half, 1, 1)[0])
    out0 = total_of([alpha, omega, c_mul(alpha2, dir0), omega2])
    out1 = total_of([c_mul(omega, one_half), c_mul(alpha2, dir1), c_mul(omega2, half1)])
    out2 = c_add(c_mul(alpha2, dir2), c_mul(omega2, half2))
    out3 = c_mul(omega2, half3)
    return [(c[0][0], c[1][0]) for c in (out0, out1, out2, out3)]


def update_kernel(sizes, rows_ref, start_ref, basis_ref, out_ref):
    depths, lats, pieces = sizes
    high = jnp.zeros((ROWS, LANES), jnp.float32)
    low = high
    for number in range(pieces * lats // ROWS):
        high, error = two_sum(high, rows_ref[number * ROWS : (number + 1) * ROWS])
        low = low + error
    for shift in (4, 2, 1):
        high, error = two_sum(high, pltpu.roll(high, shift, 0))
        low = low + pltpu.roll(low, shift, 0) + error
    high, low = quick(high, low + pltpu.roll(high, 64, 1))

    def entry(number):
        return (
            jnp.broadcast_to(high[:, number : number + 1], (ROWS, LANES)),
            jnp.broadcast_to(low[:, number : number + 1], (ROWS, LANES)),
        )

    zero = jnp.zeros((ROWS, LANES), jnp.float32)
    gram = {}
    at = 0
    for i, j in PAIRS:
        real = entry(at)
        at += 1
        if i == j:
            gram[i, i] = (real, (zero, zero))
        else:
            gram[i, j] = (real, entry(at))
            gram[j, i] = c_conj(gram[i, j])
            at += 1
    factors = coefficients(gram)

    def layer(source, carry):
        for component in range(3):
            for z in range(2):
                real = start_ref[source, slot(0, component, z)]
                imag = start_ref[source, slot(1, component, z)]
                for b, (fr, fi) in enumerate(factors):
                    br = basis_ref[b, source, slot(0, component, z)]
                    bi = basis_ref[b, source, slot(1, component, z)]
                    real = real + (fr * br - fi * bi)
                    imag = imag + (fr * bi + fi * br)
                out_ref[source, slot(0, component, z)] = real
                out_ref[source, slot(1, component, z)] = imag
        return carry

    lax.fori_loop(0, depths, layer, 0)


def output_kernel(pieces, in_ref, field_ref, term_ref):
    for piece in range(pieces):
        cols = slice(piece * LANES, (piece + 1) * LANES)
        for z in range(2):
            term = None
            for component in range(3):
                values = []
                for kind in range(KINDS):
                    for part in range(2):
                        value = in_ref[kind * pieces + piece, slot(part, component, z)]
                        field_ref[kind * 12 + slot(part, component, z), :, cols] = value
                        values.append(value)
                product = values[0] * values[2] - values[1] * values[3]
                term = product if term is None else term + product
            term_ref[piece, z] = term


def local(conductivity, field_guess, tx_cell, rx_cell, rx_weight):
    pieces, lats = lax.axis_size("piece"), lax.axis_size("lat")
    depths = KINDS * pieces
    sizes = (depths, lats, pieces)
    width = conductivity.shape[2]
    layers = 2 * depths
    f32 = jnp.float32
    params = pltpu.CompilerParams

    packed = pl.pallas_call(
        functools.partial(pack_kernel, pieces),
        out_shape=jax.ShapeDtypeStruct((depths, 16, ROWS, LANES), f32),
        in_specs=[in_vmem()] * 2,
        out_specs=in_vmem(),
        compiler_params=params(vmem_limit_bytes=4 * MIB),
    )(field_guess.reshape(24, ROWS, width), conductivity)
    mid = lax.all_to_all(packed, DEPTH, 0, 0)
    border = [(i, i + 1) for i in range(1, lats - 1, 2)]
    inner = lax.ppermute(mid, "lat", [(i, i ^ 1) for i in range(lats)])
    outer = lax.ppermute(mid, "lat", border + [(b, a) for a, b in border])

    basis, rows = pl.pallas_call(
        functools.partial(basis_kernel, sizes),
        out_shape=(
            jax.ShapeDtypeStruct((BASIS - 1, depths, 12, ROWS, LANES), f32),
            jax.ShapeDtypeStruct((pieces * lats, LANES), f32),
        ),
        in_specs=[in_smem()] * 3 + [in_vmem()] * 3,
        out_specs=(in_vmem(), in_vmem()),
        scratch_shapes=basis_scratch(depths),
        compiler_params=params(vmem_limit_bytes=28 * MIB),
    )(tx_cell, rx_cell, rx_weight.reshape(1, -1), inner, mid, outer)

    rows = lax.all_to_all(rows, ("piece", "lat"), 0, 0)
    moved = pl.pallas_call(
        functools.partial(update_kernel, sizes),
        out_shape=jax.ShapeDtypeStruct((depths, 12, ROWS, LANES), f32),
        in_specs=[in_vmem()] * 3,
        out_specs=in_vmem(),
        compiler_params=params(vmem_limit_bytes=8 * MIB),
    )(rows, mid, basis)
    moved = lax.all_to_all(moved, DEPTH, 0, 0)
    fields, terms = pl.pallas_call(
        functools.partial(output_kernel, pieces),
        out_shape=(
            jax.ShapeDtypeStruct((24, ROWS, width), f32),
            jax.ShapeDtypeStruct((pieces, 2, ROWS, LANES), f32),
        ),
        in_specs=[in_vmem()],
        out_specs=(in_vmem(), in_vmem()),
        compiler_params=params(vmem_limit_bytes=4 * MIB),
    )(moved)
    gradient = jnp.sum(lax.all_to_all(terms, "tx", 0, 0), axis=0)
    return (fields.reshape(field_guess.shape), gradient)


def solution(mesh):
    grid = mesh.devices
    split = Mesh(
        grid.reshape((KINDS, grid.shape[0] // KINDS) + grid.shape[1:]),
        DEPTH + tuple(mesh.axis_names[1:]),
    )
    return jax.shard_map(
        local,
        mesh=split,
        in_specs=(
            P(DEPTH, "lat", None),
            P("tx", None, None, None, DEPTH, "lat", None),
            P("tx"),
            P("tx", None),
            P("tx", None, None),
        ),
        out_specs=(P("tx", None, None, None, DEPTH, "lat", None), P(DEPTH, "lat", "tx")),
        check_vma=False,
    )
```

```python
import functools

import jax
import jax.numpy as jnp
from jax import lax
from jax.experimental import pallas as pl
from jax.experimental.pallas import tpu as pltpu
from jax.sharding import Mesh
from jax.sharding import PartitionSpec as P

SOURCE = 20.0
KINDS = 2
BASIS = 5
ROWS = 8
LANES = 128
DEPTH = ("kind", "piece")
PAIRS = [(i, j) for i in range(BASIS) for j in range(i, BASIS)]
ENTRIES = [(i, j, part) for i, j in PAIRS for part in range(1 if i == j else 2)]
MIB = 1 << 20


def in_vmem():
    return pl.BlockSpec(memory_space=pltpu.VMEM)


def in_smem():
    return pl.BlockSpec(memory_space=pltpu.SMEM)


def slot(part, component, layer):
    return (part * 3 + component) * 2 + layer


def pack_kernel(pieces, guess_ref, cond_ref, out_ref):
    lane = lax.broadcasted_iota(jnp.int32, (ROWS, LANES), 1)
    blank = jnp.zeros((ROWS, LANES), jnp.float32)
    for kind in range(KINDS):
        for piece in range(pieces):
            to = kind * pieces + piece
            edges = [blank, blank]
            for item in range(14):

                def tile(number):
                    if number < 0 or number >= pieces:
                        return blank
                    cols = slice(number * LANES, (number + 1) * LANES)
                    if item < 12:
                        return guess_ref[kind * 12 + item, :, cols]
                    return cond_ref[item - 12, :, cols]

                out_ref[to, item] = tile(piece)
                ends = jnp.where(lane >= LANES // 2, tile(piece - 1), tile(piece + 1))
                place = item % 8
                moved = pltpu.roll(ends, (16 * place + 8) % LANES, 1)
                edges[item // 8] = jnp.where(lane // 16 == place, moved, edges[item // 8])
            out_ref[to, 14] = edges[0]
            out_ref[to, 15] = edges[1]


def two_sum(a, b):
    total = a + b
    other = total - a
    return total, (a - (total - other)) + (b - other)


def edge_columns(ref, source, item, lane):
    edge = pltpu.roll(ref[source, 14 + item // 8], LANES - (16 * (item % 8) + 8), 1)
    return jnp.where((lane < 8) | (lane >= LANES - 8), edge, 0.0)


def early_kernel(sizes, tx_ref, rx_ref, weight_ref, mid_ref, edge_ref, source_ref):
    depths, lats, pieces = sizes
    span = 2 * LANES
    width = pieces * LANES
    lat_index = lax.axis_index("lat")
    kind = lax.axis_index("kind")
    piece = lax.axis_index("piece")
    lane = lax.broadcasted_iota(jnp.int32, (ROWS, LANES), 1)

    def spread(source, carry):
        for number, ref in enumerate((mid_ref,)):
            rows = slice(number * ROWS, (number + 1) * ROWS)
            for item in range(14):
                edge = edge_columns(ref, source, item, lane)
                edge_ref[item // 2, 2 * source + item % 2, rows] = edge
        return carry

    lax.fori_loop(0, depths, spread, 0, unroll=2)

    for z in range(2 * depths):
        for part in range(2):
            source_ref[part, z] = jnp.zeros((2 * ROWS, span), jnp.float32)
    line = lax.broadcasted_iota(jnp.int32, (1, span), 1)

    def place_of(cell):
        col = (cell & (width - 1)) - piece * LANES
        rest = lax.shift_right_logical(cell, width.bit_length() - 1)
        row = (rest & (lats * ROWS - 1)) - lat_index * ROWS
        z = lax.shift_right_logical(rest, (lats * ROWS).bit_length() - 1)
        return (row >= -4) & (row < 12) & (col >= -8) & (col < LANES + 8), z, row, col

    def add_source(cell, real, imag):
        held, z, row, col = place_of(cell)

        @pl.when(held)
        def _():
            hit = line == (col & (span - 1))
            at = pl.ds(row & (2 * ROWS - 1), 1)
            source_ref[0, z, at] = source_ref[0, z, at] + jnp.where(hit, real, 0.0)
            source_ref[1, z, at] = source_ref[1, z, at] + jnp.where(hit, imag, 0.0)

    @pl.when(kind == 0)
    def _():
        add_source(tx_ref[0], jnp.float32(0.0), jnp.float32(-SOURCE))

    @pl.when(kind == 1)
    def _():
        def each(group, carry):
            numbers = [8 * group + n for n in range(8)]
            some = place_of(rx_ref[0, numbers[0]])[0]
            for r in numbers[1:]:
                some = some | place_of(rx_ref[0, r])[0]

            @pl.when(some)
            def _():
                for r in numbers:
                    add_source(rx_ref[0, r], weight_ref[0, 2 * r], weight_ref[0, 2 * r + 1])

            return carry

        lax.fori_loop(0, rx_ref.shape[1] // 8, each, 0)


def basis_scratch(depths):
    layers = 2 * depths
    f32 = jnp.float32
    return [
        pltpu.VMEM((BASIS, 6, layers + 1, 2 * ROWS, 2 * LANES), f32),
        pltpu.VMEM((7, layers, 2 * ROWS, LANES), f32),
        pltpu.VMEM((4, 3 * ROWS, 2 * LANES), f32),
        pltpu.VMEM((4, 2 * ROWS, 2 * LANES), f32),
        pltpu.VMEM((layers, 2 * ROWS, 2 * LANES), f32),
        pltpu.VMEM((3 * ROWS, 2 * LANES), f32),
        pltpu.VMEM((2 * ROWS, 2 * LANES), f32),
        pltpu.VMEM((2 * len(ENTRIES), ROWS, LANES), f32),
    ]


def basis_kernel(
    sizes, edge_ref, source_ref, inner_ref, mid_ref, outer_ref, basis_ref, gram_ref,
    field, edges, curl_start, curl, cond, inside_start, inside, acc,
):
    depths, lats, pieces = sizes
    layers = 2 * depths
    span = 2 * LANES
    width = pieces * LANES
    lat_index = lax.axis_index("lat")
    kind = lax.axis_index("kind")
    piece = lax.axis_index("piece")
    lane = lax.broadcasted_iota(jnp.int32, (ROWS, LANES), 1)
    blank = jnp.zeros((ROWS, LANES), jnp.float32)

    def within(rows, row):
        lane_w = lax.broadcasted_iota(jnp.int32, (rows, span), 1)
        x_at = lat_index * ROWS + row
        y_at = piece * LANES + jnp.where(lane_w >= LANES + 64, lane_w - span, lane_w)
        good = (x_at >= 0) & (x_at < lats * ROWS) & (y_at >= 0) & (y_at < width)
        return jnp.where(good, 1.0, 0.0)

    row_s = lax.broadcasted_iota(jnp.int32, (3 * ROWS, span), 0)
    inside_start[...] = within(3 * ROWS, row_s - ROWS)
    row_b = lax.broadcasted_iota(jnp.int32, (2 * ROWS, span), 0)
    inside[...] = within(2 * ROWS, jnp.where(row_b >= 12, row_b - 16, row_b))

    first_core = lat_index % 2 == 0

    def received(source, item):
        outer, inner = outer_ref[source, item], inner_ref[source, item]
        left = jnp.where(first_core, outer, inner)
        right = jnp.where(first_core, inner, outer)
        return left, mid_ref[source, item], right


    def spread(source, carry):
        for item in range(14):
            at = (item // 2, 2 * source + item % 2)
            outer = edge_columns(outer_ref, source, item, lane)
            inner = edge_columns(inner_ref, source, item, lane)
            edges[at + (slice(0, ROWS),)] = jnp.where(first_core, outer, inner)
            edges[at + (slice(ROWS, 2 * ROWS),)] = jnp.where(first_core, inner, outer)
        return carry

    lax.fori_loop(0, depths, spread, 0, unroll=2)

    empty = jnp.zeros((2 * ROWS, span), jnp.float32)
    for number in range(BASIS - 1):
        for component in range(6):
            field[number, component, layers] = empty

    def ahead(values, axis):
        return pltpu.roll(values, values.shape[axis] - 1, axis) - values

    def behind(values, axis):
        return values - pltpu.roll(values, 1, axis)

    def curl_ahead(here, above, keep):
        uz, ux, uy = here
        hz = (ahead(uy, 0) - ahead(ux, 1)) * keep
        hx = (ahead(uz, 1) - (above[1] - uy)) * keep
        hy = ((above[0] - ux) - ahead(uz, 0)) * keep
        return hz, hx, hy

    def curl_behind(h, below):
        hz, hx, hy = h
        return (
            behind(hy, 0) - behind(hx, 1),
            behind(hz, 1) - (hy - below[1]),
            (hx - below[0]) - behind(hz, 0),
        )

    def start_tile(number, z, source, layer):
        body = jnp.concatenate(received(source, 2 * number + layer), axis=0)
        left, right = edges[number, z, :ROWS], edges[number, z, ROWS:]
        edge = jnp.concatenate([left, edge_ref[number, z, 0:ROWS], right], axis=0)
        return jnp.concatenate([body, edge], axis=1)

    def merge(values):
        sub = lax.broadcasted_iota(jnp.int32, (ROWS, span), 0)
        sides = jnp.where(sub < 4, values[2 * ROWS :], values[:ROWS])
        return jnp.concatenate([values[ROWS : 2 * ROWS], sides], axis=0)

    for number in range(4):
        curl_start[number] = jnp.zeros((3 * ROWS, span), jnp.float32)

    def start_layers(source, carry):
        keep = inside_start[...]
        below = [[curl_start[0], curl_start[1]], [curl_start[2], curl_start[3]]]
        for layer in range(2):
            z = 2 * source + layer
            tiles = [start_tile(c, z, source, layer) for c in range(6)]
            sigma = start_tile(6, z, source, layer)
            cond[z] = merge(sigma)
            for part in range(2):
                here = tiles[3 * part : 3 * part + 3]
                if layer == 0:
                    above = [start_tile(3 * part + c, z + 1, source, 1) for c in (1, 2)]
                else:
                    last = source == depths - 1
                    after = jnp.minimum(source + 1, depths - 1)
                    above = [
                        jnp.where(last, 0.0, start_tile(3 * part + c, 2 * after, after, 0))
                        for c in (1, 2)
                    ]
                h = curl_ahead(here, above, keep)
                outs = curl_behind(h, below[part])
                below[part] = [h[1], h[2]]
                for component, value in enumerate(outs):
                    other = sigma * tiles[3 * (1 - part) + component]
                    value = other - value if part == 0 else -value - other
                    value = merge(value) * inside[...]
                    if component == 0:
                        value = value + source_ref[part, z]
                    field[0, 3 * part + component, z] = value
        for number in range(4):
            curl_start[number] = below[number // 2][number % 2]
        return carry

    lax.fori_loop(0, depths, start_layers, 0)

    for step in range(BASIS - 1):
        for number in range(4):
            curl[number] = empty

        def apply_layers(source, carry, step=step):
            keep = inside[...]
            below = [[curl[0], curl[1]], [curl[2], curl[3]]]
            for layer in range(2):
                z = 2 * source + layer
                sigma = cond[z]
                for part in range(2):
                    here = [field[step, 3 * part + c, z] for c in range(3)]
                    above = [field[step, 3 * part + c, z + 1] for c in (1, 2)]
                    h = curl_ahead(here, above, keep)
                    outs = curl_behind(h, below[part])
                    below[part] = [h[1], h[2]]
                    for component, value in enumerate(outs):
                        if step == BASIS - 2:
                            mine = (slice(0, ROWS), slice(0, LANES))
                        else:
                            mine = (slice(None), slice(None))
                        near = field[(step, 3 * (1 - part) + component, z) + mine]
                        other = sigma[mine] * near
                        value = value[mine]
                        value = value - other if part == 0 else value + other
                        if step < BASIS - 2:
                            value = value * keep
                        field[(step + 1, 3 * part + component, z) + mine] = value
            for number in range(4):
                curl[number] = below[number // 2][number % 2]
            return carry

        lax.fori_loop(0, depths, apply_layers, 0, unroll=2)

    for entry in range(2 * len(ENTRIES)):
        acc[entry] = blank

    def gram_layers(source, carry):
        tiles = []
        for b in range(BASIS):
            group = []
            for component in range(6):
                for layer in range(2):
                    tile = field[b, component, 2 * source + layer, 0:ROWS, 0:LANES]
                    group.append(tile)
                    if b < BASIS - 1:
                        basis_ref[b, source, 2 * component + layer] = tile
            tiles.append(group)
        for entry, (i, j, part) in enumerate(ENTRIES):
            first, second = tiles[i], tiles[j]
            if part:
                terms = [first[n] * second[n + 6] - first[n + 6] * second[n] for n in range(6)]
            else:
                terms = [first[n] * second[n] + first[n + 6] * second[n + 6] for n in range(6)]
            value = (terms[0] + terms[1]) + (terms[2] + terms[3]) + (terms[4] + terms[5])
            total, error = two_sum(acc[2 * entry], value)
            acc[2 * entry] = total
            acc[2 * entry + 1] = acc[2 * entry + 1] + error
        return carry

    lax.fori_loop(0, depths, gram_layers, 0)

    def fold(high, low, shift, axis):
        total, error = two_sum(high, pltpu.roll(high, shift, axis))
        return total, low + pltpu.roll(low, shift, axis) + error

    sub = lax.broadcasted_iota(jnp.int32, (ROWS, LANES), 0)
    row = blank
    for start in range(0, len(ENTRIES), 8):
        highs, lows = blank, blank
        for entry in range(start, min(start + 8, len(ENTRIES))):
            high, low = acc[2 * entry], acc[2 * entry + 1]
            for shift in (4, 2, 1):
                high, low = fold(high, low, shift, 0)
            highs = jnp.where(sub == entry - start, high, highs)
            lows = jnp.where(sub == entry - start, low, lows)
        for shift in (64, 32, 16, 8, 4, 2, 1):
            highs, lows = fold(highs, lows, shift, 1)
        row = jnp.where(lane == sub + start, highs, row)
        row = jnp.where(lane == sub + start + 64, lows, row)
    for shift in (4, 2, 1):
        row = row + pltpu.roll(row, shift, 0)
    for number in range(pieces * lats // ROWS):
        gram_ref[number * ROWS : (number + 1) * ROWS] = row


def quick(a, b):
    total = a + b
    return total, b - (total - a)


def split(a):
    big = a * 4097.0
    high = big - (big - a)
    return high, a - high


def two_product(a, b):
    value = a * b
    ah, al = split(a)
    bh, bl = split(b)
    return value, ((ah * bh - value) + ah * bl + al * bh) + al * bl


def add(a, b):
    total, error = two_sum(a[0], b[0])
    return quick(total, error + (a[1] + b[1]))


def neg(a):
    return (-a[0], -a[1])


def mul(a, b):
    value, error = two_product(a[0], b[0])
    return quick(value, error + (a[0] * b[1] + a[1] * b[0]))


def div(a, b):
    first = a[0] / b[0]
    zero = jnp.zeros_like(first)
    rest = add(a, neg(mul(b, (first, zero))))
    second = rest[0] / b[0]
    rest = add(rest, neg(mul(b, (second, zero))))
    third = rest[0] / b[0]
    return add(quick(first, second), (third, zero))


def c_add(a, b):
    return (add(a[0], b[0]), add(a[1], b[1]))


def c_neg(a):
    return (neg(a[0]), neg(a[1]))


def c_conj(a):
    return (a[0], neg(a[1]))


def c_mul(a, b):
    return (
        add(mul(a[0], b[0]), neg(mul(a[1], b[1]))),
        add(mul(a[0], b[1]), mul(a[1], b[0])),
    )


def c_div(a, b):
    top = c_mul(a, c_conj(b))
    bottom = add(mul(b[0], b[0]), mul(b[1], b[1]))
    return (div(top[0], bottom), div(top[1], bottom))


def c_over(a, real):
    return (div(a[0], real), div(a[1], real))


def total_of(values):
    result = values[0]
    for value in values[1:]:
        result = c_add(result, value)
    return result


def coefficients(gram):
    rho = gram[0, 0]
    alpha = c_div(rho, gram[0, 1])
    one_half = c_neg(alpha)

    def form(coeffs, left, right):
        rows = []
        for i, factor in enumerate(coeffs):
            inner = total_of(
                [
                    gram[i + left, j + right]
                    if other is None
                    else c_mul(gram[i + left, j + right], other)
                    for j, other in enumerate(coeffs)
                ]
            )
            rows.append(inner if factor is None else c_mul(c_conj(factor), inner))
        return total_of(rows)

    omega = c_over(form([None, one_half], 1, 0), form([None, one_half], 1, 1)[0])
    res1 = c_neg(c_add(alpha, omega))
    res2 = c_mul(alpha, omega)
    new_rho = total_of([gram[0, 0], c_mul(gram[0, 1], res1), c_mul(gram[0, 2], res2)])
    mix = c_mul(c_div(new_rho, rho), c_div(alpha, omega))
    dir0 = (add((jnp.ones_like(mix[0][0]), jnp.zeros_like(mix[0][0])), mix[0]), mix[1])
    dir1 = c_add(res1, c_neg(c_mul(mix, omega)))
    dir2 = res2
    along = total_of(
        [c_mul(gram[0, 1], dir0), c_mul(gram[0, 2], dir1), c_mul(gram[0, 3], dir2)]
    )
    alpha2 = c_div(new_rho, along)
    half1 = c_add(res1, c_neg(c_mul(alpha2, dir0)))
    half2 = c_add(res2, c_neg(c_mul(alpha2, dir1)))
    half3 = c_neg(c_mul(alpha2, dir2))
    half = [None, half1, half2, half3]
    omega2 = c_over(form(half, 1, 0), form(half, 1, 1)[0])
    out0 = total_of([alpha, omega, c_mul(alpha2, dir0), omega2])
    out1 = total_of([c_mul(omega, one_half), c_mul(alpha2, dir1), c_mul(omega2, half1)])
    out2 = c_add(c_mul(alpha2, dir2), c_mul(omega2, half2))
    out3 = c_mul(omega2, half3)
    return [(c[0][0], c[1][0]) for c in (out0, out1, out2, out3)]


def update_kernel(sizes, rows_ref, start_ref, basis_ref, out_ref):
    depths, lats, pieces = sizes
    high = jnp.zeros((ROWS, LANES), jnp.float32)
    low = high
    for number in range(pieces * lats // ROWS):
        high, error = two_sum(high, rows_ref[number * ROWS : (number + 1) * ROWS])
        low = low + error
    for shift in (4, 2, 1):
        high, error = two_sum(high, pltpu.roll(high, shift, 0))
        low = low + pltpu.roll(low, shift, 0) + error
    high, low = quick(high, low + pltpu.roll(high, 64, 1))

    def entry(number):
        return (
            jnp.broadcast_to(high[:, number : number + 1], (ROWS, LANES)),
            jnp.broadcast_to(low[:, number : number + 1], (ROWS, LANES)),
        )

    zero = jnp.zeros((ROWS, LANES), jnp.float32)
    gram = {}
    at = 0
    for i, j in PAIRS:
        real = entry(at)
        at += 1
        if i == j:
            gram[i, i] = (real, (zero, zero))
        else:
            gram[i, j] = (real, entry(at))
            gram[j, i] = c_conj(gram[i, j])
            at += 1
    factors = coefficients(gram)

    def layer(source, carry):
        for component in range(3):
            for z in range(2):
                real = start_ref[source, slot(0, component, z)]
                imag = start_ref[source, slot(1, component, z)]
                for b, (fr, fi) in enumerate(factors):
                    br = basis_ref[b, source, slot(0, component, z)]
                    bi = basis_ref[b, source, slot(1, component, z)]
                    real = real + (fr * br - fi * bi)
                    imag = imag + (fr * bi + fi * br)
                out_ref[source, slot(0, component, z)] = real
                out_ref[source, slot(1, component, z)] = imag
        return carry

    lax.fori_loop(0, depths, layer, 0)


def output_kernel(pieces, in_ref, field_ref, term_ref):
    for piece in range(pieces):
        cols = slice(piece * LANES, (piece + 1) * LANES)
        for z in range(2):
            term = None
            for component in range(3):
                values = []
                for kind in range(KINDS):
                    for part in range(2):
                        value = in_ref[kind * pieces + piece, slot(part, component, z)]
                        field_ref[kind * 12 + slot(part, component, z), :, cols] = value
                        values.append(value)
                product = values[0] * values[2] - values[1] * values[3]
                term = product if term is None else term + product
            term_ref[piece, z] = term


def local(conductivity, field_guess, tx_cell, rx_cell, rx_weight):
    pieces, lats = lax.axis_size("piece"), lax.axis_size("lat")
    depths = KINDS * pieces
    sizes = (depths, lats, pieces)
    width = conductivity.shape[2]
    layers = 2 * depths
    f32 = jnp.float32
    params = pltpu.CompilerParams

    packed = pl.pallas_call(
        functools.partial(pack_kernel, pieces),
        out_shape=jax.ShapeDtypeStruct((depths, 16, ROWS, LANES), f32),
        in_specs=[in_vmem()] * 2,
        out_specs=in_vmem(),
        compiler_params=params(vmem_limit_bytes=4 * MIB),
    )(field_guess.reshape(24, ROWS, width), conductivity)
    mid = lax.all_to_all(packed, DEPTH, 0, 0)
    border = [(i, i + 1) for i in range(1, lats - 1, 2)]
    inner = lax.ppermute(mid, "lat", [(i, i ^ 1) for i in range(lats)])
    outer = lax.ppermute(mid, "lat", border + [(b, a) for a, b in border])

    edges, sources = pl.pallas_call(
        functools.partial(early_kernel, sizes),
        out_shape=(
            jax.ShapeDtypeStruct((7, 2 * depths, ROWS, LANES), f32),
            jax.ShapeDtypeStruct((2, 2 * depths, 2 * ROWS, 2 * LANES), f32),
        ),
        in_specs=[in_smem()] * 3 + [in_vmem()],
        out_specs=(in_vmem(), in_vmem()),
        compiler_params=params(vmem_limit_bytes=8 * MIB),
    )(tx_cell, rx_cell, rx_weight.reshape(1, -1), mid)
    basis, rows = pl.pallas_call(
        functools.partial(basis_kernel, sizes),
        out_shape=(
            jax.ShapeDtypeStruct((BASIS - 1, depths, 12, ROWS, LANES), f32),
            jax.ShapeDtypeStruct((pieces * lats, LANES), f32),
        ),
        in_specs=[in_vmem()] * 5,
        out_specs=(in_vmem(), in_vmem()),
        scratch_shapes=basis_scratch(depths),
        compiler_params=params(vmem_limit_bytes=28 * MIB),
    )(edges, sources, inner, mid, outer)

    rows = lax.all_to_all(rows, ("piece", "lat"), 0, 0)
    moved = pl.pallas_call(
        functools.partial(update_kernel, sizes),
        out_shape=jax.ShapeDtypeStruct((depths, 12, ROWS, LANES), f32),
        in_specs=[in_vmem()] * 3,
        out_specs=in_vmem(),
        compiler_params=params(vmem_limit_bytes=8 * MIB),
    )(rows, mid, basis)
    moved = lax.all_to_all(moved, DEPTH, 0, 0)
    fields, terms = pl.pallas_call(
        functools.partial(output_kernel, pieces),
        out_shape=(
            jax.ShapeDtypeStruct((24, ROWS, width), f32),
            jax.ShapeDtypeStruct((pieces, 2, ROWS, LANES), f32),
        ),
        in_specs=[in_vmem()],
        out_specs=(in_vmem(), in_vmem()),
        compiler_params=params(vmem_limit_bytes=4 * MIB),
    )(moved)
    gradient = jnp.sum(lax.all_to_all(terms, "tx", 0, 0), axis=0)
    return (fields.reshape(field_guess.shape), gradient)


def solution(mesh):
    grid = mesh.devices
    split = Mesh(
        grid.reshape((KINDS, grid.shape[0] // KINDS) + grid.shape[1:]),
        DEPTH + tuple(mesh.axis_names[1:]),
    )
    return jax.shard_map(
        local,
        mesh=split,
        in_specs=(
            P(DEPTH, "lat", None),
            P("tx", None, None, None, DEPTH, "lat", None),
            P("tx"),
            P("tx", None),
            P("tx", None, None),
        ),
        out_specs=(P("tx", None, None, None, DEPTH, "lat", None), P(DEPTH, "lat", "tx")),
        check_vma=False,
    )
```

```python
import functools

import jax
import jax.numpy as jnp
from jax import lax
from jax.experimental import pallas as pl
from jax.experimental.pallas import tpu as pltpu
from jax.sharding import Mesh
from jax.sharding import PartitionSpec as P

SOURCE = 20.0
KINDS = 2
BASIS = 5
ROWS = 8
LANES = 128
DEPTH = ("kind", "piece")
PAIRS = [(i, j) for i in range(BASIS) for j in range(i, BASIS)]
ENTRIES = [(i, j, part) for i, j in PAIRS for part in range(1 if i == j else 2)]
MIB = 1 << 20
TILES = 16
NEAR = 5
NEAR_TILES = TILES * NEAR // ROWS


def in_vmem():
    return pl.BlockSpec(memory_space=pltpu.VMEM)


def in_smem():
    return pl.BlockSpec(memory_space=pltpu.SMEM)


def slot(part, component, layer):
    return (part * 3 + component) * 2 + layer


def pack_kernel(pieces, guess_ref, cond_ref, out_ref):
    lane = lax.broadcasted_iota(jnp.int32, (ROWS, LANES), 1)
    blank = jnp.zeros((ROWS, LANES), jnp.float32)
    for kind in range(KINDS):
        for piece in range(pieces):
            to = kind * pieces + piece
            edges = [blank, blank]
            for item in range(14):

                def tile(number):
                    if number < 0 or number >= pieces:
                        return blank
                    cols = slice(number * LANES, (number + 1) * LANES)
                    if item < 12:
                        return guess_ref[kind * 12 + item, :, cols]
                    return cond_ref[item - 12, :, cols]

                out_ref[to, item] = tile(piece)
                ends = jnp.where(lane >= LANES // 2, tile(piece - 1), tile(piece + 1))
                place = item % 8
                moved = pltpu.roll(ends, (16 * place + 8) % LANES, 1)
                edges[item // 8] = jnp.where(lane // 16 == place, moved, edges[item // 8])
            out_ref[to, 14] = edges[0]
            out_ref[to, 15] = edges[1]


def two_sum(a, b):
    total = a + b
    other = total - a
    return total, (a - (total - other)) + (b - other)


def gather(read, moves, sub):
    found = {}
    for tile, row, to in moves:
        found.setdefault((tile, (to - row) % ROWS), []).append(to)
    result = jnp.zeros((ROWS, LANES), jnp.float32)
    for (tile, shift), rows in found.items():
        value = pltpu.roll(read(tile), shift, 0) if shift else read(tile)
        result = jnp.where((sub >= min(rows)) & (sub <= max(rows)), value, result)
    return result


def border_kernel(depths, mid_ref, outer_ref, inner_ref):
    sub = lax.broadcasted_iota(jnp.int32, (ROWS, LANES), 0)
    first_core = lax.axis_index("lat") % 2 == 0

    def each(source, carry):
        for number in range(NEAR_TILES):
            ends = []
            for first in (0, ROWS - NEAR):
                places = [divmod(number * ROWS + to, NEAR) for to in range(ROWS)]
                moves = [(tile, first + row, to) for to, (tile, row) in enumerate(places)]
                ends.append(gather(lambda n: mid_ref[source, n], moves, sub))
            outer_ref[source, number] = jnp.where(first_core, ends[0], ends[1])
            inner_ref[source, number] = jnp.where(first_core, ends[1], ends[0])
        return carry

    lax.fori_loop(0, depths, each, 0, unroll=2)


def edge_columns(packs, item, lane):
    edge = pltpu.roll(packs[item // 8], LANES - (16 * (item % 8) + 8), 1)
    return jnp.where((lane < 8) | (lane >= LANES - 8), edge, 0.0)


def early_kernel(sizes, tx_ref, rx_ref, weight_ref, mid_ref, edge_ref, source_ref):
    depths, lats, pieces = sizes
    span = 2 * LANES
    width = pieces * LANES
    lat_index = lax.axis_index("lat")
    kind = lax.axis_index("kind")
    piece = lax.axis_index("piece")
    lane = lax.broadcasted_iota(jnp.int32, (ROWS, LANES), 1)

    def spread(source, carry):
        packs = [mid_ref[source, 14], mid_ref[source, 15]]
        for item in range(14):
            edge_ref[item // 2, 2 * source + item % 2] = edge_columns(packs, item, lane)
        return carry

    lax.fori_loop(0, depths, spread, 0, unroll=2)

    for z in range(2 * depths):
        for part in range(2):
            source_ref[part, z] = jnp.zeros((2 * ROWS, span), jnp.float32)
    line = lax.broadcasted_iota(jnp.int32, (1, span), 1)

    def place_of(cell):
        col = (cell & (width - 1)) - piece * LANES
        rest = lax.shift_right_logical(cell, width.bit_length() - 1)
        row = (rest & (lats * ROWS - 1)) - lat_index * ROWS
        z = lax.shift_right_logical(rest, (lats * ROWS).bit_length() - 1)
        return (row >= -4) & (row < 12) & (col >= -8) & (col < LANES + 8), z, row, col

    def add_source(cell, real, imag):
        held, z, row, col = place_of(cell)

        @pl.when(held)
        def _():
            hit = line == (col & (span - 1))
            at = pl.ds(row & (2 * ROWS - 1), 1)
            source_ref[0, z, at] = source_ref[0, z, at] + jnp.where(hit, real, 0.0)
            source_ref[1, z, at] = source_ref[1, z, at] + jnp.where(hit, imag, 0.0)

    @pl.when(kind == 0)
    def _():
        add_source(tx_ref[0], jnp.float32(0.0), jnp.float32(-SOURCE))

    @pl.when(kind == 1)
    def _():
        def each(group, carry):
            numbers = [8 * group + n for n in range(8)]
            some = place_of(rx_ref[0, numbers[0]])[0]
            for r in numbers[1:]:
                some = some | place_of(rx_ref[0, r])[0]

            @pl.when(some)
            def _():
                for r in numbers:
                    add_source(rx_ref[0, r], weight_ref[0, 2 * r], weight_ref[0, 2 * r + 1])

            return carry

        lax.fori_loop(0, rx_ref.shape[1] // 8, each, 0)


def basis_scratch(depths):
    layers = 2 * depths
    f32 = jnp.float32
    return [
        pltpu.VMEM((BASIS, 6, layers + 1, 2 * ROWS, 2 * LANES), f32),
        pltpu.VMEM((7, layers, 2 * ROWS, 2 * LANES), f32),
        pltpu.VMEM((4, 3 * ROWS, 2 * LANES), f32),
        pltpu.VMEM((4, 2 * ROWS, 2 * LANES), f32),
        pltpu.VMEM((layers, 2 * ROWS, 2 * LANES), f32),
        pltpu.VMEM((3 * ROWS, 2 * LANES), f32),
        pltpu.VMEM((2 * ROWS, 2 * LANES), f32),
        pltpu.VMEM((2 * len(ENTRIES), ROWS, LANES), f32),
    ]


def basis_kernel(
    sizes, edge_ref, source_ref, outer_ref, mid_ref, inner_ref, basis_ref, gram_ref,
    field, sides, curl_start, curl, cond, inside_start, inside, acc,
):
    depths, lats, pieces = sizes
    layers = 2 * depths
    span = 2 * LANES
    width = pieces * LANES
    lat_index = lax.axis_index("lat")
    kind = lax.axis_index("kind")
    piece = lax.axis_index("piece")
    lane = lax.broadcasted_iota(jnp.int32, (ROWS, LANES), 1)
    blank = jnp.zeros((ROWS, LANES), jnp.float32)

    def within(rows, row):
        lane_w = lax.broadcasted_iota(jnp.int32, (rows, span), 1)
        x_at = lat_index * ROWS + row
        y_at = piece * LANES + jnp.where(lane_w >= LANES + 64, lane_w - span, lane_w)
        good = (x_at >= 0) & (x_at < lats * ROWS) & (y_at >= 0) & (y_at < width)
        return jnp.where(good, 1.0, 0.0)

    row_s = lax.broadcasted_iota(jnp.int32, (3 * ROWS, span), 0)
    inside_start[...] = within(3 * ROWS, row_s - ROWS)
    row_b = lax.broadcasted_iota(jnp.int32, (2 * ROWS, span), 0)
    inside[...] = within(2 * ROWS, jnp.where(row_b >= 12, row_b - 16, row_b))

    first_core = lat_index % 2 == 0

    sub = lax.broadcasted_iota(jnp.int32, (ROWS, LANES), 0)

    def spread(source, carry):
        tiles = [], []
        for number in range(NEAR_TILES):
            outer, inner = outer_ref[source, number], inner_ref[source, number]
            tiles[0].append(jnp.where(first_core, outer, inner))
            tiles[1].append(jnp.where(first_core, inner, outer))
        for number, first in enumerate((ROWS - NEAR, 0)):
            found = []
            for item in range(TILES):
                places = [divmod(item * NEAR + row, ROWS) for row in range(NEAR)]
                moves = [(tile, at, first + row) for row, (tile, at) in enumerate(places)]
                found.append(gather(lambda n: tiles[number][n], moves, sub))
            for item in range(14):
                rows = slice(number * ROWS, (number + 1) * ROWS)
                at = (item // 2, 2 * source + item % 2, rows)
                sides[at + (slice(0, LANES),)] = found[item]
                sides[at + (slice(LANES, span),)] = edge_columns(found[14:], item, lane)
        return carry

    lax.fori_loop(0, depths, spread, 0, unroll=2)

    empty = jnp.zeros((2 * ROWS, span), jnp.float32)
    for number in range(BASIS - 1):
        for component in range(6):
            field[number, component, layers] = empty

    def ahead(values, axis):
        return pltpu.roll(values, values.shape[axis] - 1, axis) - values

    def behind(values, axis):
        return values - pltpu.roll(values, 1, axis)

    def curl_ahead(here, above, keep):
        uz, ux, uy = here
        hz = (ahead(uy, 0) - ahead(ux, 1)) * keep
        hx = (ahead(uz, 1) - (above[1] - uy)) * keep
        hy = ((above[0] - ux) - ahead(uz, 0)) * keep
        return hz, hx, hy

    def curl_behind(h, below):
        hz, hx, hy = h
        return (
            behind(hy, 0) - behind(hx, 1),
            behind(hz, 1) - (hy - below[1]),
            (hx - below[0]) - behind(hz, 0),
        )

    def start_tile(number, z, source, layer):
        own = jnp.concatenate([mid_ref[source, 2 * number + layer], edge_ref[number, z]], axis=1)
        left, right = sides[number, z, :ROWS], sides[number, z, ROWS:]
        return jnp.concatenate([left, own, right], axis=0)

    def merge(values):
        sub = lax.broadcasted_iota(jnp.int32, (ROWS, span), 0)
        sides = jnp.where(sub < 4, values[2 * ROWS :], values[:ROWS])
        return jnp.concatenate([values[ROWS : 2 * ROWS], sides], axis=0)

    for number in range(4):
        curl_start[number] = jnp.zeros((3 * ROWS, span), jnp.float32)

    def start_layers(source, carry):
        keep = inside_start[...]
        below = [[curl_start[0], curl_start[1]], [curl_start[2], curl_start[3]]]
        for layer in range(2):
            z = 2 * source + layer
            tiles = [start_tile(c, z, source, layer) for c in range(6)]
            sigma = start_tile(6, z, source, layer)
            cond[z] = merge(sigma)
            for part in range(2):
                here = tiles[3 * part : 3 * part + 3]
                if layer == 0:
                    above = [start_tile(3 * part + c, z + 1, source, 1) for c in (1, 2)]
                else:
                    last = source == depths - 1
                    after = jnp.minimum(source + 1, depths - 1)
                    above = [
                        jnp.where(last, 0.0, start_tile(3 * part + c, 2 * after, after, 0))
                        for c in (1, 2)
                    ]
                h = curl_ahead(here, above, keep)
                outs = curl_behind(h, below[part])
                below[part] = [h[1], h[2]]
                for component, value in enumerate(outs):
                    other = sigma * tiles[3 * (1 - part) + component]
                    value = other - value if part == 0 else -value - other
                    value = merge(value) * inside[...]
                    if component == 0:
                        value = value + source_ref[part, z]
                    field[0, 3 * part + component, z] = value
        for number in range(4):
            curl_start[number] = below[number // 2][number % 2]
        return carry

    lax.fori_loop(0, depths, start_layers, 0)

    for step in range(BASIS - 1):
        for number in range(4):
            curl[number] = empty

        def apply_layers(source, carry, step=step):
            keep = inside[...]
            below = [[curl[0], curl[1]], [curl[2], curl[3]]]
            for layer in range(2):
                z = 2 * source + layer
                sigma = cond[z]
                for part in range(2):
                    here = [field[step, 3 * part + c, z] for c in range(3)]
                    above = [field[step, 3 * part + c, z + 1] for c in (1, 2)]
                    h = curl_ahead(here, above, keep)
                    outs = curl_behind(h, below[part])
                    below[part] = [h[1], h[2]]
                    for component, value in enumerate(outs):
                        if step == BASIS - 2:
                            mine = (slice(0, ROWS), slice(0, LANES))
                        else:
                            mine = (slice(None), slice(None))
                        near = field[(step, 3 * (1 - part) + component, z) + mine]
                        other = sigma[mine] * near
                        value = value[mine]
                        value = value - other if part == 0 else value + other
                        if step < BASIS - 2:
                            value = value * keep
                        field[(step + 1, 3 * part + component, z) + mine] = value
            for number in range(4):
                curl[number] = below[number // 2][number % 2]
            return carry

        lax.fori_loop(0, depths, apply_layers, 0, unroll=2)

    for entry in range(2 * len(ENTRIES)):
        acc[entry] = blank

    def gram_layers(source, carry):
        tiles = []
        for b in range(BASIS):
            group = []
            for component in range(6):
                for layer in range(2):
                    tile = field[b, component, 2 * source + layer, 0:ROWS, 0:LANES]
                    group.append(tile)
                    if b < BASIS - 1:
                        basis_ref[b, source, 2 * component + layer] = tile
            tiles.append(group)
        for entry, (i, j, part) in enumerate(ENTRIES):
            first, second = tiles[i], tiles[j]
            if part:
                terms = [first[n] * second[n + 6] - first[n + 6] * second[n] for n in range(6)]
            else:
                terms = [first[n] * second[n] + first[n + 6] * second[n + 6] for n in range(6)]
            value = (terms[0] + terms[1]) + (terms[2] + terms[3]) + (terms[4] + terms[5])
            total, error = two_sum(acc[2 * entry], value)
            acc[2 * entry] = total
            acc[2 * entry + 1] = acc[2 * entry + 1] + error
        return carry

    lax.fori_loop(0, depths, gram_layers, 0)

    def fold(high, low, shift, axis):
        total, error = two_sum(high, pltpu.roll(high, shift, axis))
        return total, low + pltpu.roll(low, shift, axis) + error

    sub = lax.broadcasted_iota(jnp.int32, (ROWS, LANES), 0)
    row = blank
    for start in range(0, len(ENTRIES), 8):
        highs, lows = blank, blank
        for entry in range(start, min(start + 8, len(ENTRIES))):
            high, low = acc[2 * entry], acc[2 * entry + 1]
            for shift in (4, 2, 1):
                high, low = fold(high, low, shift, 0)
            highs = jnp.where(sub == entry - start, high, highs)
            lows = jnp.where(sub == entry - start, low, lows)
        for shift in (64, 32, 16, 8, 4, 2, 1):
            highs, lows = fold(highs, lows, shift, 1)
        row = jnp.where(lane == sub + start, highs, row)
        row = jnp.where(lane == sub + start + 64, lows, row)
    for shift in (4, 2, 1):
        row = row + pltpu.roll(row, shift, 0)
    for number in range(pieces * lats // ROWS):
        gram_ref[number * ROWS : (number + 1) * ROWS] = row


def quick(a, b):
    total = a + b
    return total, b - (total - a)


def split(a):
    big = a * 4097.0
    high = big - (big - a)
    return high, a - high


def two_product(a, b):
    value = a * b
    ah, al = split(a)
    bh, bl = split(b)
    return value, ((ah * bh - value) + ah * bl + al * bh) + al * bl


def add(a, b):
    total, error = two_sum(a[0], b[0])
    return quick(total, error + (a[1] + b[1]))


def neg(a):
    return (-a[0], -a[1])


def mul(a, b):
    value, error = two_product(a[0], b[0])
    return quick(value, error + (a[0] * b[1] + a[1] * b[0]))


def div(a, b):
    first = a[0] / b[0]
    zero = jnp.zeros_like(first)
    rest = add(a, neg(mul(b, (first, zero))))
    second = rest[0] / b[0]
    rest = add(rest, neg(mul(b, (second, zero))))
    third = rest[0] / b[0]
    return add(quick(first, second), (third, zero))


def c_add(a, b):
    return (add(a[0], b[0]), add(a[1], b[1]))


def c_neg(a):
    return (neg(a[0]), neg(a[1]))


def c_conj(a):
    return (a[0], neg(a[1]))


def c_mul(a, b):
    return (
        add(mul(a[0], b[0]), neg(mul(a[1], b[1]))),
        add(mul(a[0], b[1]), mul(a[1], b[0])),
    )


def c_div(a, b):
    top = c_mul(a, c_conj(b))
    bottom = add(mul(b[0], b[0]), mul(b[1], b[1]))
    return (div(top[0], bottom), div(top[1], bottom))


def c_over(a, real):
    return (div(a[0], real), div(a[1], real))


def total_of(values):
    result = values[0]
    for value in values[1:]:
        result = c_add(result, value)
    return result


def coefficients(gram):
    rho = gram[0, 0]
    alpha = c_div(rho, gram[0, 1])
    one_half = c_neg(alpha)

    def form(coeffs, left, right):
        rows = []
        for i, factor in enumerate(coeffs):
            inner = total_of(
                [
                    gram[i + left, j + right]
                    if other is None
                    else c_mul(gram[i + left, j + right], other)
                    for j, other in enumerate(coeffs)
                ]
            )
            rows.append(inner if factor is None else c_mul(c_conj(factor), inner))
        return total_of(rows)

    omega = c_over(form([None, one_half], 1, 0), form([None, one_half], 1, 1)[0])
    res1 = c_neg(c_add(alpha, omega))
    res2 = c_mul(alpha, omega)
    new_rho = total_of([gram[0, 0], c_mul(gram[0, 1], res1), c_mul(gram[0, 2], res2)])
    mix = c_mul(c_div(new_rho, rho), c_div(alpha, omega))
    dir0 = (add((jnp.ones_like(mix[0][0]), jnp.zeros_like(mix[0][0])), mix[0]), mix[1])
    dir1 = c_add(res1, c_neg(c_mul(mix, omega)))
    dir2 = res2
    along = total_of(
        [c_mul(gram[0, 1], dir0), c_mul(gram[0, 2], dir1), c_mul(gram[0, 3], dir2)]
    )
    alpha2 = c_div(new_rho, along)
    half1 = c_add(res1, c_neg(c_mul(alpha2, dir0)))
    half2 = c_add(res2, c_neg(c_mul(alpha2, dir1)))
    half3 = c_neg(c_mul(alpha2, dir2))
    half = [None, half1, half2, half3]
    omega2 = c_over(form(half, 1, 0), form(half, 1, 1)[0])
    out0 = total_of([alpha, omega, c_mul(alpha2, dir0), omega2])
    out1 = total_of([c_mul(omega, one_half), c_mul(alpha2, dir1), c_mul(omega2, half1)])
    out2 = c_add(c_mul(alpha2, dir2), c_mul(omega2, half2))
    out3 = c_mul(omega2, half3)
    return [(c[0][0], c[1][0]) for c in (out0, out1, out2, out3)]


def update_kernel(sizes, rows_ref, start_ref, basis_ref, out_ref):
    depths, lats, pieces = sizes
    high = jnp.zeros((ROWS, LANES), jnp.float32)
    low = high
    for number in range(pieces * lats // ROWS):
        high, error = two_sum(high, rows_ref[number * ROWS : (number + 1) * ROWS])
        low = low + error
    for shift in (4, 2, 1):
        high, error = two_sum(high, pltpu.roll(high, shift, 0))
        low = low + pltpu.roll(low, shift, 0) + error
    high, low = quick(high, low + pltpu.roll(high, 64, 1))

    def entry(number):
        return (
            jnp.broadcast_to(high[:, number : number + 1], (ROWS, LANES)),
            jnp.broadcast_to(low[:, number : number + 1], (ROWS, LANES)),
        )

    zero = jnp.zeros((ROWS, LANES), jnp.float32)
    gram = {}
    at = 0
    for i, j in PAIRS:
        real = entry(at)
        at += 1
        if i == j:
            gram[i, i] = (real, (zero, zero))
        else:
            gram[i, j] = (real, entry(at))
            gram[j, i] = c_conj(gram[i, j])
            at += 1
    factors = coefficients(gram)

    def layer(source, carry):
        for component in range(3):
            for z in range(2):
                real = start_ref[source, slot(0, component, z)]
                imag = start_ref[source, slot(1, component, z)]
                for b, (fr, fi) in enumerate(factors):
                    br = basis_ref[b, source, slot(0, component, z)]
                    bi = basis_ref[b, source, slot(1, component, z)]
                    real = real + (fr * br - fi * bi)
                    imag = imag + (fr * bi + fi * br)
                out_ref[source, slot(0, component, z)] = real
                out_ref[source, slot(1, component, z)] = imag
        return carry

    lax.fori_loop(0, depths, layer, 0)


def output_kernel(pieces, in_ref, field_ref, term_ref):
    for piece in range(pieces):
        cols = slice(piece * LANES, (piece + 1) * LANES)
        for z in range(2):
            term = None
            for component in range(3):
                values = []
                for kind in range(KINDS):
                    for part in range(2):
                        value = in_ref[kind * pieces + piece, slot(part, component, z)]
                        field_ref[kind * 12 + slot(part, component, z), :, cols] = value
                        values.append(value)
                product = values[0] * values[2] - values[1] * values[3]
                term = product if term is None else term + product
            term_ref[piece, z] = term


def local(conductivity, field_guess, tx_cell, rx_cell, rx_weight):
    pieces, lats = lax.axis_size("piece"), lax.axis_size("lat")
    depths = KINDS * pieces
    sizes = (depths, lats, pieces)
    width = conductivity.shape[2]
    layers = 2 * depths
    f32 = jnp.float32
    params = pltpu.CompilerParams

    packed = pl.pallas_call(
        functools.partial(pack_kernel, pieces),
        out_shape=jax.ShapeDtypeStruct((depths, 16, ROWS, LANES), f32),
        in_specs=[in_vmem()] * 2,
        out_specs=in_vmem(),
        compiler_params=params(vmem_limit_bytes=4 * MIB),
    )(field_guess.reshape(24, ROWS, width), conductivity)
    mid = lax.all_to_all(packed, DEPTH, 0, 0)
    border = [(i, i + 1) for i in range(1, lats - 1, 2)]
    near_outer, near_inner = pl.pallas_call(
        functools.partial(border_kernel, depths),
        out_shape=(jax.ShapeDtypeStruct((depths, NEAR_TILES, ROWS, LANES), f32),) * 2,
        in_specs=[in_vmem()],
        out_specs=(in_vmem(), in_vmem()),
        compiler_params=params(vmem_limit_bytes=4 * MIB),
    )(mid)
    border = [(i, i + 1) for i in range(1, lats - 1, 2)]
    inner = lax.ppermute(near_inner, "lat", [(i, i ^ 1) for i in range(lats)])
    outer = lax.ppermute(near_outer, "lat", border + [(b, a) for a, b in border])

    edges, sources = pl.pallas_call(
        functools.partial(early_kernel, sizes),
        out_shape=(
            jax.ShapeDtypeStruct((7, 2 * depths, ROWS, LANES), f32),
            jax.ShapeDtypeStruct((2, 2 * depths, 2 * ROWS, 2 * LANES), f32),
        ),
        in_specs=[in_smem()] * 3 + [in_vmem()],
        out_specs=(in_vmem(), in_vmem()),
        compiler_params=params(vmem_limit_bytes=8 * MIB),
    )(tx_cell, rx_cell, rx_weight.reshape(1, -1), mid)
    basis, rows = pl.pallas_call(
        functools.partial(basis_kernel, sizes),
        out_shape=(
            jax.ShapeDtypeStruct((BASIS - 1, depths, 12, ROWS, LANES), f32),
            jax.ShapeDtypeStruct((pieces * lats, LANES), f32),
        ),
        in_specs=[in_vmem()] * 5,
        out_specs=(in_vmem(), in_vmem()),
        scratch_shapes=basis_scratch(depths),
        compiler_params=params(vmem_limit_bytes=28 * MIB),
    )(edges, sources, outer, mid, inner)

    rows = lax.all_to_all(rows, ("piece", "lat"), 0, 0)
    moved = pl.pallas_call(
        functools.partial(update_kernel, sizes),
        out_shape=jax.ShapeDtypeStruct((depths, 12, ROWS, LANES), f32),
        in_specs=[in_vmem()] * 3,
        out_specs=in_vmem(),
        compiler_params=params(vmem_limit_bytes=8 * MIB),
    )(rows, mid, basis)
    moved = lax.all_to_all(moved, DEPTH, 0, 0)
    fields, terms = pl.pallas_call(
        functools.partial(output_kernel, pieces),
        out_shape=(
            jax.ShapeDtypeStruct((24, ROWS, width), f32),
            jax.ShapeDtypeStruct((pieces, 2, ROWS, LANES), f32),
        ),
        in_specs=[in_vmem()],
        out_specs=(in_vmem(), in_vmem()),
        compiler_params=params(vmem_limit_bytes=4 * MIB),
    )(moved)
    gradient = jnp.sum(lax.all_to_all(terms, "tx", 0, 0), axis=0)
    return (fields.reshape(field_guess.shape), gradient)


def solution(mesh):
    grid = mesh.devices
    split = Mesh(
        grid.reshape((KINDS, grid.shape[0] // KINDS) + grid.shape[1:]),
        DEPTH + tuple(mesh.axis_names[1:]),
    )
    return jax.shard_map(
        local,
        mesh=split,
        in_specs=(
            P(DEPTH, "lat", None),
            P("tx", None, None, None, DEPTH, "lat", None),
            P("tx"),
            P("tx", None),
            P("tx", None, None),
        ),
        out_specs=(P("tx", None, None, None, DEPTH, "lat", None), P(DEPTH, "lat", "tx")),
        check_vma=False,
    )
```

```python
import functools

import jax
import jax.numpy as jnp
from jax import lax
from jax.experimental import pallas as pl
from jax.experimental.pallas import tpu as pltpu
from jax.sharding import Mesh
from jax.sharding import PartitionSpec as P

SOURCE = 20.0
KINDS = 2
BASIS = 5
ROWS = 8
LANES = 128
DEPTH = ("kind", "piece")
PAIRS = [(i, j) for i in range(BASIS) for j in range(i, BASIS)]
ENTRIES = [(i, j, part) for i, j in PAIRS for part in range(1 if i == j else 2)]
MIB = 1 << 20
TILES = 16
NEAR = 5
NEAR_TILES = TILES * NEAR // ROWS


def in_vmem():
    return pl.BlockSpec(memory_space=pltpu.VMEM)


def in_smem():
    return pl.BlockSpec(memory_space=pltpu.SMEM)


def slot(part, component, layer):
    return (part * 3 + component) * 2 + layer


def pack_kernel(pieces, guess_ref, cond_ref, out_ref):
    lane = lax.broadcasted_iota(jnp.int32, (ROWS, LANES), 1)
    blank = jnp.zeros((ROWS, LANES), jnp.float32)
    for kind in range(KINDS):
        for piece in range(pieces):
            to = kind * pieces + piece
            edges = [blank, blank]
            for item in range(14):

                def tile(number):
                    if number < 0 or number >= pieces:
                        return blank
                    cols = slice(number * LANES, (number + 1) * LANES)
                    if item < 12:
                        return guess_ref[kind * 12 + item, :, cols]
                    return cond_ref[item - 12, :, cols]

                out_ref[to, item] = tile(piece)
                ends = jnp.where(lane >= LANES // 2, tile(piece - 1), tile(piece + 1))
                place = item % 8
                moved = pltpu.roll(ends, (16 * place + 8) % LANES, 1)
                edges[item // 8] = jnp.where(lane // 16 == place, moved, edges[item // 8])
            out_ref[to, 14] = edges[0]
            out_ref[to, 15] = edges[1]


def two_sum(a, b):
    total = a + b
    other = total - a
    return total, (a - (total - other)) + (b - other)


def gather(read, moves, sub):
    found = {}
    for tile, row, to in moves:
        found.setdefault((tile, (to - row) % ROWS), []).append(to)
    result = jnp.zeros((ROWS, LANES), jnp.float32)
    for (tile, shift), rows in found.items():
        value = pltpu.roll(read(tile), shift, 0) if shift else read(tile)
        result = jnp.where((sub >= min(rows)) & (sub <= max(rows)), value, result)
    return result


def border_kernel(depths, mid_ref, outer_ref, inner_ref):
    sub = lax.broadcasted_iota(jnp.int32, (ROWS, LANES), 0)
    first_core = lax.axis_index("lat") % 2 == 0

    def each(source, carry):
        for number in range(NEAR_TILES):
            ends = []
            for first in (0, ROWS - NEAR):
                places = [divmod(number * ROWS + to, NEAR) for to in range(ROWS)]
                moves = [(tile, first + row, to) for to, (tile, row) in enumerate(places)]
                ends.append(gather(lambda n: mid_ref[source, n], moves, sub))
            outer_ref[source, number] = jnp.where(first_core, ends[0], ends[1])
            inner_ref[source, number] = jnp.where(first_core, ends[1], ends[0])
        return carry

    lax.fori_loop(0, depths, each, 0, unroll=2)


def edge_columns(packs, item, lane):
    edge = pltpu.roll(packs[item // 8], LANES - (16 * (item % 8) + 8), 1)
    return jnp.where((lane < 8) | (lane >= LANES - 8), edge, 0.0)


def early_kernel(sizes, tx_ref, rx_ref, weight_ref, mid_ref, edge_ref, source_ref):
    depths, lats, pieces = sizes
    span = 2 * LANES
    width = pieces * LANES
    lat_index = lax.axis_index("lat")
    kind = lax.axis_index("kind")
    piece = lax.axis_index("piece")
    lane = lax.broadcasted_iota(jnp.int32, (ROWS, LANES), 1)

    def spread(source, carry):
        packs = [mid_ref[source, 14], mid_ref[source, 15]]
        for item in range(14):
            edge_ref[item // 2, 2 * source + item % 2] = edge_columns(packs, item, lane)
        return carry

    lax.fori_loop(0, depths, spread, 0, unroll=2)

    for z in range(2 * depths):
        for part in range(2):
            source_ref[part, z] = jnp.zeros((2 * ROWS, span), jnp.float32)
    line = lax.broadcasted_iota(jnp.int32, (1, span), 1)

    def place_of(cell):
        col = (cell & (width - 1)) - piece * LANES
        rest = lax.shift_right_logical(cell, width.bit_length() - 1)
        row = (rest & (lats * ROWS - 1)) - lat_index * ROWS
        z = lax.shift_right_logical(rest, (lats * ROWS).bit_length() - 1)
        return (row >= -4) & (row < 12) & (col >= -8) & (col < LANES + 8), z, row, col

    def add_source(cell, real, imag):
        held, z, row, col = place_of(cell)

        @pl.when(held)
        def _():
            hit = line == (col & (span - 1))
            at = pl.ds(row & (2 * ROWS - 1), 1)
            source_ref[0, z, at] = source_ref[0, z, at] + jnp.where(hit, real, 0.0)
            source_ref[1, z, at] = source_ref[1, z, at] + jnp.where(hit, imag, 0.0)

    @pl.when(kind == 0)
    def _():
        add_source(tx_ref[0], jnp.float32(0.0), jnp.float32(-SOURCE))

    @pl.when(kind == 1)
    def _():
        def each(group, carry):
            numbers = [8 * group + n for n in range(8)]
            some = place_of(rx_ref[0, numbers[0]])[0]
            for r in numbers[1:]:
                some = some | place_of(rx_ref[0, r])[0]

            @pl.when(some)
            def _():
                for r in numbers:
                    add_source(rx_ref[0, r], weight_ref[0, 2 * r], weight_ref[0, 2 * r + 1])

            return carry

        lax.fori_loop(0, rx_ref.shape[1] // 8, each, 0)


def basis_scratch(depths):
    layers = 2 * depths
    f32 = jnp.float32
    return [
        pltpu.VMEM((BASIS, 6, layers + 1, 2 * ROWS, 2 * LANES), f32),
        pltpu.VMEM((7, layers, 2 * ROWS, 2 * LANES), f32),
        pltpu.VMEM((4, 3 * ROWS, 2 * LANES), f32),
        pltpu.VMEM((4, 2 * ROWS, 2 * LANES), f32),
        pltpu.VMEM((layers, 2 * ROWS, 2 * LANES), f32),
        pltpu.VMEM((3 * ROWS, 2 * LANES), f32),
        pltpu.VMEM((2 * ROWS, 2 * LANES), f32),
        pltpu.VMEM((2 * len(ENTRIES), ROWS, LANES), f32),
    ]


def basis_kernel(
    sizes, edge_ref, source_ref, outer_ref, mid_ref, inner_ref, basis_ref, gram_ref,
    field, sides, curl_start, curl, cond, inside_start, inside, acc,
):
    depths, lats, pieces = sizes
    layers = 2 * depths
    span = 2 * LANES
    width = pieces * LANES
    lat_index = lax.axis_index("lat")
    kind = lax.axis_index("kind")
    piece = lax.axis_index("piece")
    lane = lax.broadcasted_iota(jnp.int32, (ROWS, LANES), 1)
    blank = jnp.zeros((ROWS, LANES), jnp.float32)

    def within(rows, row):
        lane_w = lax.broadcasted_iota(jnp.int32, (rows, span), 1)
        x_at = lat_index * ROWS + row
        y_at = piece * LANES + jnp.where(lane_w >= LANES + 64, lane_w - span, lane_w)
        good = (x_at >= 0) & (x_at < lats * ROWS) & (y_at >= 0) & (y_at < width)
        return jnp.where(good, 1.0, 0.0)

    row_s = lax.broadcasted_iota(jnp.int32, (3 * ROWS, span), 0)
    inside_start[...] = within(3 * ROWS, row_s - ROWS)
    row_b = lax.broadcasted_iota(jnp.int32, (2 * ROWS, span), 0)
    inside[...] = within(2 * ROWS, jnp.where(row_b >= 12, row_b - 16, row_b))

    first_core = lat_index % 2 == 0

    sub = lax.broadcasted_iota(jnp.int32, (ROWS, LANES), 0)

    def spread(source, carry):
        tiles = [], []
        for number in range(NEAR_TILES):
            outer, inner = outer_ref[source, number], inner_ref[source, number]
            tiles[0].append(jnp.where(first_core, outer, inner))
            tiles[1].append(jnp.where(first_core, inner, outer))
        for number, first in enumerate((ROWS - NEAR, 0)):
            found = []
            for item in range(TILES):
                places = [divmod(item * NEAR + row, ROWS) for row in range(NEAR)]
                moves = [(tile, at, first + row) for row, (tile, at) in enumerate(places)]
                found.append(gather(lambda n: tiles[number][n], moves, sub))
            for item in range(14):
                rows = slice(number * ROWS, (number + 1) * ROWS)
                at = (item // 2, 2 * source + item % 2, rows)
                sides[at + (slice(0, LANES),)] = found[item]
                sides[at + (slice(LANES, span),)] = edge_columns(found[14:], item, lane)
        return carry

    lax.fori_loop(0, depths, spread, 0, unroll=4)

    empty = jnp.zeros((2 * ROWS, span), jnp.float32)
    for number in range(BASIS - 1):
        for component in range(6):
            field[number, component, layers] = empty

    def ahead(values, axis):
        return pltpu.roll(values, values.shape[axis] - 1, axis) - values

    def behind(values, axis):
        return values - pltpu.roll(values, 1, axis)

    def curl_ahead(here, above, keep):
        uz, ux, uy = here
        hz = (ahead(uy, 0) - ahead(ux, 1)) * keep
        hx = (ahead(uz, 1) - (above[1] - uy)) * keep
        hy = ((above[0] - ux) - ahead(uz, 0)) * keep
        return hz, hx, hy

    def curl_behind(h, below):
        hz, hx, hy = h
        return (
            behind(hy, 0) - behind(hx, 1),
            behind(hz, 1) - (hy - below[1]),
            (hx - below[0]) - behind(hz, 0),
        )

    def start_tile(number, z, source, layer):
        own = jnp.concatenate([mid_ref[source, 2 * number + layer], edge_ref[number, z]], axis=1)
        left, right = sides[number, z, :ROWS], sides[number, z, ROWS:]
        return jnp.concatenate([left, own, right], axis=0)

    def merge(values):
        sub = lax.broadcasted_iota(jnp.int32, (ROWS, span), 0)
        sides = jnp.where(sub < 4, values[2 * ROWS :], values[:ROWS])
        return jnp.concatenate([values[ROWS : 2 * ROWS], sides], axis=0)

    for number in range(4):
        curl_start[number] = jnp.zeros((3 * ROWS, span), jnp.float32)

    def start_layers(source, carry):
        keep = inside_start[...]
        below = [[curl_start[0], curl_start[1]], [curl_start[2], curl_start[3]]]
        for layer in range(2):
            z = 2 * source + layer
            tiles = [start_tile(c, z, source, layer) for c in range(6)]
            sigma = start_tile(6, z, source, layer)
            cond[z] = merge(sigma)
            for part in range(2):
                here = tiles[3 * part : 3 * part + 3]
                if layer == 0:
                    above = [start_tile(3 * part + c, z + 1, source, 1) for c in (1, 2)]
                else:
                    last = source == depths - 1
                    after = jnp.minimum(source + 1, depths - 1)
                    above = [
                        jnp.where(last, 0.0, start_tile(3 * part + c, 2 * after, after, 0))
                        for c in (1, 2)
                    ]
                h = curl_ahead(here, above, keep)
                outs = curl_behind(h, below[part])
                below[part] = [h[1], h[2]]
                for component, value in enumerate(outs):
                    other = sigma * tiles[3 * (1 - part) + component]
                    value = other - value if part == 0 else -value - other
                    value = merge(value) * inside[...]
                    if component == 0:
                        value = value + source_ref[part, z]
                    field[0, 3 * part + component, z] = value
        for number in range(4):
            curl_start[number] = below[number // 2][number % 2]
        return carry

    lax.fori_loop(0, depths, start_layers, 0)

    for step in range(BASIS - 1):
        for number in range(4):
            curl[number] = empty

        def apply_layers(source, carry, step=step):
            keep = inside[...]
            below = [[curl[0], curl[1]], [curl[2], curl[3]]]
            for layer in range(2):
                z = 2 * source + layer
                sigma = cond[z]
                for part in range(2):
                    here = [field[step, 3 * part + c, z] for c in range(3)]
                    above = [field[step, 3 * part + c, z + 1] for c in (1, 2)]
                    h = curl_ahead(here, above, keep)
                    outs = curl_behind(h, below[part])
                    below[part] = [h[1], h[2]]
                    for component, value in enumerate(outs):
                        if step == BASIS - 2:
                            mine = (slice(0, ROWS), slice(0, LANES))
                        else:
                            mine = (slice(None), slice(None))
                        near = field[(step, 3 * (1 - part) + component, z) + mine]
                        other = sigma[mine] * near
                        value = value[mine]
                        value = value - other if part == 0 else value + other
                        if step < BASIS - 2:
                            value = value * keep
                        field[(step + 1, 3 * part + component, z) + mine] = value
            for number in range(4):
                curl[number] = below[number // 2][number % 2]
            return carry

        lax.fori_loop(0, depths, apply_layers, 0, unroll=2)

    for entry in range(2 * len(ENTRIES)):
        acc[entry] = blank

    def gram_layers(source, carry):
        tiles = []
        for b in range(BASIS):
            group = []
            for component in range(6):
                for layer in range(2):
                    tile = field[b, component, 2 * source + layer, 0:ROWS, 0:LANES]
                    group.append(tile)
                    if b < BASIS - 1:
                        basis_ref[b, source, 2 * component + layer] = tile
            tiles.append(group)
        for entry, (i, j, part) in enumerate(ENTRIES):
            first, second = tiles[i], tiles[j]
            if part:
                terms = [first[n] * second[n + 6] - first[n + 6] * second[n] for n in range(6)]
            else:
                terms = [first[n] * second[n] + first[n + 6] * second[n + 6] for n in range(6)]
            value = (terms[0] + terms[1]) + (terms[2] + terms[3]) + (terms[4] + terms[5])
            total, error = two_sum(acc[2 * entry], value)
            acc[2 * entry] = total
            acc[2 * entry + 1] = acc[2 * entry + 1] + error
        return carry

    lax.fori_loop(0, depths, gram_layers, 0, unroll=2)

    def fold(high, low, shift, axis):
        total, error = two_sum(high, pltpu.roll(high, shift, axis))
        return total, low + pltpu.roll(low, shift, axis) + error

    sub = lax.broadcasted_iota(jnp.int32, (ROWS, LANES), 0)
    row = blank
    for start in range(0, len(ENTRIES), 8):
        highs, lows = blank, blank
        for entry in range(start, min(start + 8, len(ENTRIES))):
            high, low = acc[2 * entry], acc[2 * entry + 1]
            for shift in (4, 2, 1):
                high, low = fold(high, low, shift, 0)
            highs = jnp.where(sub == entry - start, high, highs)
            lows = jnp.where(sub == entry - start, low, lows)
        for shift in (64, 32, 16, 8, 4, 2, 1):
            highs, lows = fold(highs, lows, shift, 1)
        row = jnp.where(lane == sub + start, highs, row)
        row = jnp.where(lane == sub + start + 64, lows, row)
    for shift in (4, 2, 1):
        row = row + pltpu.roll(row, shift, 0)
    for number in range(pieces * lats // ROWS):
        gram_ref[number * ROWS : (number + 1) * ROWS] = row


def quick(a, b):
    total = a + b
    return total, b - (total - a)


def split(a):
    big = a * 4097.0
    high = big - (big - a)
    return high, a - high


def two_product(a, b):
    value = a * b
    ah, al = split(a)
    bh, bl = split(b)
    return value, ((ah * bh - value) + ah * bl + al * bh) + al * bl


def add(a, b):
    total, error = two_sum(a[0], b[0])
    return quick(total, error + (a[1] + b[1]))


def neg(a):
    return (-a[0], -a[1])


def mul(a, b):
    value, error = two_product(a[0], b[0])
    return quick(value, error + (a[0] * b[1] + a[1] * b[0]))


def div(a, b):
    first = a[0] / b[0]
    zero = jnp.zeros_like(first)
    rest = add(a, neg(mul(b, (first, zero))))
    second = rest[0] / b[0]
    rest = add(rest, neg(mul(b, (second, zero))))
    third = rest[0] / b[0]
    return add(quick(first, second), (third, zero))


def c_add(a, b):
    return (add(a[0], b[0]), add(a[1], b[1]))


def c_neg(a):
    return (neg(a[0]), neg(a[1]))


def c_conj(a):
    return (a[0], neg(a[1]))


def c_mul(a, b):
    return (
        add(mul(a[0], b[0]), neg(mul(a[1], b[1]))),
        add(mul(a[0], b[1]), mul(a[1], b[0])),
    )


def c_div(a, b):
    top = c_mul(a, c_conj(b))
    bottom = add(mul(b[0], b[0]), mul(b[1], b[1]))
    return (div(top[0], bottom), div(top[1], bottom))


def c_over(a, real):
    return (div(a[0], real), div(a[1], real))


def total_of(values):
    result = values[0]
    for value in values[1:]:
        result = c_add(result, value)
    return result


def coefficients(gram):
    rho = gram[0, 0]
    alpha = c_div(rho, gram[0, 1])
    one_half = c_neg(alpha)

    def form(coeffs, left, right):
        rows = []
        for i, factor in enumerate(coeffs):
            inner = total_of(
                [
                    gram[i + left, j + right]
                    if other is None
                    else c_mul(gram[i + left, j + right], other)
                    for j, other in enumerate(coeffs)
                ]
            )
            rows.append(inner if factor is None else c_mul(c_conj(factor), inner))
        return total_of(rows)

    omega = c_over(form([None, one_half], 1, 0), form([None, one_half], 1, 1)[0])
    res1 = c_neg(c_add(alpha, omega))
    res2 = c_mul(alpha, omega)
    new_rho = total_of([gram[0, 0], c_mul(gram[0, 1], res1), c_mul(gram[0, 2], res2)])
    mix = c_mul(c_over(new_rho, rho[0]), c_div(alpha, omega))
    dir0 = (add((jnp.ones_like(mix[0][0]), jnp.zeros_like(mix[0][0])), mix[0]), mix[1])
    dir1 = c_add(res1, c_neg(c_mul(mix, omega)))
    dir2 = res2
    along = total_of(
        [c_mul(gram[0, 1], dir0), c_mul(gram[0, 2], dir1), c_mul(gram[0, 3], dir2)]
    )
    alpha2 = c_div(new_rho, along)
    half1 = c_add(res1, c_neg(c_mul(alpha2, dir0)))
    half2 = c_add(res2, c_neg(c_mul(alpha2, dir1)))
    half3 = c_neg(c_mul(alpha2, dir2))
    half = [None, half1, half2, half3]
    omega2 = c_over(form(half, 1, 0), form(half, 1, 1)[0])
    out0 = total_of([alpha, omega, c_mul(alpha2, dir0), omega2])
    out1 = total_of([c_mul(omega, one_half), c_mul(alpha2, dir1), c_mul(omega2, half1)])
    out2 = c_add(c_mul(alpha2, dir2), c_mul(omega2, half2))
    out3 = c_mul(omega2, half3)
    return [(c[0][0], c[1][0]) for c in (out0, out1, out2, out3)]


def update_kernel(sizes, rows_ref, start_ref, basis_ref, out_ref):
    depths, lats, pieces = sizes
    high = jnp.zeros((ROWS, LANES), jnp.float32)
    low = high
    for number in range(pieces * lats // ROWS):
        high, error = two_sum(high, rows_ref[number * ROWS : (number + 1) * ROWS])
        low = low + error
    for shift in (4, 2, 1):
        high, error = two_sum(high, pltpu.roll(high, shift, 0))
        low = low + pltpu.roll(low, shift, 0) + error
    high, low = quick(high, low + pltpu.roll(high, 64, 1))

    def entry(number):
        return (
            jnp.broadcast_to(high[:, number : number + 1], (ROWS, LANES)),
            jnp.broadcast_to(low[:, number : number + 1], (ROWS, LANES)),
        )

    zero = jnp.zeros((ROWS, LANES), jnp.float32)
    gram = {}
    at = 0
    for i, j in PAIRS:
        real = entry(at)
        at += 1
        if i == j:
            gram[i, i] = (real, (zero, zero))
        else:
            gram[i, j] = (real, entry(at))
            gram[j, i] = c_conj(gram[i, j])
            at += 1
    factors = coefficients(gram)

    def layer(source, carry):
        for component in range(3):
            for z in range(2):
                real = start_ref[source, slot(0, component, z)]
                imag = start_ref[source, slot(1, component, z)]
                for b, (fr, fi) in enumerate(factors):
                    br = basis_ref[b, source, slot(0, component, z)]
                    bi = basis_ref[b, source, slot(1, component, z)]
                    real = real + (fr * br - fi * bi)
                    imag = imag + (fr * bi + fi * br)
                out_ref[source, slot(0, component, z)] = real
                out_ref[source, slot(1, component, z)] = imag
        return carry

    lax.fori_loop(0, depths, layer, 0, unroll=2)


def output_kernel(pieces, in_ref, field_ref, term_ref):
    for piece in range(pieces):
        cols = slice(piece * LANES, (piece + 1) * LANES)
        for z in range(2):
            term = None
            for component in range(3):
                values = []
                for kind in range(KINDS):
                    for part in range(2):
                        value = in_ref[kind * pieces + piece, slot(part, component, z)]
                        field_ref[kind * 12 + slot(part, component, z), :, cols] = value
                        values.append(value)
                product = values[0] * values[2] - values[1] * values[3]
                term = product if term is None else term + product
            term_ref[piece, z] = term


def local(conductivity, field_guess, tx_cell, rx_cell, rx_weight):
    pieces, lats = lax.axis_size("piece"), lax.axis_size("lat")
    depths = KINDS * pieces
    sizes = (depths, lats, pieces)
    width = conductivity.shape[2]
    layers = 2 * depths
    f32 = jnp.float32
    params = pltpu.CompilerParams

    packed = pl.pallas_call(
        functools.partial(pack_kernel, pieces),
        out_shape=jax.ShapeDtypeStruct((depths, 16, ROWS, LANES), f32),
        in_specs=[in_vmem()] * 2,
        out_specs=in_vmem(),
        compiler_params=params(vmem_limit_bytes=4 * MIB),
    )(field_guess.reshape(24, ROWS, width), conductivity)
    mid = lax.all_to_all(packed, DEPTH, 0, 0)
    border = [(i, i + 1) for i in range(1, lats - 1, 2)]
    near_outer, near_inner = pl.pallas_call(
        functools.partial(border_kernel, depths),
        out_shape=(jax.ShapeDtypeStruct((depths, NEAR_TILES, ROWS, LANES), f32),) * 2,
        in_specs=[in_vmem()],
        out_specs=(in_vmem(), in_vmem()),
        compiler_params=params(vmem_limit_bytes=4 * MIB),
    )(mid)
    border = [(i, i + 1) for i in range(1, lats - 1, 2)]
    inner = lax.ppermute(near_inner, "lat", [(i, i ^ 1) for i in range(lats)])
    outer = lax.ppermute(near_outer, "lat", border + [(b, a) for a, b in border])

    edges, sources = pl.pallas_call(
        functools.partial(early_kernel, sizes),
        out_shape=(
            jax.ShapeDtypeStruct((7, 2 * depths, ROWS, LANES), f32),
            jax.ShapeDtypeStruct((2, 2 * depths, 2 * ROWS, 2 * LANES), f32),
        ),
        in_specs=[in_smem()] * 3 + [in_vmem()],
        out_specs=(in_vmem(), in_vmem()),
        compiler_params=params(vmem_limit_bytes=8 * MIB),
    )(tx_cell, rx_cell, rx_weight.reshape(1, -1), mid)
    basis, rows = pl.pallas_call(
        functools.partial(basis_kernel, sizes),
        out_shape=(
            jax.ShapeDtypeStruct((BASIS - 1, depths, 12, ROWS, LANES), f32),
            jax.ShapeDtypeStruct((pieces * lats, LANES), f32),
        ),
        in_specs=[in_vmem()] * 5,
        out_specs=(in_vmem(), in_vmem()),
        scratch_shapes=basis_scratch(depths),
        compiler_params=params(vmem_limit_bytes=28 * MIB),
    )(edges, sources, outer, mid, inner)

    rows = lax.all_to_all(rows, ("piece", "lat"), 0, 0)
    moved = pl.pallas_call(
        functools.partial(update_kernel, sizes),
        out_shape=jax.ShapeDtypeStruct((depths, 12, ROWS, LANES), f32),
        in_specs=[in_vmem()] * 3,
        out_specs=in_vmem(),
        compiler_params=params(vmem_limit_bytes=8 * MIB),
    )(rows, mid, basis)
    moved = lax.all_to_all(moved, DEPTH, 0, 0)
    fields, terms = pl.pallas_call(
        functools.partial(output_kernel, pieces),
        out_shape=(
            jax.ShapeDtypeStruct((24, ROWS, width), f32),
            jax.ShapeDtypeStruct((pieces, 2, ROWS, LANES), f32),
        ),
        in_specs=[in_vmem()],
        out_specs=(in_vmem(), in_vmem()),
        compiler_params=params(vmem_limit_bytes=4 * MIB),
    )(moved)
    gradient = jnp.sum(lax.all_to_all(terms, "tx", 0, 0), axis=0)
    return (fields.reshape(field_guess.shape), gradient)


def solution(mesh):
    grid = mesh.devices
    split = Mesh(
        grid.reshape((KINDS, grid.shape[0] // KINDS) + grid.shape[1:]),
        DEPTH + tuple(mesh.axis_names[1:]),
    )
    return jax.shard_map(
        local,
        mesh=split,
        in_specs=(
            P(DEPTH, "lat", None),
            P("tx", None, None, None, DEPTH, "lat", None),
            P("tx"),
            P("tx", None),
            P("tx", None, None),
        ),
        out_specs=(P("tx", None, None, None, DEPTH, "lat", None), P(DEPTH, "lat", "tx")),
        check_vma=False,
    )
```

```python
import functools

import jax
import jax.numpy as jnp
from jax import lax
from jax.experimental import pallas as pl
from jax.experimental.pallas import tpu as pltpu
from jax.sharding import Mesh
from jax.sharding import PartitionSpec as P

SOURCE = 20.0
KINDS = 2
BASIS = 5
ROWS = 8
LANES = 128
DEPTH = ("kind", "piece")
PAIRS = [(i, j) for i in range(BASIS) for j in range(i, BASIS)]
ENTRIES = [(i, j, part) for i, j in PAIRS for part in range(1 if i == j else 2)]
MIB = 1 << 20
TILES = 16
NEAR = 5
NEAR_TILES = TILES * NEAR // ROWS


def in_vmem():
    return pl.BlockSpec(memory_space=pltpu.VMEM)


def in_smem():
    return pl.BlockSpec(memory_space=pltpu.SMEM)


def slot(part, component, layer):
    return (part * 3 + component) * 2 + layer


def pack_kernel(pieces, guess_hbm, cond_hbm, out_ref, guess_ref, cond_ref, arrived):
    copies = [
        pltpu.make_async_copy(
            guess_hbm.at[pl.ds(kind * 12, 12)], guess_ref.at[pl.ds(kind * 12, 12)], arrived.at[kind]
        )
        for kind in range(KINDS)
    ]
    copies.append(pltpu.make_async_copy(cond_hbm, cond_ref, arrived.at[KINDS]))
    for copy in copies:
        copy.start()
    copies[KINDS].wait()
    lane = lax.broadcasted_iota(jnp.int32, (ROWS, LANES), 1)
    blank = jnp.zeros((ROWS, LANES), jnp.float32)
    for kind in range(KINDS):
        copies[kind].wait()
        for piece in range(pieces):
            to = kind * pieces + piece
            edges = [blank, blank]
            for item in range(14):

                def tile(number):
                    if number < 0 or number >= pieces:
                        return blank
                    cols = slice(number * LANES, (number + 1) * LANES)
                    if item < 12:
                        return guess_ref[kind * 12 + item, :, cols]
                    return cond_ref[item - 12, :, cols]

                out_ref[to, item] = tile(piece)
                ends = jnp.where(lane >= LANES // 2, tile(piece - 1), tile(piece + 1))
                place = item % 8
                moved = pltpu.roll(ends, (16 * place + 8) % LANES, 1)
                edges[item // 8] = jnp.where(lane // 16 == place, moved, edges[item // 8])
            out_ref[to, 14] = edges[0]
            out_ref[to, 15] = edges[1]


def two_sum(a, b):
    total = a + b
    other = total - a
    return total, (a - (total - other)) + (b - other)


def gather(read, moves, sub):
    found = {}
    for tile, row, to in moves:
        found.setdefault((tile, (to - row) % ROWS), []).append(to)
    result = jnp.zeros((ROWS, LANES), jnp.float32)
    for (tile, shift), rows in found.items():
        value = pltpu.roll(read(tile), shift, 0) if shift else read(tile)
        result = jnp.where((sub >= min(rows)) & (sub <= max(rows)), value, result)
    return result


def border_kernel(depths, mid_ref, outer_ref, inner_ref):
    sub = lax.broadcasted_iota(jnp.int32, (ROWS, LANES), 0)
    first_core = lax.axis_index("lat") % 2 == 0

    def each(source, carry):
        for number in range(NEAR_TILES):
            ends = []
            for first in (0, ROWS - NEAR):
                places = [divmod(number * ROWS + to, NEAR) for to in range(ROWS)]
                moves = [(tile, first + row, to) for to, (tile, row) in enumerate(places)]
                ends.append(gather(lambda n: mid_ref[source, n], moves, sub))
            outer_ref[source, number] = jnp.where(first_core, ends[0], ends[1])
            inner_ref[source, number] = jnp.where(first_core, ends[1], ends[0])
        return carry

    lax.fori_loop(0, depths, each, 0, unroll=2)


def edge_columns(packs, item, lane):
    edge = pltpu.roll(packs[item // 8], LANES - (16 * (item % 8) + 8), 1)
    return jnp.where((lane < 8) | (lane >= LANES - 8), edge, 0.0)


def early_kernel(sizes, tx_ref, rx_ref, weight_ref, mid_ref, edge_ref, source_ref):
    depths, lats, pieces = sizes
    span = 2 * LANES
    width = pieces * LANES
    lat_index = lax.axis_index("lat")
    kind = lax.axis_index("kind")
    piece = lax.axis_index("piece")
    lane = lax.broadcasted_iota(jnp.int32, (ROWS, LANES), 1)

    def spread(source, carry):
        packs = [mid_ref[source, 14], mid_ref[source, 15]]
        for item in range(14):
            edge_ref[item // 2, 2 * source + item % 2] = edge_columns(packs, item, lane)
        return carry

    lax.fori_loop(0, depths, spread, 0, unroll=2)

    for z in range(2 * depths):
        for part in range(2):
            source_ref[part, z] = jnp.zeros((2 * ROWS, span), jnp.float32)
    line = lax.broadcasted_iota(jnp.int32, (1, span), 1)

    def place_of(cell):
        col = (cell & (width - 1)) - piece * LANES
        rest = lax.shift_right_logical(cell, width.bit_length() - 1)
        row = (rest & (lats * ROWS - 1)) - lat_index * ROWS
        z = lax.shift_right_logical(rest, (lats * ROWS).bit_length() - 1)
        return (row >= -4) & (row < 12) & (col >= -8) & (col < LANES + 8), z, row, col

    def add_source(cell, real, imag):
        held, z, row, col = place_of(cell)

        @pl.when(held)
        def _():
            hit = line == (col & (span - 1))
            at = pl.ds(row & (2 * ROWS - 1), 1)
            source_ref[0, z, at] = source_ref[0, z, at] + jnp.where(hit, real, 0.0)
            source_ref[1, z, at] = source_ref[1, z, at] + jnp.where(hit, imag, 0.0)

    @pl.when(kind == 0)
    def _():
        add_source(tx_ref[0], jnp.float32(0.0), jnp.float32(-SOURCE))

    @pl.when(kind == 1)
    def _():
        def each(group, carry):
            numbers = [8 * group + n for n in range(8)]
            some = place_of(rx_ref[0, numbers[0]])[0]
            for r in numbers[1:]:
                some = some | place_of(rx_ref[0, r])[0]

            @pl.when(some)
            def _():
                for r in numbers:
                    add_source(rx_ref[0, r], weight_ref[0, 2 * r], weight_ref[0, 2 * r + 1])

            return carry

        lax.fori_loop(0, rx_ref.shape[1] // 8, each, 0)


def basis_scratch(depths):
    layers = 2 * depths
    f32 = jnp.float32
    return [
        pltpu.VMEM((BASIS, 6, layers + 1, 2 * ROWS, 2 * LANES), f32),
        pltpu.VMEM((7, layers, 2 * ROWS, 2 * LANES), f32),
        pltpu.VMEM((4, 3 * ROWS, 2 * LANES), f32),
        pltpu.VMEM((4, 2 * ROWS, 2 * LANES), f32),
        pltpu.VMEM((layers, 2 * ROWS, 2 * LANES), f32),
        pltpu.VMEM((3 * ROWS, 2 * LANES), f32),
        pltpu.VMEM((2 * ROWS, 2 * LANES), f32),
        pltpu.VMEM((2 * len(ENTRIES), ROWS, LANES), f32),
    ]


def basis_kernel(
    sizes, edge_ref, source_ref, outer_ref, mid_ref, inner_ref, basis_ref, gram_ref,
    field, sides, curl_start, curl, cond, inside_start, inside, acc,
):
    depths, lats, pieces = sizes
    layers = 2 * depths
    span = 2 * LANES
    width = pieces * LANES
    lat_index = lax.axis_index("lat")
    kind = lax.axis_index("kind")
    piece = lax.axis_index("piece")
    lane = lax.broadcasted_iota(jnp.int32, (ROWS, LANES), 1)
    blank = jnp.zeros((ROWS, LANES), jnp.float32)

    def within(rows, row):
        lane_w = lax.broadcasted_iota(jnp.int32, (rows, span), 1)
        x_at = lat_index * ROWS + row
        y_at = piece * LANES + jnp.where(lane_w >= LANES + 64, lane_w - span, lane_w)
        good = (x_at >= 0) & (x_at < lats * ROWS) & (y_at >= 0) & (y_at < width)
        return jnp.where(good, 1.0, 0.0)

    row_s = lax.broadcasted_iota(jnp.int32, (3 * ROWS, span), 0)
    inside_start[...] = within(3 * ROWS, row_s - ROWS)
    row_b = lax.broadcasted_iota(jnp.int32, (2 * ROWS, span), 0)
    inside[...] = within(2 * ROWS, jnp.where(row_b >= 12, row_b - 16, row_b))

    first_core = lat_index % 2 == 0

    sub = lax.broadcasted_iota(jnp.int32, (ROWS, LANES), 0)

    def spread(source, carry):
        tiles = [], []
        for number in range(NEAR_TILES):
            outer, inner = outer_ref[source, number], inner_ref[source, number]
            tiles[0].append(jnp.where(first_core, outer, inner))
            tiles[1].append(jnp.where(first_core, inner, outer))
        for number, first in enumerate((ROWS - NEAR, 0)):
            found = []
            for item in range(TILES):
                places = [divmod(item * NEAR + row, ROWS) for row in range(NEAR)]
                moves = [(tile, at, first + row) for row, (tile, at) in enumerate(places)]
                found.append(gather(lambda n: tiles[number][n], moves, sub))
            for item in range(14):
                rows = slice(number * ROWS, (number + 1) * ROWS)
                at = (item // 2, 2 * source + item % 2, rows)
                sides[at + (slice(0, LANES),)] = found[item]
                sides[at + (slice(LANES, span),)] = edge_columns(found[14:], item, lane)
        return carry

    lax.fori_loop(0, depths, spread, 0, unroll=4)

    empty = jnp.zeros((2 * ROWS, span), jnp.float32)
    for number in range(BASIS - 1):
        for component in range(6):
            field[number, component, layers] = empty

    def ahead(values, axis):
        return pltpu.roll(values, values.shape[axis] - 1, axis) - values

    def behind(values, axis):
        return values - pltpu.roll(values, 1, axis)

    def curl_ahead(here, above, keep):
        uz, ux, uy = here
        hz = (ahead(uy, 0) - ahead(ux, 1)) * keep
        hx = (ahead(uz, 1) - (above[1] - uy)) * keep
        hy = ((above[0] - ux) - ahead(uz, 0)) * keep
        return hz, hx, hy

    def curl_behind(h, below):
        hz, hx, hy = h
        return (
            behind(hy, 0) - behind(hx, 1),
            behind(hz, 1) - (hy - below[1]),
            (hx - below[0]) - behind(hz, 0),
        )

    def start_tile(number, z, source, layer):
        own = jnp.concatenate([mid_ref[source, 2 * number + layer], edge_ref[number, z]], axis=1)
        left, right = sides[number, z, :ROWS], sides[number, z, ROWS:]
        return jnp.concatenate([left, own, right], axis=0)

    def merge(values):
        sub = lax.broadcasted_iota(jnp.int32, (ROWS, span), 0)
        sides = jnp.where(sub < 4, values[2 * ROWS :], values[:ROWS])
        return jnp.concatenate([values[ROWS : 2 * ROWS], sides], axis=0)

    for number in range(4):
        curl_start[number] = jnp.zeros((3 * ROWS, span), jnp.float32)

    def start_layers(source, carry):
        keep = inside_start[...]
        below = [[curl_start[0], curl_start[1]], [curl_start[2], curl_start[3]]]
        for layer in range(2):
            z = 2 * source + layer
            tiles = [start_tile(c, z, source, layer) for c in range(6)]
            sigma = start_tile(6, z, source, layer)
            cond[z] = merge(sigma)
            for part in range(2):
                here = tiles[3 * part : 3 * part + 3]
                if layer == 0:
                    above = [start_tile(3 * part + c, z + 1, source, 1) for c in (1, 2)]
                else:
                    last = source == depths - 1
                    after = jnp.minimum(source + 1, depths - 1)
                    above = [
                        jnp.where(last, 0.0, start_tile(3 * part + c, 2 * after, after, 0))
                        for c in (1, 2)
                    ]
                h = curl_ahead(here, above, keep)
                outs = curl_behind(h, below[part])
                below[part] = [h[1], h[2]]
                for component, value in enumerate(outs):
                    other = sigma * tiles[3 * (1 - part) + component]
                    value = other - value if part == 0 else -value - other
                    value = merge(value) * inside[...]
                    if component == 0:
                        value = value + source_ref[part, z]
                    field[0, 3 * part + component, z] = value
        for number in range(4):
            curl_start[number] = below[number // 2][number % 2]
        return carry

    lax.fori_loop(0, depths, start_layers, 0)

    for step in range(BASIS - 1):
        for number in range(4):
            curl[number] = empty

        def apply_layers(source, carry, step=step):
            keep = inside[...]
            below = [[curl[0], curl[1]], [curl[2], curl[3]]]
            for layer in range(2):
                z = 2 * source + layer
                sigma = cond[z]
                for part in range(2):
                    here = [field[step, 3 * part + c, z] for c in range(3)]
                    above = [field[step, 3 * part + c, z + 1] for c in (1, 2)]
                    h = curl_ahead(here, above, keep)
                    outs = curl_behind(h, below[part])
                    below[part] = [h[1], h[2]]
                    for component, value in enumerate(outs):
                        if step == BASIS - 2:
                            mine = (slice(0, ROWS), slice(0, LANES))
                        else:
                            mine = (slice(None), slice(None))
                        near = field[(step, 3 * (1 - part) + component, z) + mine]
                        other = sigma[mine] * near
                        value = value[mine]
                        value = value - other if part == 0 else value + other
                        if step < BASIS - 2:
                            value = value * keep
                        field[(step + 1, 3 * part + component, z) + mine] = value
            for number in range(4):
                curl[number] = below[number // 2][number % 2]
            return carry

        lax.fori_loop(0, depths, apply_layers, 0, unroll=2)

    for entry in range(2 * len(ENTRIES)):
        acc[entry] = blank

    def gram_layers(source, carry):
        tiles = []
        for b in range(BASIS):
            group = []
            for component in range(6):
                for layer in range(2):
                    tile = field[b, component, 2 * source + layer, 0:ROWS, 0:LANES]
                    group.append(tile)
                    if b < BASIS - 1:
                        basis_ref[b, source, 2 * component + layer] = tile
            tiles.append(group)
        for entry, (i, j, part) in enumerate(ENTRIES):
            first, second = tiles[i], tiles[j]
            if part:
                terms = [first[n] * second[n + 6] - first[n + 6] * second[n] for n in range(6)]
            else:
                terms = [first[n] * second[n] + first[n + 6] * second[n + 6] for n in range(6)]
            value = (terms[0] + terms[1]) + (terms[2] + terms[3]) + (terms[4] + terms[5])
            total, error = two_sum(acc[2 * entry], value)
            acc[2 * entry] = total
            acc[2 * entry + 1] = acc[2 * entry + 1] + error
        return carry

    lax.fori_loop(0, depths, gram_layers, 0, unroll=2)

    def fold(high, low, shift, axis):
        total, error = two_sum(high, pltpu.roll(high, shift, axis))
        return total, low + pltpu.roll(low, shift, axis) + error

    sub = lax.broadcasted_iota(jnp.int32, (ROWS, LANES), 0)
    row = blank
    for start in range(0, len(ENTRIES), 8):
        highs, lows = blank, blank
        for entry in range(start, min(start + 8, len(ENTRIES))):
            high, low = acc[2 * entry], acc[2 * entry + 1]
            for shift in (4, 2, 1):
                high, low = fold(high, low, shift, 0)
            highs = jnp.where(sub == entry - start, high, highs)
            lows = jnp.where(sub == entry - start, low, lows)
        for shift in (64, 32, 16, 8, 4, 2, 1):
            highs, lows = fold(highs, lows, shift, 1)
        row = jnp.where(lane == sub + start, highs, row)
        row = jnp.where(lane == sub + start + 64, lows, row)
    for shift in (4, 2, 1):
        row = row + pltpu.roll(row, shift, 0)
    for number in range(pieces * lats // ROWS):
        gram_ref[number * ROWS : (number + 1) * ROWS] = row


def quick(a, b):
    total = a + b
    return total, b - (total - a)


def split(a):
    big = a * 4097.0
    high = big - (big - a)
    return high, a - high


def two_product(a, b):
    value = a * b
    ah, al = split(a)
    bh, bl = split(b)
    return value, ((ah * bh - value) + ah * bl + al * bh) + al * bl


def add(a, b):
    total, error = two_sum(a[0], b[0])
    return quick(total, error + (a[1] + b[1]))


def neg(a):
    return (-a[0], -a[1])


def mul(a, b):
    value, error = two_product(a[0], b[0])
    return quick(value, error + (a[0] * b[1] + a[1] * b[0]))


def div(a, b):
    first = a[0] / b[0]
    zero = jnp.zeros_like(first)
    rest = add(a, neg(mul(b, (first, zero))))
    second = rest[0] / b[0]
    rest = add(rest, neg(mul(b, (second, zero))))
    third = rest[0] / b[0]
    return add(quick(first, second), (third, zero))


def c_add(a, b):
    return (add(a[0], b[0]), add(a[1], b[1]))


def c_neg(a):
    return (neg(a[0]), neg(a[1]))


def c_conj(a):
    return (a[0], neg(a[1]))


def c_mul(a, b):
    return (
        add(mul(a[0], b[0]), neg(mul(a[1], b[1]))),
        add(mul(a[0], b[1]), mul(a[1], b[0])),
    )


def c_div(a, b):
    top = c_mul(a, c_conj(b))
    bottom = add(mul(b[0], b[0]), mul(b[1], b[1]))
    return (div(top[0], bottom), div(top[1], bottom))


def c_over(a, real):
    return (div(a[0], real), div(a[1], real))


def total_of(values):
    result = values[0]
    for value in values[1:]:
        result = c_add(result, value)
    return result


def coefficients(gram):
    rho = gram[0, 0]
    alpha = c_div(rho, gram[0, 1])
    one_half = c_neg(alpha)

    def form(coeffs, left, right):
        rows = []
        for i, factor in enumerate(coeffs):
            inner = total_of(
                [
                    gram[i + left, j + right]
                    if other is None
                    else c_mul(gram[i + left, j + right], other)
                    for j, other in enumerate(coeffs)
                ]
            )
            rows.append(inner if factor is None else c_mul(c_conj(factor), inner))
        return total_of(rows)

    omega = c_over(form([None, one_half], 1, 0), form([None, one_half], 1, 1)[0])
    res1 = c_neg(c_add(alpha, omega))
    res2 = c_mul(alpha, omega)
    new_rho = total_of([gram[0, 0], c_mul(gram[0, 1], res1), c_mul(gram[0, 2], res2)])
    mix = c_mul(c_over(new_rho, rho[0]), c_div(alpha, omega))
    dir0 = (add((jnp.ones_like(mix[0][0]), jnp.zeros_like(mix[0][0])), mix[0]), mix[1])
    dir1 = c_add(res1, c_neg(c_mul(mix, omega)))
    dir2 = res2
    along = total_of(
        [c_mul(gram[0, 1], dir0), c_mul(gram[0, 2], dir1), c_mul(gram[0, 3], dir2)]
    )
    alpha2 = c_div(new_rho, along)
    half1 = c_add(res1, c_neg(c_mul(alpha2, dir0)))
    half2 = c_add(res2, c_neg(c_mul(alpha2, dir1)))
    half3 = c_neg(c_mul(alpha2, dir2))
    half = [None, half1, half2, half3]
    omega2 = c_over(form(half, 1, 0), form(half, 1, 1)[0])
    out0 = total_of([alpha, omega, c_mul(alpha2, dir0), omega2])
    out1 = total_of([c_mul(omega, one_half), c_mul(alpha2, dir1), c_mul(omega2, half1)])
    out2 = c_add(c_mul(alpha2, dir2), c_mul(omega2, half2))
    out3 = c_mul(omega2, half3)
    return [(c[0][0], c[1][0]) for c in (out0, out1, out2, out3)]


def update_kernel(sizes, rows_ref, start_ref, basis_ref, out_ref):
    depths, lats, pieces = sizes
    high = jnp.zeros((ROWS, LANES), jnp.float32)
    low = high
    for number in range(pieces * lats // ROWS):
        high, error = two_sum(high, rows_ref[number * ROWS : (number + 1) * ROWS])
        low = low + error
    for shift in (4, 2, 1):
        high, error = two_sum(high, pltpu.roll(high, shift, 0))
        low = low + pltpu.roll(low, shift, 0) + error
    high, low = quick(high, low + pltpu.roll(high, 64, 1))

    def entry(number):
        return (
            jnp.broadcast_to(high[:, number : number + 1], (ROWS, LANES)),
            jnp.broadcast_to(low[:, number : number + 1], (ROWS, LANES)),
        )

    zero = jnp.zeros((ROWS, LANES), jnp.float32)
    gram = {}
    at = 0
    for i, j in PAIRS:
        real = entry(at)
        at += 1
        if i == j:
            gram[i, i] = (real, (zero, zero))
        else:
            gram[i, j] = (real, entry(at))
            gram[j, i] = c_conj(gram[i, j])
            at += 1
    factors = coefficients(gram)

    def layer(source, carry):
        for component in range(3):
            for z in range(2):
                real = start_ref[source, slot(0, component, z)]
                imag = start_ref[source, slot(1, component, z)]
                for b, (fr, fi) in enumerate(factors):
                    br = basis_ref[b, source, slot(0, component, z)]
                    bi = basis_ref[b, source, slot(1, component, z)]
                    real = real + (fr * br - fi * bi)
                    imag = imag + (fr * bi + fi * br)
                out_ref[source, slot(0, component, z)] = real
                out_ref[source, slot(1, component, z)] = imag
        return carry

    lax.fori_loop(0, depths, layer, 0, unroll=2)


def output_kernel(pieces, in_ref, field_ref, term_ref):
    for piece in range(pieces):
        cols = slice(piece * LANES, (piece + 1) * LANES)
        for z in range(2):
            term = None
            for component in range(3):
                values = []
                for kind in range(KINDS):
                    for part in range(2):
                        value = in_ref[kind * pieces + piece, slot(part, component, z)]
                        field_ref[kind * 12 + slot(part, component, z), :, cols] = value
                        values.append(value)
                product = values[0] * values[2] - values[1] * values[3]
                term = product if term is None else term + product
            term_ref[piece, z] = term


def local(conductivity, field_guess, tx_cell, rx_cell, rx_weight):
    pieces, lats = lax.axis_size("piece"), lax.axis_size("lat")
    depths = KINDS * pieces
    sizes = (depths, lats, pieces)
    width = conductivity.shape[2]
    layers = 2 * depths
    f32 = jnp.float32
    params = pltpu.CompilerParams

    packed = pl.pallas_call(
        functools.partial(pack_kernel, pieces),
        out_shape=jax.ShapeDtypeStruct((depths, 16, ROWS, LANES), f32),
        in_specs=[pl.BlockSpec(memory_space=pl.ANY)] * 2,
        out_specs=in_vmem(),
        scratch_shapes=[
            pltpu.VMEM((24, ROWS, width), f32),
            pltpu.VMEM(conductivity.shape, f32),
            pltpu.SemaphoreType.DMA((KINDS + 1,)),
        ],
    )(field_guess.reshape(24, ROWS, width), conductivity)
    mid = lax.all_to_all(packed, DEPTH, 0, 0)
    border = [(i, i + 1) for i in range(1, lats - 1, 2)]
    near_outer, near_inner = pl.pallas_call(
        functools.partial(border_kernel, depths),
        out_shape=(jax.ShapeDtypeStruct((depths, NEAR_TILES, ROWS, LANES), f32),) * 2,
        in_specs=[in_vmem()],
        out_specs=(in_vmem(), in_vmem()),
        compiler_params=params(vmem_limit_bytes=4 * MIB),
    )(mid)
    border = [(i, i + 1) for i in range(1, lats - 1, 2)]
    inner = lax.ppermute(near_inner, "lat", [(i, i ^ 1) for i in range(lats)])
    outer = lax.ppermute(near_outer, "lat", border + [(b, a) for a, b in border])

    edges, sources = pl.pallas_call(
        functools.partial(early_kernel, sizes),
        out_shape=(
            jax.ShapeDtypeStruct((7, 2 * depths, ROWS, LANES), f32),
            jax.ShapeDtypeStruct((2, 2 * depths, 2 * ROWS, 2 * LANES), f32),
        ),
        in_specs=[in_smem()] * 3 + [in_vmem()],
        out_specs=(in_vmem(), in_vmem()),
        compiler_params=params(vmem_limit_bytes=8 * MIB),
    )(tx_cell, rx_cell, rx_weight.reshape(1, -1), mid)
    basis, rows = pl.pallas_call(
        functools.partial(basis_kernel, sizes),
        out_shape=(
            jax.ShapeDtypeStruct((BASIS - 1, depths, 12, ROWS, LANES), f32),
            jax.ShapeDtypeStruct((pieces * lats, LANES), f32),
        ),
        in_specs=[in_vmem()] * 5,
        out_specs=(in_vmem(), in_vmem()),
        scratch_shapes=basis_scratch(depths),
        compiler_params=params(vmem_limit_bytes=28 * MIB),
    )(edges, sources, outer, mid, inner)

    rows = lax.all_to_all(rows, ("piece", "lat"), 0, 0)
    moved = pl.pallas_call(
        functools.partial(update_kernel, sizes),
        out_shape=jax.ShapeDtypeStruct((depths, 12, ROWS, LANES), f32),
        in_specs=[in_vmem()] * 3,
        out_specs=in_vmem(),
        compiler_params=params(vmem_limit_bytes=8 * MIB),
    )(rows, mid, basis)
    moved = lax.all_to_all(moved, DEPTH, 0, 0)
    fields, terms = pl.pallas_call(
        functools.partial(output_kernel, pieces),
        out_shape=(
            jax.ShapeDtypeStruct((24, ROWS, width), f32),
            jax.ShapeDtypeStruct((pieces, 2, ROWS, LANES), f32),
        ),
        in_specs=[in_vmem()],
        out_specs=(in_vmem(), in_vmem()),
        compiler_params=params(vmem_limit_bytes=4 * MIB),
    )(moved)
    gradient = jnp.sum(lax.all_to_all(terms, "tx", 0, 0), axis=0)
    return (fields.reshape(field_guess.shape), gradient)


def solution(mesh):
    grid = mesh.devices
    split = Mesh(
        grid.reshape((KINDS, grid.shape[0] // KINDS) + grid.shape[1:]),
        DEPTH + tuple(mesh.axis_names[1:]),
    )
    return jax.shard_map(
        local,
        mesh=split,
        in_specs=(
            P(DEPTH, "lat", None),
            P("tx", None, None, None, DEPTH, "lat", None),
            P("tx"),
            P("tx", None),
            P("tx", None, None),
        ),
        out_specs=(P("tx", None, None, None, DEPTH, "lat", None), P(DEPTH, "lat", "tx")),
        check_vma=False,
    )
```
